32 devices in a mesh: blk: 8 (over z, y), fsdp: 4 (over x, core).
Axes of the slice: x: 2, y: 2, z: 4, core: 2. Of those that a mesh axis runs over, the one named last changes fastest.
Arguments:
- tokens: bfloat16 [4, 1024, 768], P('fsdp', 'blk'), may hold values from -6 to 6
- slot_pos: int32 [4, 1024], P('fsdp'), may hold values from 0 to 1023, as said below
- lengths: int32 [4, 4], P('fsdp'), may hold values from 128 to 512, as said below
- thoughts: int32 [4, 64], P('fsdp'), may hold values from 1 to 1023, as said below
- ln_gain: bfloat16 [2, 768], P(None, 'fsdp'), may hold values from 0.5 to 1.5
- ln_shift: bfloat16 [2, 768], P(None, 'fsdp'), may hold values from -2 to 2
- w_qkv: bfloat16 [768, 2304], P('fsdp'), may hold values from -0.21875 to 0.21875
- qv_bias: bfloat16 [2, 768], P(None, 'fsdp'), may hold values from -2 to 2
- w_out: bfloat16 [768, 768], P('fsdp'), may hold values from -0.875 to 0.875
- out_bias: bfloat16 [768], P('fsdp'), may hold values from -2 to 2
- w_fc: bfloat16 [768, 3072], P('fsdp'), may hold values from -0.21875 to 0.21875
- fc_bias: bfloat16 [3072], P('fsdp'), may hold values from -2 to 2
- w_proj: bfloat16 [3072, 768], P('fsdp'), may hold values from -0.109375 to 0.109375
- proj_bias: bfloat16 [768], P('fsdp'), may hold values from -2 to 2
- cotangent: bfloat16 [4, 1024, 768], P('fsdp', 'blk'), may hold values from -6 to 6
Outputs:
- result: bfloat16 [4, 1024, 768], P('fsdp', 'blk')
- grad_tokens: float32 [4, 1024, 768], P('fsdp', 'blk')
- grad_ln_gain: float32 [2, 768], P(None, 'fsdp')
- grad_ln_shift: float32 [2, 768], P(None, 'fsdp')
- grad_w_qkv: float32 [768, 2304], P('fsdp')
- grad_qv_bias: float32 [2, 768], P(None, 'fsdp')
- grad_w_out: float32 [768, 768], P('fsdp')
- grad_out_bias: float32 [768], P('fsdp')
- grad_w_fc: float32 [768, 3072], P('fsdp')
- grad_fc_bias: float32 [3072], P('fsdp')
- grad_w_proj: float32 [3072, 768], P('fsdp')
- grad_proj_bias: float32 [768], P('fsdp')
The draws below stay inside these ranges and needn't reach their ends.
Inputs may be any that keep to these rules, and one draw needn't show every extreme that they name: In each group slot_pos is a permutation of the group's positions; aligned runs of 8 positions lie together in order on one device of blk, each aligned run of 8 times the number of blk devices positions gives one run to every device, and a device holds its runs in order of position. Each group's 4 lengths sum to 1024; exactly one of them is 512. `thoughts`: 64 distinct positions of the group, none of them 0; positions 1 and 1023 are always among them.
All inputs are finite; a program needn't handle non-finite values.
Results may differ from the reference program's by a relative error of at most 0.015.
Values may be sent and summed in bfloat16 or wider, within the bound.
No kernel may reach another device: no remote copies, remote signals or barrier semaphores. Data moves between devices by JAX's collectives and lax.ppermute only.
A program may use at most 256 MiB of HBM per device.

```python
import math
import jax
import jax.numpy as jnp
from jax import lax

D = 768
HEADS = 12
HDIM = 64
FF = 3072
TOK_DEV = 128
UNIT = 8
NSEQ = 4
NTH = 64
GROUPS = 4
TB = 1024
SHORTEST = 128
MAXLEN = 512


def draw_slot_pos(key, part):
    devices = TB // TOK_DEV
    rounds = TOK_DEV // UNIT
    key_list = jax.random.split(key, GROUPS * rounds)

    def shuffle_devices(subkey):
        return jax.random.permutation(subkey, devices)
    shuffles = jax.vmap(shuffle_devices)(key_list).reshape(GROUPS, rounds, devices)
    unit_index = jnp.arange(rounds, dtype=jnp.int32)[None, :, None] * devices + shuffles
    unit_index = jnp.transpose(unit_index, (0, 2, 1))
    positions = unit_index[..., None] * UNIT + jnp.arange(UNIT, dtype=jnp.int32)
    return positions.reshape(GROUPS, TB).astype(jnp.int32)


def draw_lengths(key, part):
    key = jax.random.fold_in(key, 29)
    key_list = jax.random.split(key, GROUPS)
    spare = TB - MAXLEN - SHORTEST * (NSEQ - 1)

    def one_group(subkey):
        cut_key, order_key = jax.random.split(subkey)
        cuts = jnp.sort(jax.random.randint(cut_key, (NSEQ - 2,), 0, spare + 1).astype(jnp.int32))
        edges = jnp.concatenate([jnp.zeros((1,), jnp.int32), cuts, jnp.full((1,), spare, jnp.int32)])
        extras = (edges[1:] - edges[:-1]).astype(jnp.int32)
        values = jnp.concatenate([jnp.full((1,), MAXLEN, jnp.int32), extras + SHORTEST]).astype(jnp.int32)
        order = jax.random.permutation(order_key, NSEQ)
        return values[order].astype(jnp.int32)
    return jax.vmap(one_group)(key_list).astype(jnp.int32)


def draw_thoughts(key, part):
    key_list = jax.random.split(jax.random.fold_in(key, 17), GROUPS)

    def choose_positions(subkey):
        first_key, order_key = jax.random.split(subkey)
        middle = jax.random.permutation(first_key, TB - 3)[:NTH - 2].astype(jnp.int32) + 2
        ends = jnp.array([1, TB - 1], dtype=jnp.int32)
        chosen = jnp.concatenate([ends, middle]).astype(jnp.int32)
        return chosen[jax.random.permutation(order_key, NTH)]
    chosen = jax.vmap(choose_positions)(key_list)
    return chosen.astype(jnp.int32)


def level_of(own_key, extent, shards, smallest, high):
    def one(axis_at, blocks):
        steps = jax.random.uniform(jax.random.fold_in(jax.random.fold_in(own_key, 6), axis_at), (blocks,), jnp.float32, smallest / len(shards), high / len(shards))
        return jnp.repeat(jnp.exp(steps), extent[axis_at] // blocks).reshape((-1,) + (1,) * (len(extent) - axis_at - 1))

    level = one(*shards[0])
    for cut in shards[1:]:
        level = level * one(*cut)
    return level


def noise(rng, dims, scale, limit, pieces=(), kind=jnp.bfloat16):
    drawn = scale * jax.random.normal(rng, dims, jnp.float32)
    if pieces:
        drawn = drawn * level_of(rng, dims, pieces, -0.22, 0.18)
    return jnp.clip(drawn, -limit, limit).astype(kind)


def setup_inputs(seed: int = 0) -> dict:
    streams_of = jax.random.split(jax.random.key(seed), 16)
    tokens = noise(streams_of[0], (GROUPS, TB, D), 1.0, 6.0, ((0, 4), (1, 8)))
    slot_pos = draw_slot_pos(jax.random.fold_in(streams_of[15], 71), 0)
    lengths = draw_lengths(jax.random.fold_in(streams_of[15], 71), 0)
    thoughts = draw_thoughts(jax.random.fold_in(streams_of[15], 71), 0)
    ln_gain = jnp.clip(1.0 + 0.1 * jax.random.normal(streams_of[4], (2, D), jnp.float32), 0.5, 1.5).astype(jnp.bfloat16)
    ln_shift = noise(streams_of[5], (2, D), 0.3, 2.0, ((1, 4),))
    w_qkv = noise(streams_of[6], (D, 3 * D), D ** -0.5, 0.21875, ((0, 4),))
    qv_bias = noise(streams_of[7], (2, D), 0.3, 2.0, ((1, 4),))
    w_out = noise(streams_of[8], (D, D), (D // 16) ** -0.5, 0.875, ((0, 4),))
    out_bias = noise(streams_of[9], (D,), 0.3, 2.0, ((0, 4),))
    w_fc = noise(streams_of[10], (D, FF), D ** -0.5, 0.21875, ((0, 4),))
    fc_bias = noise(streams_of[11], (FF,), 0.3, 2.0, ((0, 4),))
    w_proj = noise(streams_of[12], (FF, D), FF ** -0.5, 0.109375, ((0, 4),))
    proj_bias = noise(streams_of[13], (D,), 0.3, 2.0, ((0, 4),))
    cotangent = noise(streams_of[14], (GROUPS, TB, D), 1.0, 6.0, ((0, 4), (1, 8)))
    return dict(tokens=tokens, slot_pos=slot_pos, lengths=lengths, thoughts=thoughts, ln_gain=ln_gain, ln_shift=ln_shift, w_qkv=w_qkv, qv_bias=qv_bias, w_out=w_out, out_bias=out_bias, w_fc=w_fc, fc_bias=fc_bias, w_proj=w_proj, proj_bias=proj_bias, cotangent=cotangent)


epsilon = 1e-05
masked_score = -1e+30

@jax.custom_vjp
def low(v):
    return lax.optimization_barrier(v.astype(jnp.bfloat16)).astype(jnp.float32)

@jax.custom_vjp
def low_back(v):
    return v

def low_keep(v):
    return (low(v), None)

def low_pass(kept, grad):
    return (grad,)

def back_keep(v):
    return (v, None)

def back_low(kept, grad):
    return (low(grad),)
low.defvjp(low_keep, low_pass)
low_back.defvjp(back_keep, back_low)

def layer_norm(inputs, gain, shift):
    center = inputs - lax.optimization_barrier(jnp.mean(inputs, axis=-1, keepdims=True))
    variance = lax.optimization_barrier(jnp.mean(center * center, axis=-1, keepdims=True))
    return center * lax.rsqrt(variance + epsilon) * gain + shift

def sequence_ids(positions, seq_lengths):
    seq_ends = jnp.cumsum(seq_lengths).astype(jnp.int32)
    return lax.optimization_barrier(jnp.sum((positions[:, None] >= seq_ends[None, :]).astype(jnp.int32), axis=1)).astype(jnp.int32)

def attention(queries, key_rows, value_rows, positions, sequence):
    row_count = queries.shape[0]
    block_rows = math.gcd(row_count, 256)
    score_scale = HDIM ** (-0.5)
    query_heads = queries.reshape(row_count, HEADS, HDIM)
    key_heads = key_rows.reshape(row_count, HEADS, HDIM)
    value_heads = value_rows.reshape(row_count, HEADS, HDIM)

    def one_block(number):
        offset = (number * block_rows).astype(jnp.int32)
        query_block = lax.dynamic_slice_in_dim(query_heads, offset, block_rows)
        query_pos = lax.dynamic_slice_in_dim(positions, offset, block_rows)
        query_seq = lax.dynamic_slice_in_dim(sequence, offset, block_rows)
        scores = jnp.einsum('qhd,khd->hqk', query_block, key_heads, precision=lax.Precision.HIGHEST) * score_scale
        scores = low_back(scores)
        allowed = (query_seq[:, None] == sequence[None, :]) & (positions[None, :] <= query_pos[:, None])
        scores = jnp.where(allowed[None], scores, masked_score)
        weights = low(jax.nn.softmax(scores, axis=-1))
        return jnp.einsum('hqk,khd->qhd', weights, value_heads, precision=lax.Precision.HIGHEST)
    context = lax.map(jax.checkpoint(one_block), jnp.arange(row_count // block_rows, dtype=jnp.int32))
    return context.reshape(row_count, HEADS * HDIM)

def residual_block(inputs, positions, sequence, params):
    norm_gains, norm_shifts, w_qkv, qv_bias, w_out, out_bias, w_fc, fc_bias, w_proj, proj_bias = params
    model_width = HEADS * HDIM
    normed = low(layer_norm(inputs, norm_gains[0], norm_shifts[0]))
    projected = jnp.dot(normed, w_qkv, precision=lax.Precision.HIGHEST)
    queries = low(low_back(projected[:, :model_width] + qv_bias[0]))
    key_rows = low(low_back(projected[:, model_width:2 * model_width]))
    value_rows = low(low_back(projected[:, 2 * model_width:] + qv_bias[1]))
    context = low(low_back(attention(queries, key_rows, value_rows, positions, sequence)))
    attended = low_back(jnp.dot(context, w_out, precision=lax.Precision.HIGHEST) + out_bias)
    middle = inputs + attended
    second = low(layer_norm(middle, norm_gains[1], norm_shifts[1]))
    hidden = low_back(jnp.dot(second, w_fc, precision=lax.Precision.HIGHEST) + fc_bias)
    active = low(jax.nn.gelu(hidden, approximate=True))
    output = low_back(jnp.dot(active, w_proj, precision=lax.Precision.HIGHEST) + proj_bias)
    return middle + output

def forward(inputs, slot_pos, lengths, thoughts, params):
    results = []
    for group_index in range(GROUPS):
        positions = slot_pos[group_index]
        sequence = sequence_ids(positions, lengths[group_index])
        latent = residual_block(inputs[group_index], positions, sequence, params)
        source = (positions[None, :] == thoughts[group_index][:, None] - 1).astype(jnp.float32)
        target = (positions[None, :] == thoughts[group_index][:, None]).astype(jnp.float32)
        carried = jnp.dot(source, latent, precision=lax.Precision.HIGHEST)
        placed = jnp.einsum('nt,nd->td', target, carried, precision=lax.Precision.HIGHEST)
        keep_rows = 1.0 - lax.optimization_barrier(jnp.sum(target, axis=0))
        second = inputs[group_index] * keep_rows[:, None] + placed
        results.append(residual_block(second, positions, sequence, params))
    return jnp.stack(results)

def reference(tokens, slot_pos, lengths, thoughts, ln_gain, ln_shift, w_qkv, qv_bias, w_out, out_bias, w_fc, fc_bias, w_proj, proj_bias, cotangent):
    params = (ln_gain.astype(jnp.float32), ln_shift.astype(jnp.float32), w_qkv.astype(jnp.float32), qv_bias.astype(jnp.float32), w_out.astype(jnp.float32), out_bias.astype(jnp.float32), w_fc.astype(jnp.float32), fc_bias.astype(jnp.float32), w_proj.astype(jnp.float32), proj_bias.astype(jnp.float32))

    def apply_all(inputs, weights):
        return forward(inputs, slot_pos, lengths, thoughts, weights)
    result, pullback = jax.vjp(apply_all, tokens.astype(jnp.float32), params)
    grad_inputs, gradients = pullback(cotangent.astype(jnp.float32))
    return (result.astype(jnp.bfloat16), grad_inputs, gradients[0], gradients[1], gradients[2], gradients[3], gradients[4], gradients[5], gradients[6], gradients[7], gradients[8], gradients[9])
```

```python
import jax
import jax.numpy as jnp
from jax import lax
from jax.sharding import PartitionSpec as P

HDIM = 64
PARTS = 4
EPS = 1e-05
SCALE = HDIM ** (-0.5)
F32 = jnp.float32
BF16 = jnp.bfloat16


def dot(a, b, ca=1, cb=0):
    return lax.dot_general(a, b, (((ca,), (cb,)), ((), ())), preferred_element_type=F32)


def exact(a, b, ca=1, cb=0):
    return lax.dot_general(
        a, b, (((ca,), (cb,)), ((), ())), precision=lax.Precision.HIGHEST, preferred_element_type=F32
    )


def norm(x, gain, shift):
    center = x - jnp.mean(x, axis=-1, keepdims=True)
    inverse = lax.rsqrt(jnp.mean(center * center, axis=-1, keepdims=True) + EPS)
    scaled = center * inverse
    return (scaled * gain + shift).astype(BF16), scaled, inverse


def norm_back(up, scaled, inverse, gain):
    w = up * gain
    return inverse * (
        w - jnp.mean(w, axis=-1, keepdims=True) - scaled * jnp.mean(w * scaled, axis=-1, keepdims=True)
    )


def gelu(v):
    c = 0.7978845608028654
    t = jnp.tanh(c * (v + 0.044715 * v * v * v))
    return 0.5 * v * (1.0 + t)


def gelu_back(v):
    c = 0.7978845608028654
    t = jnp.tanh(c * (v + 0.044715 * v * v * v))
    return 0.5 * (1.0 + t) + 0.5 * v * (1.0 - t * t) * c * (1.0 + 3 * 0.044715 * v * v)


def attend(q, k, v, mask):
    outs, lses = [], []
    for h in range(q.shape[1] // HDIM):
        cols = slice(h * HDIM, (h + 1) * HDIM)
        s = jnp.where(mask, dot(q[:, cols], k[:, cols], 1, 1) * SCALE, -1e30)
        m = jnp.max(s, axis=1, keepdims=True)
        e = jnp.exp(s - m)
        total = jnp.sum(e, axis=1, keepdims=True)
        p = (e / total).astype(BF16)
        outs.append(dot(p, v[:, cols]))
        lses.append(m + jnp.log(total))
    return jnp.concatenate(outs, axis=1), jnp.concatenate(lses, axis=1)


def attend_back(q, k, v, mask, lse, ctx, grad):
    dq, dk, dv = [], [], []
    for h in range(q.shape[1] // HDIM):
        cols = slice(h * HDIM, (h + 1) * HDIM)
        s = dot(q[:, cols], k[:, cols], 1, 1) * SCALE
        p = jnp.where(mask, jnp.exp(s - lse[:, h : h + 1]), 0.0)
        dp = dot(grad[:, cols], v[:, cols], 1, 1)
        delta = jnp.sum(grad[:, cols].astype(F32) * ctx[:, cols], axis=1, keepdims=True)
        ds = (p * (dp - delta)).astype(BF16)
        dq.append(dot(ds, k[:, cols]) * SCALE)
        dk.append(dot(ds, q[:, cols], 0, 0) * SCALE)
        dv.append(dot(p.astype(BF16), grad[:, cols], 0, 0))
    cat = lambda parts: jnp.concatenate(parts, axis=1)
    return cat(dq), cat(dk), cat(dv)


def local(
    tokens, slot_pos, lengths, thoughts, ln_gain, ln_shift, w_qkv, qv_bias, w_out, out_bias,
    w_fc, fc_bias, w_proj, proj_bias, cotangent,
):
    n_blk, n_f = lax.axis_size("blk"), lax.axis_size("fsdp")
    H = PARTS
    Q = n_blk // H
    b, f = lax.axis_index("blk"), lax.axis_index("fsdp")
    z, y = b // Q, b % Q
    R, D = tokens.shape[1], tokens.shape[2]
    T = R * n_blk
    W = D // H
    S = D // n_f
    FS = w_proj.shape[0]

    def take(x, i, axis=0):
        return lax.dynamic_index_in_dim(x, i, axis, keepdims=False)

    def shift_h(x, k):
        return lax.ppermute(
            x, "blk", [(((c // Q + k) % H) * Q + c % Q, c) for c in range(n_blk)]
        )

    def shift_q(x, j):
        return lax.ppermute(x, "blk", [((c // Q) * Q + (c % Q + j) % Q, c) for c in range(n_blk)])

    def flip(x, bit):
        return lax.ppermute(x, "fsdp", [(c, c ^ bit) for c in range(n_f)])

    def ag_h(x):
        return jnp.roll(jnp.stack([x] + [shift_h(x, k) for k in range(1, H)]), z, axis=0)

    def ag_q(x):
        return jnp.roll(jnp.stack([x] + [shift_q(x, j) for j in range(1, Q)]), y, axis=0)

    def rs_h(x):
        got = [take(x, z).astype(F32)] + [
            shift_h(take(x, (z - k) % H), k).astype(F32) for k in range(1, H)
        ]
        return (got[0] + got[2]) + (got[1] + got[3])

    def rs_q(x):
        got = [take(x, y).astype(F32)] + [
            shift_q(take(x, (y - j) % Q), j).astype(F32) for j in range(1, Q)
        ]
        return sum(got[1:], got[0])

    def sum_q(x):
        if Q == 2:
            return x + shift_q(x, 1)
        return jnp.sum(ag_q(x), axis=0)

    def sum_h(x):
        return (x + shift_h(x, 2)) + (shift_h(x, 1) + shift_h(x, 3))

    def ag_f(x):
        far = flip(x, 2)
        near = flip(jnp.stack([x, far]), 1)
        return jnp.stack([x, near[0], far, near[1]])

    def rs_f(x):
        near = flip(jnp.stack([x[1], x[3]]).astype(BF16), 1).astype(F32)
        mine = x[0] + near[0]
        far = (x[2] + near[1]).astype(BF16)
        return mine + flip(far, 2).astype(F32)

    def in_order(x):
        near, far = (f % 2) == 1, (f // 2) == 1
        x = [jnp.where(near, x[i ^ 1], x[i]) for i in range(4)]
        return jnp.stack([jnp.where(far, x[i ^ 2], x[i]) for i in range(4)])

    own = tokens[0]
    X = jnp.transpose(ag_q(ag_h(own)), (1, 0, 2, 3))
    small = jnp.concatenate(
        [ln_gain, ln_shift, qv_bias, out_bias[None], proj_bias[None]], axis=0
    )
    part = jnp.concatenate(
        [lax.dynamic_slice_in_dim(w_qkv, i * D + z * W, W, axis=1) for i in range(3)], axis=1
    )
    pad = jnp.concatenate([small, jnp.zeros((8, 3 * W - S), BF16)], axis=1)
    pad = jnp.concatenate([pad, jnp.zeros((8, 3 * W), BF16)], axis=0)
    gathered = in_order(ag_f(jnp.concatenate([part, pad], axis=0)))
    wq = gathered[:, :S].reshape(D, 3 * W)
    small = jnp.transpose(gathered[:, S : S + 8, :S], (1, 0, 2)).reshape(8, D).astype(F32)
    gain1, gain2, shift1, shift2, q_bias, v_bias, o_bias, p_bias = [small[i : i + 1] for i in range(8)]
    qb, vb = (lax.dynamic_slice_in_dim(t, z * W, W, axis=1) for t in (q_bias, v_bias))
    bias3 = jnp.concatenate([qb, jnp.zeros_like(qb), vb], axis=1)
    wo = in_order(ag_f(w_out)).reshape(D, D)
    blocks = [lax.dynamic_slice_in_dim(w_fc, (f ^ i) * FS, FS, axis=1) for i in range(4)]
    wf = in_order([blocks[0]] + [flip(blocks[i], i) for i in range(1, 4)]).reshape(D, FS)
    fb = fc_bias.astype(F32)[None]
    dm_all = ag_f(cotangent[0]).reshape(4 * R, D)

    pos = slot_pos[0]
    ends = jnp.sum(jnp.tril(jnp.ones((lengths.shape[1],) * 2, jnp.int32)) * lengths[0][None], axis=1)

    def start_of(p):
        return jnp.max(jnp.where(ends[None, :] <= p[:, None], ends[None, :], 0), axis=1)

    th = thoughts[0]
    NT = th.shape[0]
    pos_y = take(pos.reshape(H, Q, R), y, 1).reshape(H * R)
    own_pos = take(pos.reshape(n_blk, R), b)

    def mask_of(p):
        return (pos[None, :] <= p[:, None]) & (pos[None, :] >= start_of(p)[:, None])

    mask_lat, mask_y = mask_of(th - 1), mask_of(pos_y)
    src = (pos[None, :] == th[:, None] - 1).astype(BF16)
    tgt = (pos[None, :] == th[:, None]).astype(BF16)
    tgt_y = (pos_y[None, :] == th[:, None]).astype(BF16)
    src_own = (own_pos[None, :] == th[:, None] - 1).astype(F32)
    tgt_own = (own_pos[None, :] == th[:, None]).astype(F32)
    is_th = jnp.sum(tgt, axis=0)[:, None] > 0
    is_th_y = jnp.sum(tgt_y, axis=0)[:, None] > 0
    is_th_own = jnp.sum(tgt_own, axis=0)[:, None] > 0

    X = X.reshape(T, D)
    normed, _, _ = norm(X.astype(F32), gain1, shift1)
    qkv = (dot(normed, wq) + bias3).astype(BF16)
    k0, v0 = qkv[:, W : 2 * W], qkv[:, 2 * W :]

    x_lat = dot(src, X)
    q_lat = dot(src, qkv[:, :W]).astype(BF16)
    ctx_lat, lse_lat = attend(q_lat, k0, v0, mask_lat)
    ctx_lat_all = jnp.transpose(ag_h(ctx_lat.astype(BF16)), (1, 0, 2)).reshape(NT, D)
    mid_lat = x_lat + (dot(ctx_lat_all, wo) + o_bias)
    second_lat, scaled2_lat, inv2_lat = norm(mid_lat, gain2, shift2)
    second_lat_all = ag_f(second_lat).reshape(4 * NT, D)
    hidden_lat = dot(second_lat_all, wf) + fb
    active_lat = gelu(hidden_lat).astype(BF16)
    lat_out = mid_lat + (rs_f(dot(active_lat, w_proj).reshape(4, NT, D)) + p_bias)
    normed_th, scaled_th, inv_th = norm(lat_out, gain1, shift1)
    qkv_th = (dot(normed_th, wq) + bias3).astype(BF16)

    qkv_tok = jnp.where(is_th, dot(tgt, qkv_th, 0, 0).astype(BF16), qkv)
    kt, vt = qkv_tok[:, W : 2 * W], qkv_tok[:, 2 * W :]
    q_y = take(qkv_tok[:, :W].reshape(H, Q, R, W), y, 1).reshape(H * R, W)
    ctx, lse = attend(q_y, kt, vt, mask_y)
    ctx_low = ctx.astype(BF16).reshape(H, R, W)
    got = jnp.stack([take(ctx_low, z)] + [shift_h(take(ctx_low, (z - k) % H), k) for k in range(1, H)])
    ctx_own = jnp.transpose(jnp.roll(got, z, axis=0), (1, 0, 2)).reshape(R, D)
    x_own = jnp.where(is_th_own, exact(tgt_own, lat_out, 0, 0), own.astype(F32))
    mid = x_own + (dot(ctx_own, wo) + o_bias)
    second, scaled2, inv2 = norm(mid, gain2, shift2)
    second_all = ag_f(second).reshape(4 * R, D)
    hidden = dot(second_all, wf) + fb
    active = gelu(hidden).astype(BF16)
    out = mid + (rs_f(dot(active, w_proj).reshape(4, R, D)) + p_bias)

    dh = (dot(dm_all, w_proj, 1, 1) * gelu_back(hidden)).astype(BF16)
    d_second = rs_f(dot(dh, wf, 1, 1).reshape(4, R, D))
    d_mid = cotangent[0].astype(F32) + norm_back(d_second, scaled2, inv2, gain2)
    da = d_mid.astype(BF16)
    d_ctx = dot(da, wo, 1, 1).astype(BF16).reshape(R, H, W)
    got = [take(d_ctx, z, 1)] + [shift_h(take(d_ctx, (z - k) % H, 1), k) for k in range(1, H)]
    grad_y = jnp.roll(jnp.stack(got), z, axis=0).reshape(H * R, W)
    dq, dk, dv = attend_back(q_y, kt, vt, mask_y, lse, ctx, grad_y)
    dq, dk, dv = dq.astype(BF16), dk.astype(BF16), dv.astype(BF16)
    d_th = jnp.concatenate([dot(tgt_y, dq), dot(tgt, dk), dot(tgt, dv)], axis=1).astype(BF16)
    gn_th = dot(d_th, wq, 1, 1)
    up = norm_back(gn_th, scaled_th, inv_th, gain1) + exact(tgt_own, d_mid)
    up = sum_q(up.astype(BF16).astype(F32).astype(BF16).astype(F32)) if Q != 2 else (
        up.astype(BF16).astype(F32) + shift_q(up.astype(BF16), 1).astype(F32)
    )
    up = up.astype(BF16)
    up = (up.astype(F32) + shift_h(up, 2).astype(F32)) + (
        shift_h(up, 1).astype(F32) + shift_h(up, 3).astype(F32)
    )

    dm_lat = up.astype(BF16)
    dm_lat_all = ag_f(dm_lat).reshape(4 * NT, D)
    dh_lat = (dot(dm_lat_all, w_proj, 1, 1) * gelu_back(hidden_lat)).astype(BF16)
    d_second_lat = rs_f(dot(dh_lat, wf, 1, 1).reshape(4, NT, D))
    d_mid_lat = up + norm_back(d_second_lat, scaled2_lat, inv2_lat, gain2)
    da_lat = d_mid_lat.astype(BF16)
    wo_h = take(wo.reshape(H, W, D), z)
    grad_lat = dot(da_lat, wo_h, 1, 1).astype(BF16)
    k_y = take(k0.reshape(H, Q, R, W), y, 1).reshape(H * R, W)
    v_y = take(v0.reshape(H, Q, R, W), y, 1).reshape(H * R, W)
    dq_l, dk_l, dv_l = attend_back(q_lat, k0, v0, mask_lat, lse_lat, ctx_lat, grad_lat)
    dk_l = take(dk_l.reshape(H, Q, R, W), y, 1).reshape(H * R, W)
    dv_l = take(dv_l.reshape(H, Q, R, W), y, 1).reshape(H * R, W)
    src_y = (pos_y[None, :] == th[:, None] - 1).astype(BF16)
    d_lat = jnp.concatenate([dot(src_y, dq_l.astype(BF16), 0, 0), dk_l, dv_l], axis=1)

    kv = jnp.concatenate([dk, dv], axis=1).reshape(H, Q, R, 2 * W)
    d_kv = rs_q(jnp.transpose(kv, (1, 0, 2, 3))).reshape(H * R, 2 * W)
    d_tok = jnp.concatenate([dq.astype(F32), d_kv], axis=1)
    d_all = (jnp.where(is_th_y, 0.0, d_tok) + d_lat).astype(BF16)
    d_tok_th = dot(tgt_y, d_tok.astype(BF16)).astype(BF16)
    normed_y = take(normed.reshape(H, Q, R, D), y, 1).reshape(H * R, D)
    g_q = dot(normed_y, d_all, 0, 0) + dot(normed_th, d_tok_th, 0, 0)
    gn = dot(d_all, wq, 1, 1).astype(BF16).reshape(H, R, D)
    gn_own = rs_h(gn)
    _, scaled1, inv1 = norm(own.astype(F32), gain1, shift1)
    grad_in = jnp.where(is_th_own, 0.0, d_mid) + norm_back(gn_own, scaled1, inv1, gain1)
    grad_in = grad_in + exact(src_own, d_mid_lat, 0, 0)

    da_all = ag_f(da).reshape(4 * R, D)
    ctx_cols = [lax.dynamic_slice_in_dim(ctx_own, (f ^ i) * S, S, axis=1) for i in range(4)]
    ctx_all = jnp.concatenate([ctx_cols[0]] + [flip(ctx_cols[i], i) for i in range(1, 4)], axis=0)
    g_proj = dot(active, dm_all, 0, 0)
    g_fc = dot(second_all, dh, 0, 0)
    g_out = dot(ctx_all, da_all, 0, 0)
    stack = jnp.concatenate(
        [
            g_proj.astype(BF16).reshape(n_blk, FS // n_blk, D),
            jnp.transpose(
                g_fc.astype(BF16).reshape(n_f, n_blk, S // n_blk, FS), (1, 0, 2, 3)
            ).reshape(n_blk, D // n_blk, FS),
            g_out.astype(BF16).reshape(n_blk, S // n_blk, D),
        ],
        axis=1,
    )
    rows = stack.shape[1]
    stack = stack.reshape(H, Q, rows, D)
    mine = rs_h(rs_q(jnp.transpose(stack, (1, 0, 2, 3))).astype(BF16)).astype(BF16)
    c1, c2 = FS // n_blk, FS // n_blk + D // n_blk
    fc_mine = mine[c1:c2].reshape(n_f, S // n_blk, FS)
    fc_cols = in_order(
        [take(fc_mine, f)] + [flip(take(fc_mine, f ^ i), i) for i in range(1, 4)]
    )
    piece = jnp.concatenate([mine[:c1], fc_cols.reshape(D // n_blk, FS), mine[c2:]], axis=0)
    every = jnp.transpose(ag_q(ag_h(piece)), (1, 0, 2, 3)).reshape(n_blk, rows, D)
    w_proj_g = every[:, :c1].reshape(FS, D).astype(F32)
    w_fc_g = jnp.transpose(
        every[:, c1:c2].reshape(n_blk, n_f, S // n_blk, FS), (0, 2, 1, 3)
    ).reshape(S, n_f * FS).astype(F32)
    w_out_g = every[:, c2:].reshape(S, D).astype(F32)
    w_proj_g = w_proj_g + dot(active_lat, dm_lat_all, 0, 0)
    dh_lat_all = in_order(ag_f(dh_lat))
    second_cols = lax.dynamic_slice_in_dim(second_lat_all, f * S, S, axis=1).reshape(4, NT, S)
    parts = []
    for i in range(4):
        order = in_order(second_cols)
        mine_rows = jnp.concatenate([order[i ^ j] for j in range(4)], axis=0)
        parts.append(dot(mine_rows, dh_lat_all[i], 0, 0))
    w_fc_g = w_fc_g + jnp.concatenate(parts, axis=1)
    lat_cols = [lax.dynamic_slice_in_dim(ctx_lat_all, (f ^ i) * S, S, axis=1) for i in range(4)]
    ctx_lat_cols = jnp.concatenate([lat_cols[0]] + [flip(lat_cols[i], i) for i in range(1, 4)], axis=0)
    da_lat_all = ag_f(da_lat).reshape(4 * NT, D)
    w_out_g = w_out_g + dot(ctx_lat_cols, da_lat_all, 0, 0)

    gq = g_q.reshape(4, S, 3 * W)
    gq = rs_f(in_order(gq)).astype(BF16)
    gq = gq.astype(F32) + shift_q(gq, 1).astype(F32) if Q == 2 else sum_q(gq.astype(F32))
    gq = ag_h(gq.astype(BF16))
    w_qkv_g = jnp.transpose(gq.reshape(H, S, 3, W), (1, 2, 0, 3)).reshape(S, 3 * D).astype(F32)

    once = jnp.where(b == 0, 1.0, 0.0)
    col = lambda t: jnp.sum(t.astype(F32), axis=0)
    d_bias = col(d_all) + col(d_tok_th)
    place = lambda v: lax.dynamic_update_slice(jnp.zeros((D,), F32), v, (z * W,))
    gn_f = gn.reshape(H * R, D).astype(F32)
    X_y = take(X.reshape(H, Q, R, D), y, 1).reshape(H * R, D)
    _, scaled_y, _ = norm(X_y.astype(F32), gain1, shift1)
    rows_small = jnp.stack(
        [
            col(gn_f * scaled_y) + col(gn_th * scaled_th),
            col(d_second * scaled2) + once * col(d_second_lat * scaled2_lat),
            col(gn_f) + col(gn_th),
            col(d_second) + once * col(d_second_lat),
            place(d_bias[:W]),
            place(d_bias[2 * W :]),
            col(da) + once * col(da_lat),
            col(cotangent[0]) + once * col(dm_lat),
        ]
    )
    d_fc_bias = lax.dynamic_update_slice(
        jnp.zeros((4, FS), F32), (col(dh) + once * col(dh_lat))[None], (f, 0)
    )
    sums = jnp.concatenate([rows_small, d_fc_bias], axis=0)
    sums = sums + flip(sums, 1)
    sums = sums + flip(sums, 2)
    sums = sum_h(sum_q(sums))
    mine_small = lax.dynamic_slice_in_dim(sums[:8], f * S, S, axis=1)
    return (
        out.astype(BF16)[None],
        grad_in[None],
        mine_small[0:2],
        mine_small[2:4],
        w_qkv_g,
        mine_small[4:6],
        w_out_g,
        mine_small[6],
        w_fc_g,
        take(sums[8:], f),
        w_proj_g,
        mine_small[7],
    )


def solution(mesh):
    a, r, v = P("fsdp", "blk", None), P("fsdp", None), P("fsdp")
    c = P(None, "fsdp")
    return jax.shard_map(
        local,
        mesh=mesh,
        in_specs=(a, r, r, r, c, c, r, c, r, v, r, v, r, v, a),
        out_specs=(a, a, c, c, r, c, r, v, r, v, r, v),
        check_vma=False,
    )
```

```python
import jax
import jax.numpy as jnp
from jax import lax
from jax.experimental import pallas as pl
from jax.experimental.pallas import tpu as pltpu
from jax.sharding import PartitionSpec as P

HDIM = 64
PARTS = 4
EPS = 1e-05
SCALE = HDIM ** (-0.5)
F32 = jnp.float32
BF16 = jnp.bfloat16
VMEM_BYTES = 60 * 1024 * 1024
INTERPRET = False


def dot(a, b, ca=1, cb=0):
    return lax.dot_general(a, b, (((ca,), (cb,)), ((), ())), preferred_element_type=F32)


def spread(hot, x, axis):
    total = None
    for _ in range(3):
        low = x.astype(BF16)
        x = x - low.astype(F32)
        part = dot(hot, low, axis, 0)
        total = part if total is None else total + part
    return total


def norm(x, gain, shift):
    center = x - jnp.mean(x, axis=-1, keepdims=True)
    inverse = lax.rsqrt(jnp.mean(center * center, axis=-1, keepdims=True) + EPS)
    scaled = center * inverse
    return (scaled * gain + shift).astype(BF16), scaled, inverse


def norm_back(up, scaled, inverse, gain):
    w = up * gain
    return inverse * (
        w - jnp.mean(w, axis=-1, keepdims=True) - scaled * jnp.mean(w * scaled, axis=-1, keepdims=True)
    )


C0 = 0.7978845608028654
C1 = 0.044715


def gelu(v):
    return 0.5 * v * (1.0 + jnp.tanh(C0 * (v + C1 * v * v * v)))


def gelu_back(v):
    t = jnp.tanh(C0 * (v + C1 * v * v * v))
    return 0.5 * (1.0 + t) + 0.5 * v * (1.0 - t * t) * C0 * (1.0 + 3 * C1 * v * v)


def start_of(p, len_ref):
    start = jnp.zeros_like(p)
    end = jnp.int32(0)
    for i in range(len_ref.shape[1] - 1):
        end = end + len_ref[0, i]
        start = jnp.where(p >= end, end, start)
    return start


def sds(shape, dtype):
    return jax.ShapeDtypeStruct(shape, dtype)


def call(body, name, args, outs, scratch=(), n_smem=1):
    vm = pl.BlockSpec(memory_space=pltpu.VMEM)
    sm = pl.BlockSpec(memory_space=pltpu.SMEM)
    return pl.pallas_call(
        body,
        name=name,
        out_shape=list(outs),
        in_specs=[sm] * n_smem + [vm] * (len(args) - n_smem),
        out_specs=[vm] * len(outs),
        scratch_shapes=list(scratch),
        compiler_params=pltpu.CompilerParams(vmem_limit_bytes=VMEM_BYTES),
        interpret=INTERPRET,
    )(*args)


def local(
    tokens, slot_pos, lengths, thoughts, ln_gain, ln_shift, w_qkv, qv_bias, w_out, out_bias,
    w_fc, fc_bias, w_proj, proj_bias, cotangent,
):
    n_blk, n_f = lax.axis_size("blk"), lax.axis_size("fsdp")
    H = PARTS
    Q = n_blk // H
    b, f = lax.axis_index("blk"), lax.axis_index("fsdp")
    z, y = b // Q, b % Q
    R, D = tokens.shape[1], tokens.shape[2]
    T = R * n_blk
    W = D // H
    NH = W // HDIM
    S = D // n_f
    FS = w_proj.shape[0]
    NT = thoughts.shape[1]
    NQ = H * R
    KB = min(T, 256)

    def take(x, i, axis=0):
        return lax.dynamic_index_in_dim(x, i, axis, keepdims=False)

    def flip_h(x, k):
        return lax.ppermute(x, "blk", [((((c // Q) ^ k) * Q) + c % Q, c) for c in range(n_blk)])

    def shift_q(x, j):
        return lax.ppermute(x, "blk", [((c // Q) * Q + (c % Q + j) % Q, c) for c in range(n_blk)])

    def flip(x, bit):
        return lax.ppermute(x, "fsdp", [(c, c ^ bit) for c in range(n_f)])

    def gather_f(x):
        far = flip(x, 2)
        return [x, flip(x, 1), far, flip(far, 1)]

    def gather_h(x):
        return [x] + [flip_h(x, k) for k in range(1, H)]

    def barrier(*xs):
        return lax.optimization_barrier(xs)

    ids = jnp.stack([z, y, f, b]).astype(jnp.int32)[None]

    own = tokens[0]
    cot = cotangent[0]
    small = jnp.concatenate(
        [ln_gain, ln_shift, qv_bias, out_bias[None], proj_bias[None]], axis=0
    )

    def pack_body(ids_ref, w_ref, small_ref, out_ref):
        zz = ids_ref[0, 0]
        for c in range(H):

            @pl.when(zz == c)
            def _():
                for i in range(3):
                    out_ref[0:S, i * W : (i + 1) * W] = w_ref[:, i * D + c * W : i * D + (c + 1) * W]

        rows = jnp.concatenate([small_ref[...].astype(F32), jnp.zeros((8, S), F32)], axis=0)
        rows = jnp.concatenate([rows, jnp.zeros((16, 3 * W - S), F32)], axis=1)
        out_ref[S : S + 16, :] = rows.astype(BF16)

    def pack2_body(ids_ref, fc_ref, wo_ref, cot_ref, far_ref, near_ref):
        ff = ids_ref[0, 2]

        def block(i):
            return fc_ref[:, pl.ds(pl.multiple_of((ff ^ i) * FS, 128), FS)]

        for ref in (far_ref, near_ref):
            ref[0:S] = wo_ref[...]
            ref[S : S + R] = cot_ref[...]
        far_ref[S + R : 2 * S + R] = block(3)
        far_ref[2 * S + R :] = block(2)
        near_ref[S + R :] = block(1)

    [part] = call(pack_body, "pack", [ids, w_qkv, small], [sds((S + 16, 3 * W), BF16)])
    blocks_y = gather_h(own)
    parts = gather_f(part)
    blocks = [blocks_y]
    for j in range(1, Q):
        blocks.append([shift_q(x, j) for x in blocks_y])
    far0, near0 = call(
        pack2_body, "pack2", [ids, w_fc, w_out, cot],
        [sds((3 * S + R, D), BF16), sds((2 * S + R, D), BF16)],
    )
    far_got = flip(far0, 2)
    near_got = flip(near0, 1)
    both_got = flip(far_got, 1)

    pos = slot_pos
    pos_col = slot_pos.reshape(T, 1)
    pos_blk = slot_pos.reshape(n_blk, R)
    th_row = thoughts
    th_col = thoughts.reshape(NT, 1)

    def proj_body(ids_ref, p0, p1, p2, p3, x0, x1, x2, x3, qkv_ref, wq_ref, vec_ref, normed_ref):
        zz, ff = ids_ref[0, 0], ids_ref[0, 2]
        smalls = []
        for i, p in enumerate((p0, p1, p2, p3)):
            wq_ref[pl.ds(pl.multiple_of((ff ^ i) * S, 64), S), :] = p[0:S, :]
            smalls.append(p[S : S + 16, 0:S].astype(F32)[0:8])
        for a in range(4):
            v = smalls[0]
            for i in range(1, 4):
                v = jnp.where((ff ^ i) == a, smalls[i], v)
            vec_ref[:, a * S : (a + 1) * S] = v
        bias = bias_of(vec_ref, zz)
        for k, x in enumerate((x0, x1, x2, x3)):
            n, _, _ = norm(x[...].astype(F32), vec_ref[0:1, :], vec_ref[2:3, :])
            normed_ref[k] = n
            qkv_ref[k] = (dot(n, wq_ref[...]) + bias).astype(BF16)

    def bias_of(vec_ref, zz):
        qb = vec_ref[4:5, 0:W]
        vb = vec_ref[5:6, 0:W]
        for c in range(1, H):
            qb = jnp.where(zz == c, vec_ref[4:5, c * W : (c + 1) * W], qb)
            vb = jnp.where(zz == c, vec_ref[5:6, c * W : (c + 1) * W], vb)
        return jnp.concatenate([qb, jnp.zeros_like(qb), vb], axis=1)

    def proj_more(ids_ref, wq_ref, vec_ref, x0, x1, x2, x3, qkv_ref):
        bias = bias_of(vec_ref, ids_ref[0, 0])
        for k, x in enumerate((x0, x1, x2, x3)):
            n, _, _ = norm(x[...].astype(F32), vec_ref[0:1, :], vec_ref[2:3, :])
            qkv_ref[k] = (dot(n, wq_ref[...]) + bias).astype(BF16)

    qkv_y, wq, vec, normed_y = call(
        proj_body, "project", [ids, *parts, *blocks[0]],
        [sds((H, R, 3 * W), BF16), sds((D, 3 * W), BF16), sds((8, D), F32), sds((H, R, D), BF16)],
    )
    qkvs = [qkv_y]
    for j in range(1, Q):
        qkvs += call(
            proj_more, "project_more", [ids, wq, vec, *blocks[j]], [sds((H, R, 3 * W), BF16)]
        )

    def attend(q, read_k, read_v, key_pos, q_pos, q_start, s_ref):
        n = q.shape[0]
        ctx, lse = [], []
        for h in range(NH):
            lanes = slice(h * HDIM, (h + 1) * HDIM)
            qh = q[:, lanes]

            def score(i, m):
                at = pl.multiple_of(i * KB, KB)
                s = dot(read_k(at, lanes), qh, 1, 1) * SCALE
                kp = key_pos(at)
                s = jnp.where((kp <= q_pos) & (kp >= q_start), s, -1e30)
                s_ref[pl.ds(at, KB), 0:n] = s
                return jnp.maximum(m, jnp.max(s, axis=0, keepdims=True))

            m = lax.fori_loop(0, T // KB, score, jnp.full((1, n), -1e30, F32), unroll=T // KB <= 4)

            def add(i, carry):
                total, acc = carry
                at = pl.multiple_of(i * KB, KB)
                e = jnp.exp(s_ref[pl.ds(at, KB), 0:n] - m)
                total = total + jnp.sum(e, axis=0, keepdims=True)
                return total, acc + dot(read_v(at, lanes), e.astype(BF16), 0, 0)

            total, acc = lax.fori_loop(
                0, T // KB, add, (jnp.zeros((1, n), F32), jnp.zeros((HDIM, n), F32)), unroll=T // KB <= 4
            )
            ctx.append(acc / total)
            lse.append(m + jnp.log(total))
        return jnp.concatenate(ctx, axis=0), jnp.concatenate(lse, axis=0)

    def latent_body(*refs):
        ids_ref, len_ref, pos_ref, posb_ref, posc_ref, thr_ref, thc_ref = refs[:7]
        qkv_refs = refs[7 : 7 + Q]
        x_refs = refs[7 + Q : 7 + Q + n_blk]
        low_ref, ctx_ref, lse_ref, q_ref, x_ref, abs_ref, s_ref = refs[7 + Q + n_blk :]
        zz, yy = ids_ref[0, 0], ids_ref[0, 1]
        src = thc_ref[...] - 1
        x_lat = jnp.zeros((NT, D), F32)
        for j in range(Q):
            for k in range(H):
                a = (zz ^ k) * Q + lax.rem(yy + j, Q)
                abs_ref[pl.ds(pl.multiple_of(a * R, R), R), :] = qkv_refs[j][k]
                hot = jnp.where(posb_ref[pl.ds(a, 1), :] == src, 1.0, 0.0).astype(BF16)
                x_lat = x_lat + dot(hot, x_refs[j * H + k][...])
        x_ref[...] = x_lat
        hot = jnp.where(pos_ref[...] == src, 1.0, 0.0).astype(BF16)
        q = dot(hot, abs_ref[:, 0:W]).astype(BF16)
        q_ref[...] = q
        p = thr_ref[...] - 1
        ctx, lse = attend(
            q,
            lambda at, c: abs_ref[pl.ds(at, KB), W + c.start : W + c.stop],
            lambda at, c: abs_ref[pl.ds(at, KB), 2 * W + c.start : 2 * W + c.stop],
            lambda at: posc_ref[pl.ds(at, KB), :],
            p,
            start_of(p, len_ref),
            s_ref,
        )
        ctx_ref[...] = ctx
        lse_ref[...] = lse
        low_ref[...] = ctx.T.astype(BF16)

    flat = [x for group in blocks for x in group]
    ctx_lat_low, ctx_lat, lse_lat, q_lat, x_lat, qkv_abs = call(
        latent_body, "latent_attention",
        [ids, lengths, pos, pos_blk, pos_col, th_row, th_col, *qkvs, *flat],
        [
            sds((NT, W), BF16), sds((W, NT), F32), sds((NH, NT), F32), sds((NT, W), BF16),
            sds((NT, D), F32), sds((T, 3 * W), BF16),
        ],
        scratch=[pltpu.VMEM((T, 128), F32)],
        n_smem=2,
    )
    ctx_lat_blocks = gather_h(ctx_lat_low)

    def place_body(ids_ref, far0_ref, near0_ref, far_ref, near_ref, both_ref, fc_ref, wo_ref, wf_ref, dm_ref):
        ff = ids_ref[0, 2]

        def at(i):
            return pl.ds(pl.multiple_of((ff ^ i) * S, 64), S)

        for i, ref in enumerate((far0_ref, near_ref, far_ref, both_ref)):
            wo_ref[at(i), :] = ref[0:S]
            dm_ref[i * R : (i + 1) * R] = ref[S : S + R]
        wf_ref[at(0), :] = fc_ref[:, pl.ds(pl.multiple_of(ff * FS, 128), FS)]
        wf_ref[at(1), :] = near_ref[S + R :]
        wf_ref[at(2), :] = far_ref[2 * S + R :]
        wf_ref[at(3), :] = both_ref[S + R : 2 * S + R]

    wo, wf, dm_all = call(
        place_body, "place", [ids, far0, near0, far_got, near_got, both_got, w_fc],
        [sds((D, D), BF16), sds((D, FS), BF16), sds((4 * R, D), BF16)],
    )
    fb = fc_bias[None]

    def latent_out_body(ids_ref, c0, c1, c2, c3, x_ref, wo_ref, vec_ref, mid_ref, low_ref, all_ref, tmp):
        zz = ids_ref[0, 0]
        for k, c in enumerate((c0, c1, c2, c3)):
            tmp[zz ^ k] = c[...]
        for i in range(H):
            all_ref[:, i * W : (i + 1) * W] = tmp[i]
        mid = x_ref[...] + (dot(all_ref[...], wo_ref[...]) + vec_ref[6:7, :])
        mid_ref[...] = mid
        low_ref[...] = norm(mid, vec_ref[1:2, :], vec_ref[3:4, :])[0]

    mid_lat, second_lat, ctx_lat_all = call(
        latent_out_body, "latent_out", [ids, *ctx_lat_blocks, x_lat, wo, vec],
        [sds((NT, D), F32), sds((NT, D), BF16), sds((NT, D), BF16)],
        scratch=[pltpu.VMEM((H, NT, W), BF16)],
    )
    second_lat_blocks = gather_f(second_lat)

    def latent_ffn_body(s0, s1, s2, s3, wf_ref, wp_ref, fb_ref, hid_ref, act_ref, all_ref, o0, o1, o2, o3):
        for i, s in enumerate((s0, s1, s2, s3)):
            all_ref[i * NT : (i + 1) * NT] = s[...]
        hidden = dot(all_ref[...], wf_ref[...]) + fb_ref[...].astype(F32)
        hid_ref[...] = hidden
        act_ref[...] = gelu(hidden).astype(BF16)
        out = dot(act_ref[...], wp_ref[...])
        for i, o in enumerate((o0, o1, o2, o3)):
            o[...] = out[i * NT : (i + 1) * NT].astype(o.dtype)

    hidden_lat, active_lat, second_lat_all, *outs = call(
        latent_ffn_body, "latent_ffn", [*second_lat_blocks, wf, w_proj, fb],
        [sds((4 * NT, FS), F32), sds((4 * NT, FS), BF16), sds((4 * NT, D), BF16), sds((NT, D), F32)]
        + [sds((NT, D), BF16)] * 3,
        n_smem=0,
    )
    outs = [outs[0]] + [flip(outs[i], i) for i in range(1, 4)]

    def token_body(
        ids_ref, len_ref, o0, o1, o2, o3, mid_ref, vec_ref, wq_ref, abs_ref, qy_ref, posb_ref, posc_ref, thr_ref,
        lat_ref, nth_ref, kv_ref, q_ref, ctx_ref, lse_ref, c0, c1, c2, c3, s_ref,
    ):
        zz, yy = ids_ref[0, 0], ids_ref[0, 1]
        lat = mid_ref[...] + (
            (o0[...] + o1[...].astype(F32) + (o2[...].astype(F32) + o3[...].astype(F32))) + vec_ref[7:8, :]
        )
        lat_ref[...] = lat
        nth = norm(lat, vec_ref[0:1, :], vec_ref[2:3, :])[0]
        nth_ref[...] = nth
        qkv_th = (dot(nth, wq_ref[...]) + bias_of(vec_ref, zz)).astype(BF16)

        def fill(i, _):
            at = pl.multiple_of(i * KB, KB)
            hot = posc_ref[pl.ds(at, KB), :] == thr_ref[...]
            is_th = jnp.max(jnp.where(hot, 1.0, 0.0), axis=1, keepdims=True) > 0
            new = dot(jnp.where(hot, 1.0, 0.0).astype(BF16), qkv_th[:, W:])
            kv_ref[pl.ds(at, KB), :] = jnp.where(is_th, new, abs_ref[pl.ds(at, KB), W:].astype(F32)).astype(BF16)
            return 0

        lax.fori_loop(0, T // KB, fill, 0, unroll=T // KB <= 4)
        rows = []
        for k in range(H):
            a = (zz ^ k) * Q + yy
            hot = posc_ref[pl.ds(pl.multiple_of(a * R, R), R), :] == thr_ref[...]
            is_th = jnp.max(jnp.where(hot, 1.0, 0.0), axis=1, keepdims=True) > 0
            new = dot(jnp.where(hot, 1.0, 0.0).astype(BF16), qkv_th[:, 0:W])
            q_ref[k] = jnp.where(is_th, new, qy_ref[k][:, 0:W].astype(F32)).astype(BF16)
            rows.append(posb_ref[pl.ds(a, 1), :])
        p = jnp.concatenate(rows, axis=1)
        ctx, lse = attend(
            q_ref[...].reshape(NQ, W),
            lambda at, c: kv_ref[pl.ds(at, KB), c],
            lambda at, c: kv_ref[pl.ds(at, KB), W + c.start : W + c.stop],
            lambda at: posc_ref[pl.ds(at, KB), :],
            p,
            start_of(p, len_ref),
            s_ref,
        )
        ctx_ref[...] = ctx
        lse_ref[...] = lse
        low = ctx.T.astype(BF16)
        for k, c in enumerate((c0, c1, c2, c3)):
            c[...] = low[k * R : (k + 1) * R]

    lat_out, normed_th, kv_tok, q_tok, ctx_t, lse, *ctx_blocks = call(
        token_body, "token_attention",
        [ids, lengths, *outs, mid_lat, vec, wq, qkv_abs, qkv_y, pos_blk, pos_col, th_row],
        [
            sds((NT, D), F32), sds((NT, D), BF16), sds((T, 2 * W), BF16), sds((H, R, W), BF16),
            sds((W, NQ), F32), sds((NH, NQ), F32),
        ]
        + [sds((R, W), BF16)] * 4,
        scratch=[pltpu.VMEM((T, NQ), F32)],
        n_smem=2,
    )
    ctx_blocks = [ctx_blocks[0]] + [flip_h(ctx_blocks[k], k) for k in range(1, H)]
    own_pos = lax.dynamic_slice_in_dim(pos_col, b * R, R, axis=0)

    def token_out_body(
        ids_ref, c0, c1, c2, c3, x_ref, posc_ref, thr_ref, lat_ref, wo_ref, vec_ref, mid_ref, low_ref, all_ref, tmp
    ):
        zz = ids_ref[0, 0]
        for k, c in enumerate((c0, c1, c2, c3)):
            tmp[zz ^ k] = c[...]
        for i in range(H):
            all_ref[:, i * W : (i + 1) * W] = tmp[i]
        hot = jnp.where(posc_ref[...] == thr_ref[...], 1.0, 0.0)
        is_th = jnp.max(hot, axis=1, keepdims=True) > 0
        x = jnp.where(is_th, spread(hot.astype(BF16), lat_ref[...], 1), x_ref[...].astype(F32))
        mid = x + (dot(all_ref[...], wo_ref[...]) + vec_ref[6:7, :])
        mid_ref[...] = mid
        low_ref[...] = norm(mid, vec_ref[1:2, :], vec_ref[3:4, :])[0]

    mid, second, ctx_own = call(
        token_out_body, "token_out", [ids, *ctx_blocks, own, own_pos, th_row, lat_out, wo, vec],
        [sds((R, D), F32), sds((R, D), BF16), sds((R, D), BF16)],
        scratch=[pltpu.VMEM((H, R, W), BF16)],
    )
    second_blocks = gather_f(second)

    def ffn_body(s0, s1, s2, s3, dm_ref, wf_ref, wp_ref, fb_ref, act_ref, dh_ref, all_ref, sum_ref, o0, o1, o2, o3):
        for i, (s, o) in enumerate(zip((s0, s1, s2, s3), (o0, o1, o2, o3))):
            rows = slice(i * R, (i + 1) * R)
            all_ref[rows] = s[...]
            hidden = dot(s[...], wf_ref[...]) + fb_ref[...].astype(F32)
            t = jnp.tanh(C0 * (hidden + C1 * hidden * hidden * hidden))
            act_ref[rows] = (0.5 * hidden * (1.0 + t)).astype(BF16)
            back = 0.5 * (1.0 + t) + 0.5 * hidden * (1.0 - t * t) * C0 * (1.0 + 3 * C1 * hidden * hidden)
            dh = (dot(dm_ref[rows], wp_ref[...], 1, 1) * back).astype(BF16)
            dh_ref[rows] = dh
            o[...] = dot(dh, wf_ref[...], 1, 1).astype(o.dtype)
        sum_ref[...] = jnp.sum(dh_ref[...].astype(F32), axis=0, keepdims=True)

    active, dh, second_all, dh_sum, *back = call(
        ffn_body, "ffn", [*second_blocks, dm_all, wf, w_proj, fb],
        [sds((4 * R, FS), BF16), sds((4 * R, FS), BF16), sds((4 * R, D), BF16), sds((1, FS), F32), sds((R, D), F32)]
        + [sds((R, D), BF16)] * 3,
        n_smem=0,
    )
    back = [back[0]] + [flip(back[i], i) for i in range(1, 4)]

    def grads_body(act_ref, dh_ref, all_ref, dm_ref, wp_ref, gp_ref, gf_ref, o0, o1, o2, o3):
        out = dot(act_ref[...], wp_ref[...])
        for i, o in enumerate((o0, o1, o2, o3)):
            o[...] = out[i * R : (i + 1) * R].astype(o.dtype)
        gp_ref[...] = dot(act_ref[...], dm_ref[...], 0, 0).astype(BF16)
        gf_ref[...] = dot(dh_ref[...], all_ref[...], 0, 0).astype(BF16)

    g_proj, g_fct, *res = call(
        grads_body, "ffn_grads", [active, dh, second_all, dm_all, w_proj],
        [sds((FS, D), BF16), sds((FS, D), BF16), sds((R, D), F32)] + [sds((R, D), BF16)] * 3,
        n_smem=0,
    )
    res = [res[0]] + [flip(res[i], i) for i in range(1, 4)]

    def attn_in_body(ids_ref, b0, b1, b2, b3, mid_ref, cot_ref, wo_ref, vec_ref, dmid_ref, da_ref, sum_ref, c0, c1, c2, c3):
        zz = ids_ref[0, 0]
        up = (b0[...] + b1[...].astype(F32)) + (b2[...].astype(F32) + b3[...].astype(F32))
        _, scaled, inverse = norm(mid_ref[...], vec_ref[1:2, :], vec_ref[3:4, :])
        cot_now = cot_ref[...].astype(F32)
        d_mid = cot_now + norm_back(up, scaled, inverse, vec_ref[1:2, :])
        dmid_ref[...] = d_mid
        da = d_mid.astype(BF16)
        da_ref[...] = da
        for k, c in enumerate((c0, c1, c2, c3)):
            w = wo_ref[pl.ds(pl.multiple_of((zz ^ k) * W, 64), W), :]
            c[...] = dot(da, w, 1, 1).astype(BF16)
        sum_ref[0:1] = jnp.sum(up * scaled, axis=0, keepdims=True)
        sum_ref[1:2] = jnp.sum(up, axis=0, keepdims=True)
        sum_ref[2:3] = jnp.sum(da.astype(F32), axis=0, keepdims=True)
        sum_ref[3:4] = jnp.sum(cot_now, axis=0, keepdims=True)

    d_mid, da, sums2, *grad_blocks = call(
        attn_in_body, "attention_gradient", [ids, *back, mid, cot, wo, vec],
        [sds((R, D), F32), sds((R, D), BF16), sds((4, D), F32)] + [sds((R, W), BF16)] * 4,
    )
    grad_blocks = [grad_blocks[0]] + [flip_h(grad_blocks[k], k) for k in range(1, H)]

    def out_grad_body(ids_ref, ctx_ref, da_ref, o0, o1, o2, o3, tmp):
        ff = ids_ref[0, 2]
        tmp[...] = dot(ctx_ref[...], da_ref[...], 0, 0)
        for i, o in enumerate((o0, o1, o2, o3)):
            o[...] = tmp[pl.ds(pl.multiple_of((ff ^ i) * S, 64), S), :].astype(o.dtype)

    g_out = call(
        out_grad_body, "out_grad", [ids, ctx_own, da],
        [sds((S, D), F32)] + [sds((S, D), BF16)] * 3,
        scratch=[pltpu.VMEM((D, D), F32)],
    )
    g_out = [g_out[0]] + [flip(g_out[i], i) for i in range(1, 4)]

    def attend_back(q, g, read_k, read_v, key_pos, q_pos, q_start, lse, ctx, n_keys, put):
        n = q.shape[0]
        g_t = g.astype(F32).T
        dqs = []
        deltas = [
            jnp.sum(g_t[h * HDIM : (h + 1) * HDIM] * ctx[h * HDIM : (h + 1) * HDIM], axis=0, keepdims=True)
            for h in range(NH)
        ]

        def step(i, dq):
            at = pl.multiple_of(i * KB, KB)
            kp = key_pos(at)
            mask = (kp <= q_pos) & (kp >= q_start)
            dks, dvs, new = [], [], []
            for h in range(NH):
                lanes = slice(h * HDIM, (h + 1) * HDIM)
                kh = read_k(at, lanes)
                s = dot(kh, q[:, lanes], 1, 1) * SCALE
                p = jnp.where(mask, jnp.exp(s - lse[h : h + 1]), 0.0)
                dp = dot(read_v(at, lanes), g[:, lanes], 1, 1)
                ds = (p * (dp - deltas[h])).astype(BF16)
                new.append(dq[h] + dot(kh, ds, 0, 0))
                dks.append(dot(ds, q[:, lanes]) * SCALE)
                dvs.append(dot(p.astype(BF16), g[:, lanes]))
            put(at, jnp.concatenate(dks, axis=1), jnp.concatenate(dvs, axis=1))
            return tuple(new)

        dq = lax.fori_loop(
            0, n_keys // KB, step, tuple(jnp.zeros((HDIM, n), F32) for _ in range(NH)), unroll=n_keys // KB <= 4
        )
        return jnp.concatenate(dq, axis=0).T * SCALE

    def token_back_body(
        ids_ref, len_ref, g0, g1, g2, g3, q_ref, kv_ref, ctx_ref, lse_ref, pos_ref, posb_ref, posc_ref, thr_ref, thc_ref,
        ownp_ref, wq_ref, lat_ref, vec_ref, dmid_ref,
        up_ref, dq_ref, dkv_ref, sum_ref, *rest,
    ):
        msgs, acc = rest[:-1], rest[-1]
        zz, yy = ids_ref[0, 0], ids_ref[0, 1]
        rows = [posb_ref[pl.ds((zz ^ k) * Q + yy, 1), :] for k in range(H)]
        p = jnp.concatenate(rows, axis=1)

        def put(at, dk, dv):
            acc[pl.ds(at, KB), 0:W] = dk
            acc[pl.ds(at, KB), W:] = dv

        dq = attend_back(
            q_ref[...].reshape(NQ, W),
            jnp.concatenate([g0[...], g1[...], g2[...], g3[...]], axis=0),
            lambda at, c: kv_ref[pl.ds(at, KB), c],
            lambda at, c: kv_ref[pl.ds(at, KB), W + c.start : W + c.stop],
            lambda at: posc_ref[pl.ds(at, KB), :],
            p,
            start_of(p, len_ref),
            lse_ref[...],
            ctx_ref[...],
            T,
            put,
        ).astype(BF16)
        hot_y = jnp.where(p == thc_ref[...], 1.0, 0.0).astype(BF16)
        hot = jnp.where(pos_ref[...] == thc_ref[...], 1.0, 0.0).astype(BF16)
        d_q = dot(hot_y, dq).astype(BF16)
        d_kv = dot(hot, acc[...].astype(BF16)).astype(BF16)
        gn = dot(d_q, wq_ref[:, 0:W], 1, 1) + dot(d_kv, wq_ref[:, W:], 1, 1)
        _, scaled, inverse = norm(lat_ref[...], vec_ref[0:1, :], vec_ref[2:3, :])
        sum_ref[0:1] = jnp.sum(gn * scaled, axis=0, keepdims=True)
        sum_ref[1:2] = jnp.sum(gn, axis=0, keepdims=True)
        hot_own = jnp.where(ownp_ref[...] == thr_ref[...], 1.0, 0.0).astype(BF16)
        up = norm_back(gn, scaled, inverse, vec_ref[0:1, :]) + spread(hot_own, dmid_ref[...], 0)
        up_ref[...] = up.astype(BF16)
        for k in range(H):
            dq_ref[k] = dq[k * R : (k + 1) * R]
            for j in range(Q):
                a = (zz ^ k) * Q + lax.rem(yy - j + Q, Q)
                block = acc[pl.ds(pl.multiple_of(a * R, R), R), :]
                if j == 0:
                    dkv_ref[k] = block
                else:
                    msgs[j - 1][k] = block.astype(BF16)

    up, dq, dkv, sums1, *kv_msgs = call(
        token_back_body, "token_backward",
        [
            ids, lengths, *grad_blocks, q_tok, kv_tok, ctx_t, lse, pos, pos_blk, pos_col, th_row, th_col,
            own_pos, wq, lat_out, vec, d_mid,
        ],
        [sds((NT, D), BF16), sds((H, R, W), BF16), sds((H, R, 2 * W), F32), sds((2, D), F32)]
        + [sds((H, R, 2 * W), BF16)] * (Q - 1),
        scratch=[pltpu.VMEM((T, 2 * W), F32)],
        n_smem=2,
    )
    if Q == 2:
        up = (up.astype(F32) + shift_q(up, 1).astype(F32)).astype(BF16)
    else:
        ups = jnp.roll(jnp.stack([up] + [shift_q(up, j) for j in range(1, Q)]), y, axis=0)
        up = jnp.sum(ups.astype(F32), axis=0).astype(BF16)
    ups = [x.astype(F32) for x in gather_h(up)]
    up = (ups[0] + ups[2]) + (ups[1] + ups[3])
    kv_msgs = [shift_q(kv_msgs[j - 1], j) for j in range(1, Q)]

    dm_lat = up.astype(BF16)
    dm_lat_blocks = gather_f(dm_lat)

    def latent_ffn_back_body(d0, d1, d2, d3, hid_ref, wf_ref, wp_ref, all_ref, dh_ref, sum_ref, o0, o1, o2, o3):
        for i, d in enumerate((d0, d1, d2, d3)):
            all_ref[i * NT : (i + 1) * NT] = d[...]
        dh = (dot(all_ref[...], wp_ref[...], 1, 1) * gelu_back(hid_ref[...])).astype(BF16)
        dh_ref[...] = dh
        out = dot(dh, wf_ref[...], 1, 1)
        for i, o in enumerate((o0, o1, o2, o3)):
            o[...] = out[i * NT : (i + 1) * NT].astype(o.dtype)
        sum_ref[...] = jnp.sum(dh.astype(F32), axis=0, keepdims=True)

    dm_lat_all, dh_lat, dh_lat_sum, *lat_back = call(
        latent_ffn_back_body, "latent_ffn_backward", [*dm_lat_blocks, hidden_lat, wf, w_proj],
        [sds((4 * NT, D), BF16), sds((4 * NT, FS), BF16), sds((1, FS), F32), sds((NT, D), F32)]
        + [sds((NT, D), BF16)] * 3,
        n_smem=0,
    )
    lat_back = [lat_back[0]] + [flip(lat_back[i], i) for i in range(1, 4)]

    def latent_back_body(*refs):
        ids_ref, len_ref, b0, b1, b2, b3, up_ref, mid_ref, wo_ref, vec_ref, q_ref, ctx_ref, lse_ref = refs[:13]
        qkv_refs = refs[13 : 13 + Q]
        posb_ref, posc_ref, thr_ref, thc_ref, dq_ref, dkv_ref = refs[13 + Q : 19 + Q]
        msgs = refs[19 + Q : 18 + 2 * Q]
        normed_ref, nth_ref, wq_ref = refs[18 + 2 * Q : 21 + 2 * Q]
        dmid_ref, da_ref, sum_ref, bias_ref, o0, o1, o2, o3, n0, n1, n2, n3, tmp, acc = refs[21 + 2 * Q :]
        zz, yy, ff = ids_ref[0, 0], ids_ref[0, 1], ids_ref[0, 2]
        back = (b0[...] + b1[...].astype(F32)) + (b2[...].astype(F32) + b3[...].astype(F32))
        _, scaled, inverse = norm(mid_ref[...], vec_ref[1:2, :], vec_ref[3:4, :])
        d_mid = up_ref[...] + norm_back(back, scaled, inverse, vec_ref[1:2, :])
        dmid_ref[...] = d_mid
        da = d_mid.astype(BF16)
        da_ref[...] = da
        sum_ref[0:1] = jnp.sum(back * scaled, axis=0, keepdims=True)
        sum_ref[1:2] = jnp.sum(back, axis=0, keepdims=True)
        sum_ref[2:3] = jnp.sum(da.astype(F32), axis=0, keepdims=True)
        sum_ref[3:4] = jnp.sum(up_ref[...].astype(BF16).astype(F32), axis=0, keepdims=True)
        g = dot(da, wo_ref[pl.ds(pl.multiple_of(zz * W, 64), W), :], 1, 1).astype(BF16)
        q = q_ref[...]
        p_row = thr_ref[...] - 1
        start = start_of(p_row, len_ref)
        lse = lse_ref[...]
        g_t = g.astype(F32).T
        deltas = [
            jnp.sum(g_t[h * HDIM : (h + 1) * HDIM] * ctx_ref[h * HDIM : (h + 1) * HDIM], axis=0, keepdims=True)
            for h in range(NH)
        ]
        dq_t = [jnp.zeros((HDIM, NT), F32) for _ in range(NH)]
        for j in range(Q):
            for k in range(H):
                a = (zz ^ k) * Q + lax.rem(yy + j, Q)
                kp = posc_ref[pl.ds(pl.multiple_of(a * R, R), R), :]
                mask = (kp <= p_row) & (kp >= start)
                dks, dvs = [], []
                for h in range(NH):
                    c = slice(h * HDIM, (h + 1) * HDIM)
                    kh = qkv_refs[j][k][:, W + c.start : W + c.stop]
                    vh = qkv_refs[j][k][:, 2 * W + c.start : 2 * W + c.stop]
                    s = dot(kh, q[:, c], 1, 1) * SCALE
                    p = jnp.where(mask, jnp.exp(s - lse[h : h + 1]), 0.0)
                    dp = dot(vh, g[:, c], 1, 1)
                    ds = (p * (dp - deltas[h])).astype(BF16)
                    dq_t[h] = dq_t[h] + dot(kh, ds, 0, 0)
                    if j == 0:
                        dks.append(dot(ds, q[:, c]) * SCALE)
                        dvs.append(dot(p.astype(BF16), g[:, c]))
                if j == 0:
                    rows = slice(k * R, (k + 1) * R)
                    acc[rows, W : 2 * W] = jnp.concatenate(dks, axis=1)
                    acc[rows, 2 * W :] = jnp.concatenate(dvs, axis=1)
        dq_l = (jnp.concatenate(dq_t, axis=0).T * SCALE).astype(BF16)
        th_grad = jnp.zeros((NT, 3 * W), F32)
        bias = jnp.zeros((1, 3 * W), F32)
        for k in range(H):
            a = (zz ^ k) * Q + yy
            rows = slice(k * R, (k + 1) * R)
            kp = posc_ref[pl.ds(pl.multiple_of(a * R, R), R), :]
            src = jnp.where(kp == thr_ref[...] - 1, 1.0, 0.0).astype(BF16)
            tgt = jnp.where(kp == thr_ref[...], 1.0, 0.0)
            is_th = jnp.max(tgt, axis=1, keepdims=True) > 0
            kv = dkv_ref[k]
            for m in msgs:
                kv = kv + m[k].astype(F32)
            tok = jnp.concatenate([dq_ref[k].astype(F32), kv], axis=1)
            lat = jnp.concatenate([dot(src, dq_l), acc[rows, W:]], axis=1)
            both = (jnp.where(is_th, 0.0, tok) + lat).astype(BF16)
            hot = jnp.where(posb_ref[pl.ds(a, 1), :] == thc_ref[...], 1.0, 0.0).astype(BF16)
            th_grad = th_grad + dot(hot, tok.astype(BF16))
            tmp[rows] = both
        th_low = th_grad.astype(BF16)
        both = tmp[...]
        bias_ref[...] = jnp.sum(both.astype(F32), axis=0, keepdims=True) + jnp.sum(
            th_low.astype(F32), axis=0, keepdims=True
        )
        acc[...] = dot(normed_ref[...].reshape(NQ, D), both, 0, 0) + dot(nth_ref[...], th_low, 0, 0)
        for i, o in enumerate((o0, o1, o2, o3)):
            o[...] = acc[pl.ds(pl.multiple_of((ff ^ i) * S, 64), S), :].astype(o.dtype)
        for k, o in enumerate((n0, n1, n2, n3)):
            o[...] = dot(tmp[k * R : (k + 1) * R], wq_ref[...], 1, 1).astype(o.dtype)

    d_mid_lat, da_lat, sums3, d_bias, *more = call(
        latent_back_body, "latent_backward",
        [
            ids, lengths, *lat_back, up, mid_lat, wo, vec, q_lat, ctx_lat, lse_lat, *qkvs,
            pos_blk, pos_col, th_row, th_col, dq, dkv, *kv_msgs, normed_y, normed_th, wq,
        ],
        [
            sds((NT, D), F32), sds((NT, D), BF16), sds((4, D), F32), sds((1, 3 * W), F32),
            sds((S, 3 * W), F32), *[sds((S, 3 * W), BF16)] * 3, sds((R, D), F32), *[sds((R, D), BF16)] * 3,
        ],
        scratch=[pltpu.VMEM((NQ, 3 * W), BF16), pltpu.VMEM((D, 3 * W), F32)],
        n_smem=2,
    )
    gq, gn = more[:4], more[4:]
    gq = [gq[0]] + [flip(gq[i], i) for i in range(1, 4)]
    gn = [gn[0]] + [flip_h(gn[k], k) for k in range(1, H)]

    gq = ((gq[0] + gq[1].astype(F32)) + (gq[2].astype(F32) + gq[3].astype(F32))).astype(BF16)
    if Q == 2:
        gq = (gq.astype(F32) + shift_q(gq, 1).astype(F32)).astype(BF16)
    else:
        every = jnp.roll(jnp.stack([gq] + [shift_q(gq, j) for j in range(1, Q)]), y, axis=0)
        gq = jnp.sum(every.astype(F32), axis=0).astype(BF16)
    gq_blocks = gather_h(gq)

    def final_body(
        ids_ref, n0, n1, n2, n3, x_ref, dmid_ref, ownp_ref, thr_ref, dlat_ref, vec_ref, bias_ref, s1_ref, s2_ref, s3_ref,
        grad_ref, sum_ref,
    ):
        zz, bb = ids_ref[0, 0], ids_ref[0, 3]
        gn_now = (n0[...] + n1[...].astype(F32)) + (n2[...].astype(F32) + n3[...].astype(F32))
        _, scaled, inverse = norm(x_ref[...].astype(F32), vec_ref[0:1, :], vec_ref[2:3, :])
        tgt = jnp.where(ownp_ref[...] == thr_ref[...], 1.0, 0.0)
        is_th = jnp.max(tgt, axis=1, keepdims=True) > 0
        src = jnp.where(ownp_ref[...] == thr_ref[...] - 1, 1.0, 0.0).astype(BF16)
        grad = jnp.where(is_th, 0.0, dmid_ref[...]) + norm_back(gn_now, scaled, inverse, vec_ref[0:1, :])
        grad_ref[...] = grad + spread(src, dlat_ref[...], 1)
        once = jnp.where(bb == 0, 1.0, 0.0)
        sum_ref[0:1] = jnp.sum(gn_now * scaled, axis=0, keepdims=True) + s1_ref[0:1]
        sum_ref[2:3] = jnp.sum(gn_now, axis=0, keepdims=True) + s1_ref[1:2]
        sum_ref[1:2] = s2_ref[0:1] + once * s3_ref[0:1]
        sum_ref[3:4] = s2_ref[1:2] + once * s3_ref[1:2]
        sum_ref[6:7] = s2_ref[2:3] + once * s3_ref[2:3]
        sum_ref[7:8] = s2_ref[3:4] + once * s3_ref[3:4]
        for c in range(H):
            mine = jnp.where(zz == c, 1.0, 0.0)
            sum_ref[4:5, c * W : (c + 1) * W] = bias_ref[:, 0:W] * mine
            sum_ref[5:6, c * W : (c + 1) * W] = bias_ref[:, 2 * W :] * mine

    grad_in, sums = call(
        final_body, "input_grad",
        [ids, *gn, own, d_mid, own_pos, th_row, d_mid_lat, vec, d_bias, sums1, sums2, sums3],
        [sds((R, D), F32), sds((8, D), F32)],
    )
    once = jnp.where(b == 0, 1.0, 0.0)
    d_fc_bias = jnp.where(
        jnp.arange(4)[:, None] == f, dh_sum + once * dh_lat_sum, jnp.zeros((4, FS), F32)
    )
    sums = jnp.concatenate([sums, d_fc_bias], axis=0)
    sums = sums + flip(sums, 1)
    sums = sums + flip(sums, 2)
    if Q == 2:
        sums = sums + shift_q(sums, 1)
    else:
        sums = jnp.sum(jnp.roll(jnp.stack([sums] + [shift_q(sums, j) for j in range(1, Q)]), y, axis=0), axis=0)
    sg = gather_h(sums)
    sums = (sg[0] + sg[2]) + (sg[1] + sg[3])
    mine_small = lax.dynamic_slice_in_dim(sums[:8], f * S, S, axis=1)

    def result_body(o0, o1, o2, o3, mid_ref, vec_ref, out_ref):
        out = (o0[...] + o1[...].astype(F32)) + (o2[...].astype(F32) + o3[...].astype(F32))
        out_ref[...] = (mid_ref[...] + (out + vec_ref[7:8, :])).astype(BF16)

    [result] = call(result_body, "result", [*res, mid, vec], [sds((R, D), BF16)], n_smem=0)

    CR = FS // n_blk
    g_out = (g_out[0] + g_out[1].astype(F32)) + (g_out[2].astype(F32) + g_out[3].astype(F32))
    stack = jnp.concatenate(
        [g_proj, g_fct, g_out.astype(BF16).T], axis=1
    ).reshape(H, Q, CR, 2 * D + S)
    mine = take(stack, y, 1)
    if Q > 1:
        mine = mine.astype(F32)
        for j in range(1, Q):
            mine = mine + shift_q(take(stack, (y - j) % Q, 1), j).astype(F32)
        mine = mine.astype(BF16)
    got = [take(mine, z).astype(F32)] + [flip_h(take(mine, z ^ k), k).astype(F32) for k in range(1, H)]
    mine = ((got[0] + got[2]) + (got[1] + got[3])).astype(BF16)
    fc = mine[:, D : 2 * D].reshape(CR, 4, S)
    fc = [take(fc, f, 1)] + [flip(take(fc, f ^ i, 1), i) for i in range(1, 4)]
    piece = jnp.concatenate([mine[:, :D], *fc, mine[:, 2 * D :]], axis=1)
    rel = [piece] + [flip_h(piece, k) for k in range(1, H)]
    zs = [rel[0]] * H
    for i in range(H):
        zs[i] = rel[0]
        for k in range(1, H):
            zs[i] = jnp.where((z ^ k) == i, rel[k], zs[i])
    col = jnp.stack(zs)
    if Q > 1:
        col = jnp.roll(jnp.stack([col] + [shift_q(col, j) for j in range(1, Q)]), y, axis=0)
        every = jnp.transpose(col, (1, 0, 2, 3)).reshape(FS, 2 * D + S)
    w_proj_g = every[:, :D].astype(F32) + dot(active_lat, dm_lat_all, 0, 0)
    w_out_g = every[:, D + 4 * S :].astype(F32).T
    dh_lat_blocks = gather_f(dh_lat)
    second_cols = lax.dynamic_slice_in_dim(second_lat_all, f * S, S, axis=1).reshape(4, NT, S)
    fc_parts = []
    for i in range(4):
        rows = jnp.concatenate([second_cols[i ^ m] for m in range(4)], axis=0)
        fc_parts.append(
            every[:, D + i * S : D + (i + 1) * S].astype(F32).T + dot(rows, dh_lat_blocks[i], 0, 0)
        )
    near, far = (f % 2) == 1, (f // 2) == 1
    fc_parts = [jnp.where(near, fc_parts[i ^ 1], fc_parts[i]) for i in range(4)]
    fc_parts = [jnp.where(far, fc_parts[i ^ 2], fc_parts[i]) for i in range(4)]
    w_fc_g = jnp.concatenate(fc_parts, axis=1)
    lat_cols = [lax.dynamic_slice_in_dim(ctx_lat_all, (f ^ i) * S, S, axis=1) for i in range(4)]
    lat_cols = jnp.concatenate([lat_cols[0]] + [flip(lat_cols[i], i) for i in range(1, 4)], axis=0)
    da_lat_all = jnp.concatenate(gather_f(da_lat), axis=0)
    w_out_g = w_out_g + dot(lat_cols, da_lat_all, 0, 0)

    def qkv_grad_body(ids_ref, g0, g1, g2, g3, out_ref, tmp):
        zz = ids_ref[0, 0]
        for k, g in enumerate((g0, g1, g2, g3)):
            tmp[zz ^ k] = g[...]
        for c in range(H):
            for i in range(3):
                out_ref[:, i * D + c * W : i * D + (c + 1) * W] = tmp[c][:, i * W : (i + 1) * W].astype(F32)

    [w_qkv_g] = call(
        qkv_grad_body, "qkv_grad", [ids, *gq_blocks], [sds((S, 3 * D), F32)],
        scratch=[pltpu.VMEM((H, S, 3 * W), BF16)],
    )
    return (
        result[None],
        grad_in[None],
        mine_small[0:2],
        mine_small[2:4],
        w_qkv_g,
        mine_small[4:6],
        w_out_g,
        mine_small[6],
        w_fc_g,
        take(sums[8:], f),
        w_proj_g,
        mine_small[7],
    )


def solution(mesh):
    a, r, v = P("fsdp", "blk", None), P("fsdp", None), P("fsdp")
    c = P(None, "fsdp")
    return jax.shard_map(
        local,
        mesh=mesh,
        in_specs=(a, r, r, r, c, c, r, c, r, v, r, v, r, v, a),
        out_specs=(a, a, c, c, r, c, r, v, r, v, r, v),
        check_vma=False,
    )
```

```python
import jax
import jax.numpy as jnp
from jax import lax
from jax.experimental import pallas as pl
from jax.experimental.pallas import tpu as pltpu
from jax.sharding import PartitionSpec as P

HDIM = 64
PARTS = 4
EPS = 1e-05
SCALE = HDIM ** (-0.5)
F32 = jnp.float32
BF16 = jnp.bfloat16
VMEM_BYTES = 60 * 1024 * 1024
INTERPRET = False


def dot(a, b, ca=1, cb=0):
    return lax.dot_general(a, b, (((ca,), (cb,)), ((), ())), preferred_element_type=F32)


def spread(hot, x, axis):
    total = None
    for _ in range(3):
        low = x.astype(BF16)
        x = x - low.astype(F32)
        part = dot(hot, low, axis, 0)
        total = part if total is None else total + part
    return total


def norm(x, gain, shift):
    center = x - jnp.mean(x, axis=-1, keepdims=True)
    inverse = lax.rsqrt(jnp.mean(center * center, axis=-1, keepdims=True) + EPS)
    scaled = center * inverse
    return (scaled * gain + shift).astype(BF16), scaled, inverse


def norm_back(up, scaled, inverse, gain):
    w = up * gain
    return inverse * (
        w - jnp.mean(w, axis=-1, keepdims=True) - scaled * jnp.mean(w * scaled, axis=-1, keepdims=True)
    )


C0 = 0.7978845608028654
C1 = 0.044715


def gelu(v):
    return 0.5 * v * (1.0 + jnp.tanh(C0 * (v + C1 * v * v * v)))


def gelu_back(v):
    t = jnp.tanh(C0 * (v + C1 * v * v * v))
    return 0.5 * (1.0 + t) + 0.5 * v * (1.0 - t * t) * C0 * (1.0 + 3 * C1 * v * v)


def start_of(p, len_ref):
    start = jnp.zeros_like(p)
    end = jnp.int32(0)
    for i in range(len_ref.shape[1] - 1):
        end = end + len_ref[0, i]
        start = jnp.where(p >= end, end, start)
    return start


def sds(shape, dtype):
    return jax.ShapeDtypeStruct(shape, dtype)


TIMES = {
    "pack": 2.0, "pack2": 2.5, "project": 4.1, "project_more": 3.5, "latent_attention": 4.6, "place": 3.8,
    "latent_out": 2.9, "latent_ffn": 3.8, "token_attention": 8.0, "token_out": 3.1, "ffn": 7.3, "ffn_grads": 5.6,
    "attention_gradient": 3.4, "out_grad": 3.2, "token_backward": 9.8, "out_sum": 2.9, "latent_ffn_backward": 3.9,
    "join": 2.0, "latent_backward": 9.6, "tail_sum": 2.3, "input_grad": 2.8, "proj_out_grad": 4.7, "fc_grad": 4.6,
    "qkv_grad": 3.1,
}
FLOPS_PER_US = 330_000_000


def call(body, name, args, outs, scratch=(), n_smem=1):
    vm = pl.BlockSpec(memory_space=pltpu.VMEM)
    sm = pl.BlockSpec(memory_space=pltpu.SMEM)
    return pl.pallas_call(
        body,
        name=name,
        out_shape=list(outs),
        in_specs=[sm] * n_smem + [vm] * (len(args) - n_smem),
        out_specs=[vm] * len(outs),
        scratch_shapes=list(scratch),
        cost_estimate=pl.CostEstimate(
            flops=int(TIMES.get(name, 2.0) * FLOPS_PER_US), bytes_accessed=0, transcendentals=0
        ),
        compiler_params=pltpu.CompilerParams(vmem_limit_bytes=VMEM_BYTES),
        interpret=INTERPRET,
    )(*args)


def local(
    tokens, slot_pos, lengths, thoughts, ln_gain, ln_shift, w_qkv, qv_bias, w_out, out_bias,
    w_fc, fc_bias, w_proj, proj_bias, cotangent,
):
    n_blk, n_f = lax.axis_size("blk"), lax.axis_size("fsdp")
    H = PARTS
    Q = n_blk // H
    b, f = lax.axis_index("blk"), lax.axis_index("fsdp")
    z, y = b // Q, b % Q
    R, D = tokens.shape[1], tokens.shape[2]
    T = R * n_blk
    W = D // H
    NH = W // HDIM
    S = D // n_f
    FS = w_proj.shape[0]
    NT = thoughts.shape[1]
    NQ = H * R
    KB = min(T, 256)

    def take(x, i, axis=0):
        return lax.dynamic_index_in_dim(x, i, axis, keepdims=False)

    def flip_h(x, k):
        return lax.ppermute(x, "blk", [((((c // Q) ^ k) * Q) + c % Q, c) for c in range(n_blk)])

    def shift_q(x, j):
        return lax.ppermute(x, "blk", [((c // Q) * Q + (c % Q + j) % Q, c) for c in range(n_blk)])

    def flip(x, bit):
        return lax.ppermute(x, "fsdp", [(c, c ^ bit) for c in range(n_f)])

    def gather_f(x):
        far = flip(x, 2)
        return [x, flip(x, 1), far, flip(far, 1)]

    def gather_h(x):
        return [x] + [flip_h(x, k) for k in range(1, H)]

    def barrier(*xs):
        return lax.optimization_barrier(xs)

    ids = jnp.stack([z, y, f, b]).astype(jnp.int32)[None]

    own = tokens[0]
    cot = cotangent[0]
    small = jnp.concatenate(
        [ln_gain, ln_shift, qv_bias, out_bias[None], proj_bias[None]], axis=0
    )

    def pack_body(ids_ref, w_ref, small_ref, out_ref):
        zz = ids_ref[0, 0]
        for c in range(H):

            @pl.when(zz == c)
            def _():
                for i in range(3):
                    out_ref[0:S, i * W : (i + 1) * W] = w_ref[:, i * D + c * W : i * D + (c + 1) * W]

        rows = jnp.concatenate([small_ref[...].astype(F32), jnp.zeros((8, S), F32)], axis=0)
        rows = jnp.concatenate([rows, jnp.zeros((16, 3 * W - S), F32)], axis=1)
        out_ref[S : S + 16, :] = rows.astype(BF16)

    def pack2_body(ids_ref, fc_ref, wo_ref, far_ref, near_ref):
        ff = ids_ref[0, 2]

        def block(i):
            return fc_ref[:, pl.ds(pl.multiple_of((ff ^ i) * FS, 128), FS)]

        for ref in (far_ref, near_ref):
            ref[0:S] = wo_ref[...]
        far_ref[S : 2 * S] = block(3)
        far_ref[2 * S :] = block(2)
        near_ref[S:] = block(1)

    [part] = call(pack_body, "pack", [ids, w_qkv, small], [sds((S + 16, 3 * W), BF16)])
    own1, own3 = flip_h(own, 1), flip_h(own, 3)
    own_y = [shift_q(own, j) for j in range(1, Q)]
    part, own1, own3 = barrier(part, own1, own3, own_y[0])[:3]
    own2 = flip_h(own1, 3)
    parts = gather_f(part)
    blocks = [[own, own1, own2, own3]]
    for j in range(1, Q):
        blocks.append([own_y[j - 1], shift_q(own1, j), shift_q(own2, j), shift_q(own3, j)])
    far0, near0 = call(
        pack2_body, "pack2", [ids, w_fc, w_out], [sds((3 * S, D), BF16), sds((2 * S, D), BF16)]
    )
    far0 = barrier(far0, parts[2], own2, blocks[1][1], blocks[1][3])[0]
    far_got = flip(far0, 2)

    pos = slot_pos
    pos_col = slot_pos.reshape(T, 1)
    pos_blk = slot_pos.reshape(n_blk, R)
    th_row = thoughts
    th_col = thoughts.reshape(NT, 1)

    def proj_body(ids_ref, p0, p1, p2, p3, x0, x1, x2, x3, qkv_ref, wq_ref, vec_ref, normed_ref, scaled_ref):
        zz, ff = ids_ref[0, 0], ids_ref[0, 2]
        smalls = []
        for i, p in enumerate((p0, p1, p2, p3)):
            wq_ref[pl.ds(pl.multiple_of((ff ^ i) * S, 64), S), :] = p[0:S, :]
            smalls.append(p[S : S + 16, 0:S].astype(F32)[0:8])
        for a in range(4):
            v = smalls[0]
            for i in range(1, 4):
                v = jnp.where((ff ^ i) == a, smalls[i], v)
            vec_ref[:, a * S : (a + 1) * S] = v
        bias = bias_of(vec_ref, zz)
        for k, x in enumerate((x0, x1, x2, x3)):
            n, scaled, _ = norm(x[...].astype(F32), vec_ref[0:1, :], vec_ref[2:3, :])
            normed_ref[k] = n
            scaled_ref[k] = scaled.astype(BF16)
            qkv_ref[k] = (dot(n, wq_ref[...]) + bias).astype(BF16)

    def bias_of(vec_ref, zz):
        qb = vec_ref[4:5, 0:W]
        vb = vec_ref[5:6, 0:W]
        for c in range(1, H):
            qb = jnp.where(zz == c, vec_ref[4:5, c * W : (c + 1) * W], qb)
            vb = jnp.where(zz == c, vec_ref[5:6, c * W : (c + 1) * W], vb)
        return jnp.concatenate([qb, jnp.zeros_like(qb), vb], axis=1)

    def proj_more(ids_ref, wq_ref, vec_ref, x0, x1, x2, x3, qkv_ref):
        bias = bias_of(vec_ref, ids_ref[0, 0])
        for k, x in enumerate((x0, x1, x2, x3)):
            n, _, _ = norm(x[...].astype(F32), vec_ref[0:1, :], vec_ref[2:3, :])
            qkv_ref[k] = (dot(n, wq_ref[...]) + bias).astype(BF16)

    qkv_y, wq, vec, normed_y, scaled_y = call(
        proj_body, "project", [ids, *parts, *blocks[0]],
        [sds((H, R, 3 * W), BF16), sds((D, 3 * W), BF16), sds((8, D), F32), sds((H, R, D), BF16), sds((H, R, D), BF16)],
    )
    qkvs = [qkv_y]
    for j in range(1, Q):
        qkvs += call(
            proj_more, "project_more", [ids, wq, vec, *blocks[j]], [sds((H, R, 3 * W), BF16)]
        )

    def attend(q, read_k, read_v, key_pos, q_pos, q_start, s_ref):
        n = q.shape[0]
        ctx, lse = [], []
        for h in range(NH):
            lanes = slice(h * HDIM, (h + 1) * HDIM)
            qh = q[:, lanes]

            def score(i, m):
                at = pl.multiple_of(i * KB, KB)
                s = dot(read_k(at, lanes), qh, 1, 1) * SCALE
                kp = key_pos(at)
                s = jnp.where((kp <= q_pos) & (kp >= q_start), s, -1e30)
                s_ref[pl.ds(at, KB), 0:n] = s
                return jnp.maximum(m, jnp.max(s, axis=0, keepdims=True))

            m = lax.fori_loop(0, T // KB, score, jnp.full((1, n), -1e30, F32), unroll=T // KB <= 4)

            def add(i, carry):
                total, acc = carry
                at = pl.multiple_of(i * KB, KB)
                e = jnp.exp(s_ref[pl.ds(at, KB), 0:n] - m)
                total = total + jnp.sum(e, axis=0, keepdims=True)
                return total, acc + dot(read_v(at, lanes), e.astype(BF16), 0, 0)

            total, acc = lax.fori_loop(
                0, T // KB, add, (jnp.zeros((1, n), F32), jnp.zeros((HDIM, n), F32)), unroll=T // KB <= 4
            )
            ctx.append(acc / total)
            lse.append(m + jnp.log(total))
        return jnp.concatenate(ctx, axis=0), jnp.concatenate(lse, axis=0)

    def latent_body(*refs):
        ids_ref, len_ref, pos_ref, posb_ref, posc_ref, thr_ref, thc_ref = refs[:7]
        qkv_refs = refs[7 : 7 + Q]
        x_refs = refs[7 + Q : 7 + Q + n_blk]
        low_ref, ctx_ref, lse_ref, q_ref, x_ref, abs_ref, s_ref = refs[7 + Q + n_blk :]
        zz, yy = ids_ref[0, 0], ids_ref[0, 1]
        src = thc_ref[...] - 1
        x_lat = jnp.zeros((NT, D), F32)
        for j in range(Q):
            for k in range(H):
                a = (zz ^ k) * Q + lax.rem(yy + j, Q)
                abs_ref[pl.ds(pl.multiple_of(a * R, R), R), :] = qkv_refs[j][k]
                hot = jnp.where(posb_ref[pl.ds(a, 1), :] == src, 1.0, 0.0).astype(BF16)
                x_lat = x_lat + dot(hot, x_refs[j * H + k][...])
        x_ref[...] = x_lat
        hot = jnp.where(pos_ref[...] == src, 1.0, 0.0).astype(BF16)
        q = dot(hot, abs_ref[:, 0:W]).astype(BF16)
        q_ref[...] = q
        p = thr_ref[...] - 1
        ctx, lse = attend(
            q,
            lambda at, c: abs_ref[pl.ds(at, KB), W + c.start : W + c.stop],
            lambda at, c: abs_ref[pl.ds(at, KB), 2 * W + c.start : 2 * W + c.stop],
            lambda at: posc_ref[pl.ds(at, KB), :],
            p,
            start_of(p, len_ref),
            s_ref,
        )
        ctx_ref[...] = ctx
        lse_ref[...] = lse
        low_ref[...] = ctx.T.astype(BF16)

    flat = [x for group in blocks for x in group]
    ctx_lat_low, ctx_lat, lse_lat, q_lat, x_lat, qkv_abs = call(
        latent_body, "latent_attention",
        [ids, lengths, pos, pos_blk, pos_col, th_row, th_col, *qkvs, *flat],
        [
            sds((NT, W), BF16), sds((W, NT), F32), sds((NH, NT), F32), sds((NT, W), BF16),
            sds((NT, D), F32), sds((T, 3 * W), BF16),
        ],
        scratch=[pltpu.VMEM((T, 128), F32)],
        n_smem=2,
    )
    ctx_lat_blocks = gather_h(ctx_lat_low)

    far_got, near0 = barrier(far_got, near0, ctx_lat_low)[:2]
    near_got = flip(near0, 1)
    both_got = flip(far_got, 1)

    def place_body(ids_ref, far0_ref, far_ref, near_ref, both_ref, fc_ref, wo_ref, wf_ref):
        ff = ids_ref[0, 2]

        def at(i):
            return pl.ds(pl.multiple_of((ff ^ i) * S, 64), S)

        for i, ref in enumerate((far0_ref, near_ref, far_ref, both_ref)):
            wo_ref[at(i), :] = ref[0:S]
        wf_ref[at(0), :] = fc_ref[:, pl.ds(pl.multiple_of(ff * FS, 128), FS)]
        wf_ref[at(1), :] = near_ref[S:]
        wf_ref[at(2), :] = far_ref[2 * S :]
        wf_ref[at(3), :] = both_ref[S : 2 * S]

    wo, wf = call(
        place_body, "place", [ids, far0, far_got, near_got, both_got, w_fc], [sds((D, D), BF16), sds((D, FS), BF16)]
    )
    fb = fc_bias[None]

    def columns(x, i):
        v = x[:, 0:S]
        for c in range(1, 4):
            v = jnp.where(i == c, x[:, c * S : (c + 1) * S], v)
        return v

    def latent_out_body(ids_ref, c0, c1, c2, c3, x_ref, wo_ref, vec_ref, mid_ref, low_ref, l0, l1, l2, l3, all_ref, tmp):
        zz, ff = ids_ref[0, 0], ids_ref[0, 2]
        for k, c in enumerate((c0, c1, c2, c3)):
            tmp[zz ^ k] = c[...]
        for i in range(H):
            all_ref[:, i * W : (i + 1) * W] = tmp[i]
        mid = x_ref[...] + (dot(all_ref[...], wo_ref[...]) + vec_ref[6:7, :])
        mid_ref[...] = mid
        low_ref[...] = norm(mid, vec_ref[1:2, :], vec_ref[3:4, :])[0]
        both = all_ref[...].astype(F32)
        for i, o in enumerate((l0, l1, l2, l3)):
            o[...] = columns(both, ff ^ i).astype(BF16)

    mid_lat, second_lat, *lat_cols = call(
        latent_out_body, "latent_out", [ids, *ctx_lat_blocks, x_lat, wo, vec],
        [sds((NT, D), F32), sds((NT, D), BF16)] + [sds((NT, S), BF16)] * 4,
        scratch=[pltpu.VMEM((NT, D), BF16), pltpu.VMEM((H, NT, W), BF16)],
    )
    second_lat_blocks = gather_f(second_lat)

    def latent_ffn_body(s0, s1, s2, s3, wf_ref, wp_ref, fb_ref, hid_ref, act_ref, all_ref, o0, o1, o2, o3):
        for i, s in enumerate((s0, s1, s2, s3)):
            all_ref[i * NT : (i + 1) * NT] = s[...]
        hidden = dot(all_ref[...], wf_ref[...]) + fb_ref[...].astype(F32)
        hid_ref[...] = hidden
        act_ref[...] = gelu(hidden).astype(BF16)
        out = dot(act_ref[...], wp_ref[...])
        for i, o in enumerate((o0, o1, o2, o3)):
            o[...] = out[i * NT : (i + 1) * NT].astype(o.dtype)

    hidden_lat, active_lat, second_lat_all, *outs = call(
        latent_ffn_body, "latent_ffn", [*second_lat_blocks, wf, w_proj, fb],
        [sds((4 * NT, FS), F32), sds((4 * NT, FS), BF16), sds((4 * NT, D), BF16), sds((NT, D), F32)]
        + [sds((NT, D), BF16)] * 3,
        n_smem=0,
    )
    outs = [outs[0]] + [flip(outs[i], i) for i in range(1, 4)]
    dm_blocks = gather_f(barrier(cot, outs[2], outs[3])[0])

    def token_body(
        ids_ref, len_ref, o0, o1, o2, o3, mid_ref, vec_ref, wq_ref, abs_ref, qy_ref, posb_ref, posc_ref, thr_ref,
        lat_ref, nth_ref, kv_ref, q_ref, ctx_ref, lse_ref, c0, c1, c2, c3, s_ref,
    ):
        zz, yy = ids_ref[0, 0], ids_ref[0, 1]
        lat = mid_ref[...] + (
            (o0[...] + o1[...].astype(F32) + (o2[...].astype(F32) + o3[...].astype(F32))) + vec_ref[7:8, :]
        )
        lat_ref[...] = lat
        nth = norm(lat, vec_ref[0:1, :], vec_ref[2:3, :])[0]
        nth_ref[...] = nth
        qkv_th = (dot(nth, wq_ref[...]) + bias_of(vec_ref, zz)).astype(BF16)

        def fill(i, _):
            at = pl.multiple_of(i * KB, KB)
            hot = posc_ref[pl.ds(at, KB), :] == thr_ref[...]
            is_th = jnp.max(jnp.where(hot, 1.0, 0.0), axis=1, keepdims=True) > 0
            new = dot(jnp.where(hot, 1.0, 0.0).astype(BF16), qkv_th[:, W:])
            kv_ref[pl.ds(at, KB), :] = jnp.where(is_th, new, abs_ref[pl.ds(at, KB), W:].astype(F32)).astype(BF16)
            return 0

        lax.fori_loop(0, T // KB, fill, 0, unroll=T // KB <= 4)
        rows = []
        for k in range(H):
            a = (zz ^ k) * Q + yy
            hot = posc_ref[pl.ds(pl.multiple_of(a * R, R), R), :] == thr_ref[...]
            is_th = jnp.max(jnp.where(hot, 1.0, 0.0), axis=1, keepdims=True) > 0
            new = dot(jnp.where(hot, 1.0, 0.0).astype(BF16), qkv_th[:, 0:W])
            q_ref[k] = jnp.where(is_th, new, qy_ref[k][:, 0:W].astype(F32)).astype(BF16)
            rows.append(posb_ref[pl.ds(a, 1), :])
        p = jnp.concatenate(rows, axis=1)
        ctx, lse = attend(
            q_ref[...].reshape(NQ, W),
            lambda at, c: kv_ref[pl.ds(at, KB), c],
            lambda at, c: kv_ref[pl.ds(at, KB), W + c.start : W + c.stop],
            lambda at: posc_ref[pl.ds(at, KB), :],
            p,
            start_of(p, len_ref),
            s_ref,
        )
        ctx_ref[...] = ctx
        lse_ref[...] = lse
        low = ctx.T.astype(BF16)
        for k, c in enumerate((c0, c1, c2, c3)):
            c[...] = low[k * R : (k + 1) * R]

    lat_out, normed_th, kv_tok, q_tok, ctx_t, lse, *ctx_blocks = call(
        token_body, "token_attention",
        [ids, lengths, *outs, mid_lat, vec, wq, qkv_abs, qkv_y, pos_blk, pos_col, th_row],
        [
            sds((NT, D), F32), sds((NT, D), BF16), sds((T, 2 * W), BF16), sds((H, R, W), BF16),
            sds((W, NQ), F32), sds((NH, NQ), F32),
        ]
        + [sds((R, W), BF16)] * 4,
        scratch=[pltpu.VMEM((T, NQ), F32)],
        n_smem=2,
    )
    ctx_blocks = [ctx_blocks[0]] + [flip_h(ctx_blocks[k], k) for k in range(1, H)]
    own_pos = lax.dynamic_slice_in_dim(pos_col, b * R, R, axis=0)

    def token_out_body(
        ids_ref, c0, c1, c2, c3, x_ref, posc_ref, thr_ref, lat_ref, wo_ref, vec_ref, mid_ref, low_ref, all_ref, tmp
    ):
        zz = ids_ref[0, 0]
        for k, c in enumerate((c0, c1, c2, c3)):
            tmp[zz ^ k] = c[...]
        for i in range(H):
            all_ref[:, i * W : (i + 1) * W] = tmp[i]
        hot = jnp.where(posc_ref[...] == thr_ref[...], 1.0, 0.0)
        is_th = jnp.max(hot, axis=1, keepdims=True) > 0
        x = jnp.where(is_th, spread(hot.astype(BF16), lat_ref[...], 1), x_ref[...].astype(F32))
        mid = x + (dot(all_ref[...], wo_ref[...]) + vec_ref[6:7, :])
        mid_ref[...] = mid
        low_ref[...] = norm(mid, vec_ref[1:2, :], vec_ref[3:4, :])[0]

    mid, second, ctx_own = call(
        token_out_body, "token_out", [ids, *ctx_blocks, own, own_pos, th_row, lat_out, wo, vec],
        [sds((R, D), F32), sds((R, D), BF16), sds((R, D), BF16)],
        scratch=[pltpu.VMEM((H, R, W), BF16)],
    )
    second_blocks = gather_f(second)

    def ffn_body(s0, s1, s2, s3, d0, d1, d2, d3, wf_ref, wp_ref, fb_ref, act_ref, dh_ref, all_ref, dm_ref, sum_ref, o0, o1, o2, o3):
        for i, (s, d, o) in enumerate(zip((s0, s1, s2, s3), (d0, d1, d2, d3), (o0, o1, o2, o3))):
            rows = slice(i * R, (i + 1) * R)
            all_ref[rows] = s[...]
            dm_ref[rows] = d[...]
            hidden = dot(s[...], wf_ref[...]) + fb_ref[...].astype(F32)
            t = jnp.tanh(C0 * (hidden + C1 * hidden * hidden * hidden))
            act_ref[rows] = (0.5 * hidden * (1.0 + t)).astype(BF16)
            back = 0.5 * (1.0 + t) + 0.5 * hidden * (1.0 - t * t) * C0 * (1.0 + 3 * C1 * hidden * hidden)
            dh = (dot(d[...], wp_ref[...], 1, 1) * back).astype(BF16)
            dh_ref[rows] = dh
            o[...] = dot(dh, wf_ref[...], 1, 1).astype(o.dtype)
        sum_ref[...] = jnp.sum(dh_ref[...].astype(F32), axis=0, keepdims=True)

    active, dh, second_all, dm_all, dh_sum, *back = call(
        ffn_body, "ffn", [*second_blocks, *dm_blocks, wf, w_proj, fb],
        [sds((4 * R, FS), BF16), sds((4 * R, FS), BF16), sds((4 * R, D), BF16), sds((4 * R, D), BF16), sds((1, FS), F32), sds((R, D), F32)]
        + [sds((R, D), BF16)] * 3,
        n_smem=0,
    )
    back = [back[0]] + [flip(back[i], i) for i in range(1, 4)]

    def grads_body(act_ref, dh_ref, all_ref, dm_ref, wp_ref, g_ref, o0, o1, o2, o3):
        out = dot(act_ref[...], wp_ref[...])
        for i, o in enumerate((o0, o1, o2, o3)):
            o[...] = out[i * R : (i + 1) * R].astype(o.dtype)
        g_ref[:, 0:D] = dot(act_ref[...], dm_ref[...], 0, 0).astype(BF16)
        g_ref[:, D:] = dot(dh_ref[...], all_ref[...], 0, 0).astype(BF16)

    g_ffn, *res = call(
        grads_body, "ffn_grads", [active, dh, second_all, dm_all, w_proj],
        [sds((FS, 2 * D), BF16), sds((R, D), F32)] + [sds((R, D), BF16)] * 3,
        n_smem=0,
    )
    g_ffn_later = barrier(g_ffn, back[2], back[3])[0]
    g_sum = lax.psum_scatter(g_ffn_later, "blk", scatter_dimension=0, tiled=True)
    back[0] = barrier(back[0], g_ffn)[0]

    def attn_in_body(ids_ref, b0, b1, b2, b3, mid_ref, cot_ref, wo_ref, vec_ref, dmid_ref, da_ref, sum_ref, c0, c1, c2, c3):
        zz = ids_ref[0, 0]
        up = (b0[...] + b1[...].astype(F32)) + (b2[...].astype(F32) + b3[...].astype(F32))
        _, scaled, inverse = norm(mid_ref[...], vec_ref[1:2, :], vec_ref[3:4, :])
        cot_now = cot_ref[...].astype(F32)
        d_mid = cot_now + norm_back(up, scaled, inverse, vec_ref[1:2, :])
        dmid_ref[...] = d_mid
        da = d_mid.astype(BF16)
        da_ref[...] = da
        for k, c in enumerate((c0, c1, c2, c3)):
            w = wo_ref[pl.ds(pl.multiple_of((zz ^ k) * W, 64), W), :]
            c[...] = dot(da, w, 1, 1).astype(BF16)
        sum_ref[0:1] = jnp.sum(up * scaled, axis=0, keepdims=True)
        sum_ref[1:2] = jnp.sum(up, axis=0, keepdims=True)
        sum_ref[2:3] = jnp.sum(da.astype(F32), axis=0, keepdims=True)
        sum_ref[3:4] = jnp.sum(cot_now, axis=0, keepdims=True)

    d_mid, da, sums2, *grad_blocks = call(
        attn_in_body, "attention_gradient", [ids, *back, mid, cot, wo, vec],
        [sds((R, D), F32), sds((R, D), BF16), sds((4, D), F32)] + [sds((R, W), BF16)] * 4,
    )
    grad_blocks = [grad_blocks[0]] + [flip_h(grad_blocks[k], k) for k in range(1, H)]

    def out_grad_body(ids_ref, ctx_ref, da_ref, r1, r2, r3, l1, l2, l3, o0, o1, o2, o3, tmp):
        ff = ids_ref[0, 2]
        tmp[...] = dot(ctx_ref[...], da_ref[...], 0, 0)
        own_rows = pl.ds(pl.multiple_of(ff * S, 64), S)
        o0[...] = tmp[own_rows, :]
        for i, (r, l, o) in enumerate(((r1, l1, o1), (r2, l2, o2), (r3, l3, o3)), 1):
            o[0:R] = r[...]
            o[R : R + S] = tmp[pl.ds(pl.multiple_of((ff ^ i) * S, 64), S), :].astype(BF16)
            for c in range(4):
                o[R + S :, c * S : (c + 1) * S] = l[c * NT // 4 : (c + 1) * NT // 4, :]

    g_out, *mix = call(
        out_grad_body, "out_grad", [ids, ctx_own, da, *res[1:], *lat_cols[1:]],
        [sds((S, D), F32)] + [sds((R + S + NT // 4, D), BF16)] * 3,
        scratch=[pltpu.VMEM((D, D), F32)],
    )
    grad_blocks[0] = barrier(grad_blocks[0], g_out)[0]
    mix = list(barrier(*mix, *grad_blocks[1:])[:3])
    mix = [flip(mix[i - 1], i) for i in range(1, 4)]

    def attend_back(q, g, read_k, read_v, key_pos, q_pos, q_start, lse, ctx, n_keys, put):
        n = q.shape[0]
        g_t = g.astype(F32).T
        dqs = []
        deltas = [
            jnp.sum(g_t[h * HDIM : (h + 1) * HDIM] * ctx[h * HDIM : (h + 1) * HDIM], axis=0, keepdims=True)
            for h in range(NH)
        ]

        def step(i, dq):
            at = pl.multiple_of(i * KB, KB)
            kp = key_pos(at)
            mask = (kp <= q_pos) & (kp >= q_start)
            dks, dvs, new = [], [], []
            for h in range(NH):
                lanes = slice(h * HDIM, (h + 1) * HDIM)
                kh = read_k(at, lanes)
                s = dot(kh, q[:, lanes], 1, 1) * SCALE
                p = jnp.where(mask, jnp.exp(s - lse[h : h + 1]), 0.0)
                dp = dot(read_v(at, lanes), g[:, lanes], 1, 1)
                ds = (p * (dp - deltas[h])).astype(BF16)
                new.append(dq[h] + dot(kh, ds, 0, 0))
                dks.append(dot(ds, q[:, lanes]) * SCALE)
                dvs.append(dot(p.astype(BF16), g[:, lanes]))
            put(at, jnp.concatenate(dks, axis=1), jnp.concatenate(dvs, axis=1))
            return tuple(new)

        dq = lax.fori_loop(
            0, n_keys // KB, step, tuple(jnp.zeros((HDIM, n), F32) for _ in range(NH)), unroll=n_keys // KB <= 4
        )
        return jnp.concatenate(dq, axis=0).T * SCALE

    def token_back_body(
        ids_ref, len_ref, g0, g1, g2, g3, q_ref, kv_ref, ctx_ref, lse_ref, pos_ref, posb_ref, posc_ref, thr_ref, thc_ref,
        ownp_ref, wq_ref, lat_ref, vec_ref, dmid_ref,
        up_ref, dq_ref, dkv_ref, sum_ref, *rest,
    ):
        msgs, acc = rest[:-1], rest[-1]
        zz, yy = ids_ref[0, 0], ids_ref[0, 1]
        rows = [posb_ref[pl.ds((zz ^ k) * Q + yy, 1), :] for k in range(H)]
        p = jnp.concatenate(rows, axis=1)

        def put(at, dk, dv):
            acc[pl.ds(at, KB), 0:W] = dk
            acc[pl.ds(at, KB), W:] = dv

        dq = attend_back(
            q_ref[...].reshape(NQ, W),
            jnp.concatenate([g0[...], g1[...], g2[...], g3[...]], axis=0),
            lambda at, c: kv_ref[pl.ds(at, KB), c],
            lambda at, c: kv_ref[pl.ds(at, KB), W + c.start : W + c.stop],
            lambda at: posc_ref[pl.ds(at, KB), :],
            p,
            start_of(p, len_ref),
            lse_ref[...],
            ctx_ref[...],
            T,
            put,
        ).astype(BF16)
        hot_y = jnp.where(p == thc_ref[...], 1.0, 0.0).astype(BF16)
        hot = jnp.where(pos_ref[...] == thc_ref[...], 1.0, 0.0).astype(BF16)
        d_q = dot(hot_y, dq).astype(BF16)
        d_kv = dot(hot, acc[...].astype(BF16)).astype(BF16)
        gn = dot(d_q, wq_ref[:, 0:W], 1, 1) + dot(d_kv, wq_ref[:, W:], 1, 1)
        _, scaled, inverse = norm(lat_ref[...], vec_ref[0:1, :], vec_ref[2:3, :])
        sum_ref[0:1] = jnp.sum(gn * scaled, axis=0, keepdims=True)
        sum_ref[1:2] = jnp.sum(gn, axis=0, keepdims=True)
        hot_own = jnp.where(ownp_ref[...] == thr_ref[...], 1.0, 0.0).astype(BF16)
        up = norm_back(gn, scaled, inverse, vec_ref[0:1, :]) + spread(hot_own, dmid_ref[...], 0)
        up_ref[...] = up.astype(BF16)
        for k in range(H):
            dq_ref[k] = dq[k * R : (k + 1) * R]
            for j in range(Q):
                a = (zz ^ k) * Q + lax.rem(yy - j + Q, Q)
                block = acc[pl.ds(pl.multiple_of(a * R, R), R), :]
                if j == 0:
                    dkv_ref[k] = block
                else:
                    msgs[j - 1][k] = block.astype(BF16)

    up, dq, dkv, sums1, *kv_msgs = call(
        token_back_body, "token_backward",
        [
            ids, lengths, *grad_blocks, q_tok, kv_tok, ctx_t, lse, pos, pos_blk, pos_col, th_row, th_col,
            own_pos, wq, lat_out, vec, d_mid,
        ],
        [sds((NT, D), BF16), sds((H, R, W), BF16), sds((H, R, 2 * W), F32), sds((2, D), F32)]
        + [sds((H, R, 2 * W), BF16)] * (Q - 1),
        scratch=[pltpu.VMEM((T, 2 * W), F32)],
        n_smem=2,
    )
    if Q == 2:
        up = (up.astype(F32) + shift_q(up, 1).astype(F32)).astype(BF16)
    else:
        ups = jnp.roll(jnp.stack([up] + [shift_q(up, j) for j in range(1, Q)]), y, axis=0)
        up = jnp.sum(ups.astype(F32), axis=0).astype(BF16)
    ups = [x.astype(F32) for x in gather_h(up)]
    up = (ups[0] + ups[2]) + (ups[1] + ups[3])
    kv_msgs = list(barrier(*kv_msgs, up)[:-1])
    kv_msgs = [shift_q(kv_msgs[j - 1], j) for j in range(1, Q)]

    dm_lat = up.astype(BF16)
    dm_lat_blocks = gather_f(dm_lat)

    def latent_ffn_back_body(d0, d1, d2, d3, hid_ref, wf_ref, wp_ref, all_ref, dh_ref, sum_ref, o0, o1, o2, o3):
        for i, d in enumerate((d0, d1, d2, d3)):
            all_ref[i * NT : (i + 1) * NT] = d[...]
        dh = (dot(all_ref[...], wp_ref[...], 1, 1) * gelu_back(hid_ref[...])).astype(BF16)
        dh_ref[...] = dh
        out = dot(dh, wf_ref[...], 1, 1)
        for i, o in enumerate((o0, o1, o2, o3)):
            o[...] = out[i * NT : (i + 1) * NT].astype(o.dtype)
        sum_ref[...] = jnp.sum(dh.astype(F32), axis=0, keepdims=True)

    CR = FS // n_blk
    FR = CR // 3

    def out_sum_body(g0, m1, m2, m3, mid_ref, vec_ref, r0, out_ref, g_ref):
        rows = slice(R, R + S)
        g = (g0[...] + m1[rows].astype(F32)) + (m2[rows].astype(F32) + m3[rows].astype(F32))
        g_ref[...] = g.T.astype(BF16)
        out = (r0[...] + m1[0:R].astype(F32)) + (m2[0:R].astype(F32) + m3[0:R].astype(F32))
        out_ref[...] = (mid_ref[...] + (out + vec_ref[7:8, :])).astype(BF16)

    mix_now = barrier(*mix, ups[2])[:3]
    result, g_out = call(
        out_sum_body, "out_sum", [g_out, *mix_now, mid, vec, res[0]], [sds((R, D), BF16), sds((D, S), BF16)], n_smem=0
    )
    g_out = g_out.reshape(H, Q, CR, S)
    got = [shift_q(take(g_out, (y - j) % Q, 1), j).astype(F32) for j in range(1, Q)]
    g_out = take(g_out, y, 1).astype(F32)
    for t in got:
        g_out = g_out + t
    g_out = g_out.astype(BF16)
    dm_lat_blocks[0], g_out = barrier(dm_lat_blocks[0], g_out)
    g_out = [take(g_out, z)] + [flip_h(take(g_out, z ^ k), k) for k in range(1, H)]

    dm_lat_all, dh_lat, dh_lat_sum, *lat_back = call(
        latent_ffn_back_body, "latent_ffn_backward", [*dm_lat_blocks, hidden_lat, wf, w_proj],
        [sds((4 * NT, D), BF16), sds((4 * NT, FS), BF16), sds((1, FS), F32), sds((NT, D), F32)]
        + [sds((NT, D), BF16)] * 3,
        n_smem=0,
    )
    lat_back = [lat_back[0]] + [flip(lat_back[i], i) for i in range(1, 4)]
    def join_body(g_ref, c0, c1, c2, c3, out_ref):
        out_ref[:, 0:D] = g_ref[:, 0:D]
        c = (c0[...].astype(F32) + c2[...].astype(F32)) + (c1[...].astype(F32) + c3[...].astype(F32))
        out_ref[:, D:] = c.astype(BF16)

    def gather_blk(x):
        x1 = flip_h(x, 1)
        x32 = flip_h(jnp.concatenate([x, x1], axis=0), 3)
        got = [x, x1, x32]
        for j in range(1, Q):
            got += [shift_q(t, j) for t in (x, x1, x32)]
        return got

    g_sum = barrier(g_sum, lat_back[2], lat_back[3])[0]
    [piece_a] = call(join_body, "join", [g_sum, *g_out], [sds((CR, D + S), BF16)], n_smem=0)
    lat_back[0] = barrier(lat_back[0], piece_a)[0]
    every_a = gather_blk(piece_a) if CR % 16 == 0 else [lax.all_gather(piece_a, "blk", axis=0, tiled=True)]
    dh_lat_blocks = gather_f(barrier(dh_lat, lat_back[2], lat_back[3])[0])

    def latent_back_body(*refs):
        ids_ref, len_ref, b0, b1, b2, b3, up_ref, mid_ref, wo_ref, vec_ref, q_ref, ctx_ref, lse_ref = refs[:13]
        qkv_refs = refs[13 : 13 + Q]
        posb_ref, posc_ref, thr_ref, thc_ref, dq_ref, dkv_ref = refs[13 + Q : 19 + Q]
        msgs = refs[19 + Q : 18 + 2 * Q]
        normed_ref, nth_ref, wq_ref, scaled_ref, s1_ref, s2_ref, dh1_ref, dh2_ref, gsum_ref = refs[18 + 2 * Q : 27 + 2 * Q]
        dmid_ref, da_ref, o0, o1, o2, o3, n0, n1, n32, tmp, acc, small_ref = refs[27 + 2 * Q :]
        once = jnp.where(ids_ref[0, 3] == 0, 1.0, 0.0)
        zz, yy, ff = ids_ref[0, 0], ids_ref[0, 1], ids_ref[0, 2]
        back = (b0[...] + b1[...].astype(F32)) + (b2[...].astype(F32) + b3[...].astype(F32))
        _, scaled, inverse = norm(mid_ref[...], vec_ref[1:2, :], vec_ref[3:4, :])
        d_mid = up_ref[...] + norm_back(back, scaled, inverse, vec_ref[1:2, :])
        dmid_ref[...] = d_mid
        da = d_mid.astype(BF16)
        da_ref[...] = da
        col = lambda t: jnp.sum(t, axis=0, keepdims=True)
        small_ref[1:2] = s2_ref[0:1] + once * col(back * scaled)
        small_ref[3:4] = s2_ref[1:2] + once * col(back)
        small_ref[6:7] = s2_ref[2:3] + once * col(da.astype(F32))
        small_ref[7:8] = s2_ref[3:4] + once * col(up_ref[...].astype(BF16).astype(F32))
        g = dot(da, wo_ref[pl.ds(pl.multiple_of(zz * W, 64), W), :], 1, 1).astype(BF16)
        q = q_ref[...]
        p_row = thr_ref[...] - 1
        start = start_of(p_row, len_ref)
        lse = lse_ref[...]
        g_t = g.astype(F32).T
        deltas = [
            jnp.sum(g_t[h * HDIM : (h + 1) * HDIM] * ctx_ref[h * HDIM : (h + 1) * HDIM], axis=0, keepdims=True)
            for h in range(NH)
        ]
        dq_t = [jnp.zeros((HDIM, NT), F32) for _ in range(NH)]
        for j in range(Q):
            kps = [posc_ref[pl.ds(pl.multiple_of(((zz ^ k) * Q + lax.rem(yy + j, Q)) * R, R), R), :] for k in range(H)]
            kp = jnp.concatenate(kps, axis=0)
            mask = (kp <= p_row) & (kp >= start)
            dks, dvs = [], []
            for h in range(NH):
                c = slice(h * HDIM, (h + 1) * HDIM)
                kh = qkv_refs[j][:, :, W + c.start : W + c.stop].reshape(NQ, HDIM)
                vh = qkv_refs[j][:, :, 2 * W + c.start : 2 * W + c.stop].reshape(NQ, HDIM)
                s = dot(kh, q[:, c], 1, 1) * SCALE
                p = jnp.where(mask, jnp.exp(s - lse[h : h + 1]), 0.0)
                dp = dot(vh, g[:, c], 1, 1)
                ds = (p * (dp - deltas[h])).astype(BF16)
                dq_t[h] = dq_t[h] + dot(kh, ds, 0, 0)
                if j == 0:
                    dks.append(dot(ds, q[:, c]) * SCALE)
                    dvs.append(dot(p.astype(BF16), g[:, c]))
            if j == 0:
                acc[0:NQ, W : 2 * W] = jnp.concatenate(dks, axis=1)
                acc[0:NQ, 2 * W :] = jnp.concatenate(dvs, axis=1)
        dq_l = (jnp.concatenate(dq_t, axis=0).T * SCALE).astype(BF16)
        th_grad = jnp.zeros((NT, 3 * W), F32)
        bias = jnp.zeros((1, 3 * W), F32)
        for k in range(H):
            a = (zz ^ k) * Q + yy
            rows = slice(k * R, (k + 1) * R)
            kp = posc_ref[pl.ds(pl.multiple_of(a * R, R), R), :]
            src = jnp.where(kp == thr_ref[...] - 1, 1.0, 0.0).astype(BF16)
            tgt = jnp.where(kp == thr_ref[...], 1.0, 0.0)
            is_th = jnp.max(tgt, axis=1, keepdims=True) > 0
            kv = dkv_ref[k]
            for m in msgs:
                kv = kv + m[k].astype(F32)
            tok = jnp.concatenate([dq_ref[k].astype(F32), kv], axis=1)
            lat = jnp.concatenate([dot(src, dq_l), acc[rows, W:]], axis=1)
            both = (jnp.where(is_th, 0.0, tok) + lat).astype(BF16)
            hot = jnp.where(posb_ref[pl.ds(a, 1), :] == thc_ref[...], 1.0, 0.0).astype(BF16)
            th_grad = th_grad + dot(hot, tok.astype(BF16))
            tmp[rows] = both
        th_low = th_grad.astype(BF16)
        both = tmp[...]
        bias = col(both.astype(F32)) + col(th_low.astype(F32))
        for c in range(H):
            mine = jnp.where(zz == c, 1.0, 0.0)
            small_ref[4:5, c * W : (c + 1) * W] = bias[:, 0:W] * mine
            small_ref[5:6, c * W : (c + 1) * W] = bias[:, 2 * W :] * mine
        gain, shift = s1_ref[0:1], s1_ref[1:2]
        for k in range(H):
            gn = dot(tmp[k * R : (k + 1) * R], wq_ref[...], 1, 1)
            gain = gain + col(gn * scaled_ref[k].astype(F32))
            shift = shift + col(gn)
            if k < 2:
                (n0, n1)[k][...] = gn
            else:
                n32[(3 - k) * R : (4 - k) * R] = gn.astype(BF16)
        small_ref[0:1] = gain
        small_ref[2:3] = shift
        acc[...] = dot(normed_ref[...].reshape(NQ, D), both, 0, 0) + dot(nth_ref[...], th_low, 0, 0)
        fc = dh1_ref[...] + once * dh2_ref[...]
        fc_part = gsum_ref[:, D:].astype(F32)
        smalls = small_ref[...]
        for i, o in enumerate((o0, o1, o2, o3)):
            o[0:S] = acc[pl.ds(pl.multiple_of((ff ^ i) * S, 64), S), :].astype(o.dtype)
            rows = [jnp.concatenate([columns(smalls, ff ^ i), jnp.zeros((8, 3 * W - S), F32)], axis=1)]
            if i == 0:
                rows += [fc[:, c * S : (c + 1) * S] for c in range(FS // S)]
                rows[1:] = [
                    jnp.concatenate([jnp.concatenate(rows[1:], axis=0), jnp.zeros((8 - FS // S, S), F32)], axis=0)
                ]
                rows[1] = jnp.concatenate([rows[1], jnp.zeros((8, 3 * W - S), F32)], axis=1)
            else:
                rows += [jnp.zeros((8, 3 * W), F32)]
            o[S : S + 16] = jnp.concatenate(rows, axis=0).astype(o.dtype)
            block = columns(fc_part, ff ^ i)
            for c in range(3):
                o[S + 16 :, c * W : (c + 1) * W] = block[c * FR : (c + 1) * FR].astype(o.dtype)

    d_mid_lat, da_lat, *more = call(
        latent_back_body, "latent_backward",
        [
            ids, lengths, *lat_back, up, mid_lat, wo, vec, q_lat, ctx_lat, lse_lat, *qkvs,
            pos_blk, pos_col, th_row, th_col, dq, dkv, *kv_msgs, normed_y, normed_th, wq, scaled_y, sums1, sums2,
            dh_sum, dh_lat_sum, g_sum,
        ],
        [
            sds((NT, D), F32), sds((NT, D), BF16),
            sds((S + 16 + FR, 3 * W), F32), *[sds((S + 16 + FR, 3 * W), BF16)] * 3,
            sds((R, D), F32), sds((R, D), F32), sds((2 * R, D), BF16),
        ],
        scratch=[pltpu.VMEM((NQ, 3 * W), BF16), pltpu.VMEM((D, 3 * W), F32), pltpu.VMEM((8, D), F32)],
        n_smem=2,
    )
    gq, gn = more[:4], more[4:]
    gq = [gq[0]] + [flip(gq[i], i) for i in range(1, 4)]
    gn32 = flip_h(gn[2], 3)
    gn1 = flip_h((gn[1] + gn32[R:].astype(F32)).astype(BF16), 1)

    def tail_sum_body(g0, m1, m2, m3, gq_ref, fc_ref):
        rows = slice(0, S + 16)
        g = (g0[rows] + m1[rows].astype(F32)) + (m2[rows].astype(F32) + m3[rows].astype(F32))
        gq_ref[...] = g.astype(BF16)
        for i, m in enumerate((g0, m1, m2, m3)):
            for c in range(3):
                fc_ref[c * FR : (c + 1) * FR, i * S : (i + 1) * S] = m[S + 16 :, c * W : (c + 1) * W].astype(BF16)

    gq[0] = barrier(gq[0], gn32)[0]
    gq, piece_b = call(
        tail_sum_body, "tail_sum", gq, [sds((S + 16, 3 * W), BF16), sds((CR, 4 * S), BF16)], n_smem=0
    )
    if Q == 2:
        gq = (gq.astype(F32) + shift_q(gq, 1).astype(F32)).astype(BF16)
    else:
        every = jnp.roll(jnp.stack([gq] + [shift_q(gq, j) for j in range(1, Q)]), y, axis=0)
        gq = jnp.sum(every.astype(F32), axis=0).astype(BF16)
    gq1 = flip_h(gq, 1)
    gq32 = flip_h(jnp.concatenate([gq, gq1], axis=0), 3)
    piece_b = barrier(piece_b, gq)[0]
    every_b = gather_blk(piece_b) if CR % 16 == 0 else [lax.all_gather(piece_b, "blk", axis=0, tiled=True)]

    def final_body(n0, n1, n32, x_ref, dmid_ref, ownp_ref, thr_ref, dlat_ref, vec_ref, grad_ref):
        gn_now = (n0[...] + n1[...].astype(F32)) + n32[0:R].astype(F32)
        _, scaled, inverse = norm(x_ref[...].astype(F32), vec_ref[0:1, :], vec_ref[2:3, :])
        tgt = jnp.where(ownp_ref[...] == thr_ref[...], 1.0, 0.0)
        is_th = jnp.max(tgt, axis=1, keepdims=True) > 0
        src = jnp.where(ownp_ref[...] == thr_ref[...] - 1, 1.0, 0.0).astype(BF16)
        grad = jnp.where(is_th, 0.0, dmid_ref[...]) + norm_back(gn_now, scaled, inverse, vec_ref[0:1, :])
        grad_ref[...] = grad + spread(src, dlat_ref[...], 1)

    [grad_in] = call(
        final_body, "input_grad", [gn[0], gn1, gn32, own, d_mid, own_pos, th_row, d_mid_lat, vec], [sds((R, D), F32)], n_smem=0
    )

    da_lat_blocks = gather_f(barrier(da_lat, gq)[0])

    def place_blocks(ids_ref, refs, tmp):
        if len(refs) == 1:
            tmp[...] = refs[0][...]
            return
        for j in range(Q):
            for k in range(H):
                a = (ids_ref[0, 0] ^ k) * Q + lax.rem(ids_ref[0, 1] + j, Q)
                ref = refs[3 * j + min(k, 2)]
                block = ref[...] if k < 2 else ref[(3 - k) * CR : (4 - k) * CR]
                tmp[pl.ds(pl.multiple_of(a * CR, CR), CR), :] = block

    def a_grad_body(*refs):
        ids_ref, parts_a = refs[0], refs[1 : 1 + len(every_a)]
        act_ref, dm_ref, l0, m1, m2, m3, a0, a1, a2, a3, wp_ref, wo_ref, tmp = refs[1 + len(every_a) :]
        place_blocks(ids_ref, parts_a, tmp)
        wp_ref[...] = tmp[:, 0:D].astype(F32) + dot(act_ref[...], dm_ref[...], 0, 0)
        lats = [l0[...]]
        for m in (m1, m2, m3):
            lats.append(jnp.concatenate([m[R + S :, c * S : (c + 1) * S] for c in range(4)], axis=0))
        lat = [dot(l, a[...], 0, 0) for l, a in zip(lats, (a0, a1, a2, a3))]
        wo_ref[...] = tmp[:, D:].astype(F32).T + ((lat[0] + lat[1]) + (lat[2] + lat[3]))

    def b_grad_body(*refs):
        ids_ref, parts_b = refs[0], refs[1 : 1 + len(every_b)]
        second_ref, d0, d1, d2, d3, out_ref, tmp = refs[1 + len(every_b) :]
        ff = ids_ref[0, 2]
        place_blocks(ids_ref, parts_b, tmp)
        cols = columns(second_ref[...].astype(F32), ff).astype(BF16)
        for i, d in enumerate((d0, d1, d2, d3)):
            rows = jnp.concatenate([cols[(i ^ m) * NT : ((i ^ m) + 1) * NT] for m in range(4)], axis=0)
            block = tmp[:, i * S : (i + 1) * S].astype(F32).T + dot(rows, d[...], 0, 0)
            out_ref[:, pl.ds(pl.multiple_of((ff ^ i) * FS, 128), FS)] = block

    w_proj_g, w_out_g = call(
        a_grad_body, "proj_out_grad",
        [ids, *every_a, active_lat, dm_lat_all, lat_cols[0], *mix, *da_lat_blocks],
        [sds((FS, D), F32), sds((S, D), F32)],
        scratch=[pltpu.VMEM((FS, D + S), BF16)],
    )
    [w_fc_g] = call(
        b_grad_body, "fc_grad", [ids, *every_b, second_lat_all, *dh_lat_blocks], [sds((S, 4 * FS), F32)],
        scratch=[pltpu.VMEM((FS, 4 * S), BF16)],
    )

    def qkv_grad_body(
        ids_ref, g0, g1, g32, out_ref, small_ref, fb_ref, tmp
    ):
        zz = ids_ref[0, 0]
        tmp[zz] = g0[...]
        tmp[zz ^ 1] = g1[...]
        tmp[zz ^ 3] = g32[0 : S + 16]
        tmp[zz ^ 2] = g32[S + 16 :]
        small = [tmp[c][S:, 0:S].astype(F32) for c in range(H)]
        small = (small[0] + small[2]) + (small[1] + small[3])
        small_ref[...] = small[0:8]
        for c in range(FS // S):
            fb_ref[:, c * S : (c + 1) * S] = small[8 + c : 9 + c]
        for c in range(H):
            for i in range(3):
                out_ref[:, i * D + c * W : i * D + (c + 1) * W] = tmp[c][0:S, i * W : (i + 1) * W].astype(F32)

    w_qkv_g, small_g, fb_g = call(
        qkv_grad_body, "qkv_grad", [ids, gq, gq1, gq32],
        [sds((S, 3 * D), F32), sds((8, S), F32), sds((1, FS), F32)],
        scratch=[pltpu.VMEM((H, S + 16, 3 * W), BF16)],
    )
    return (
        result[None],
        grad_in[None],
        small_g[0:2],
        small_g[2:4],
        w_qkv_g,
        small_g[4:6],
        w_out_g,
        small_g[6],
        w_fc_g,
        fb_g[0],
        w_proj_g,
        small_g[7],
    )


def solution(mesh):
    a, r, v = P("fsdp", "blk", None), P("fsdp", None), P("fsdp")
    c = P(None, "fsdp")
    return jax.shard_map(
        local,
        mesh=mesh,
        in_specs=(a, r, r, r, c, c, r, c, r, v, r, v, r, v, a),
        out_specs=(a, a, c, c, r, c, r, v, r, v, r, v),
        check_vma=False,
    )
```

```python
import jax
import jax.numpy as jnp
from jax import lax
from jax.experimental import pallas as pl
from jax.experimental.pallas import tpu as pltpu
from jax.sharding import PartitionSpec as P

HDIM = 64
PARTS = 4
EPS = 1e-05
SCALE = HDIM ** (-0.5)
F32 = jnp.float32
BF16 = jnp.bfloat16
VMEM_BYTES = 60 * 1024 * 1024
INTERPRET = False


def dot(a, b, ca=1, cb=0):
    return lax.dot_general(a, b, (((ca,), (cb,)), ((), ())), preferred_element_type=F32)


def spread(hot, x, axis):
    total = None
    for _ in range(3):
        low = x.astype(BF16)
        x = x - low.astype(F32)
        part = dot(hot, low, axis, 0)
        total = part if total is None else total + part
    return total


def norm(x, gain, shift):
    center = x - jnp.mean(x, axis=-1, keepdims=True)
    inverse = lax.rsqrt(jnp.mean(center * center, axis=-1, keepdims=True) + EPS)
    scaled = center * inverse
    return (scaled * gain + shift).astype(BF16), scaled, inverse


def norm_back(up, scaled, inverse, gain):
    w = up * gain
    return inverse * (
        w - jnp.mean(w, axis=-1, keepdims=True) - scaled * jnp.mean(w * scaled, axis=-1, keepdims=True)
    )


C0 = 0.7978845608028654
C1 = 0.044715


def gelu(v):
    return 0.5 * v * (1.0 + jnp.tanh(C0 * (v + C1 * v * v * v)))


def gelu_back(v):
    t = jnp.tanh(C0 * (v + C1 * v * v * v))
    return 0.5 * (1.0 + t) + 0.5 * v * (1.0 - t * t) * C0 * (1.0 + 3 * C1 * v * v)


def start_of(p, len_ref):
    start = jnp.zeros_like(p)
    end = jnp.int32(0)
    for i in range(len_ref.shape[1] - 1):
        end = end + len_ref[0, i]
        start = jnp.where(p >= end, end, start)
    return start


def sds(shape, dtype):
    return jax.ShapeDtypeStruct(shape, dtype)


TIMES = {
    "pack": 2.0, "pack2": 2.5, "project": 4.1, "project_more": 3.5, "latent_attention": 4.6, "place": 3.8,
    "latent_out": 2.9, "latent_ffn": 3.8, "token_attention": 8.0, "token_out": 3.1, "ffn": 7.3, "ffn_grads": 5.6,
    "attention_gradient": 3.4, "out_grad": 3.2, "token_backward": 9.8, "out_sum": 2.9, "latent_ffn_backward": 3.9,
    "latent_grads": 3.1, "proj_grad": 2.9, "fc_out_grad": 3.7, "join": 2.0, "latent_backward": 9.6, "tail_sum": 2.3, "input_grad": 2.8, "proj_out_grad": 4.7, "fc_grad": 4.6,
    "qkv_grad": 3.1,
}
FLOPS_PER_US = 330_000_000


def call(body, name, args, outs, scratch=(), n_smem=1):
    vm = pl.BlockSpec(memory_space=pltpu.VMEM)
    sm = pl.BlockSpec(memory_space=pltpu.SMEM)
    return pl.pallas_call(
        body,
        name=name,
        out_shape=list(outs),
        in_specs=[sm] * n_smem + [vm] * (len(args) - n_smem),
        out_specs=[vm] * len(outs),
        scratch_shapes=list(scratch),
        cost_estimate=pl.CostEstimate(
            flops=int(TIMES.get(name, 2.0) * FLOPS_PER_US), bytes_accessed=0, transcendentals=0
        ),
        compiler_params=pltpu.CompilerParams(vmem_limit_bytes=VMEM_BYTES),
        interpret=INTERPRET,
    )(*args)


def local(
    tokens, slot_pos, lengths, thoughts, ln_gain, ln_shift, w_qkv, qv_bias, w_out, out_bias,
    w_fc, fc_bias, w_proj, proj_bias, cotangent,
):
    n_blk, n_f = lax.axis_size("blk"), lax.axis_size("fsdp")
    H = PARTS
    Q = n_blk // H
    b, f = lax.axis_index("blk"), lax.axis_index("fsdp")
    z, y = b // Q, b % Q
    R, D = tokens.shape[1], tokens.shape[2]
    T = R * n_blk
    W = D // H
    NH = W // HDIM
    S = D // n_f
    FS = w_proj.shape[0]
    NT = thoughts.shape[1]
    NQ = H * R
    KB = min(T, 256)

    def take(x, i, axis=0):
        return lax.dynamic_index_in_dim(x, i, axis, keepdims=False)

    def flip_h(x, k):
        return lax.ppermute(x, "blk", [((((c // Q) ^ k) * Q) + c % Q, c) for c in range(n_blk)])

    def shift_q(x, j):
        return lax.ppermute(x, "blk", [((c // Q) * Q + (c % Q + j) % Q, c) for c in range(n_blk)])

    def flip(x, bit):
        return lax.ppermute(x, "fsdp", [(c, c ^ bit) for c in range(n_f)])

    def gather_f(x):
        far = flip(x, 2)
        return [x, flip(x, 1), far, flip(far, 1)]

    def gather_h(x):
        return [x] + [flip_h(x, k) for k in range(1, H)]

    def barrier(*xs):
        return lax.optimization_barrier(xs)

    ids = jnp.stack([z, y, f, b]).astype(jnp.int32)[None]

    own = tokens[0]
    cot = cotangent[0]
    def pack_body(ids_ref, w_ref, gain_ref, shift_ref, qv_ref, ob_ref, pb_ref, out_ref):
        zz = ids_ref[0, 0]
        for c in range(H):

            @pl.when(zz == c)
            def _():
                for i in range(3):
                    out_ref[0:S, i * W : (i + 1) * W] = w_ref[:, i * D + c * W : i * D + (c + 1) * W]

        rows = [gain_ref[...].astype(F32), shift_ref[...].astype(F32), qv_ref[...].astype(F32)]
        rows += [ob_ref[...].astype(F32)[None, :], pb_ref[...].astype(F32)[None, :], jnp.zeros((8, S), F32)]
        rows = jnp.concatenate(rows, axis=0)
        rows = jnp.concatenate([rows, jnp.zeros((16, 3 * W - S), F32)], axis=1)
        out_ref[S : S + 16, :] = rows.astype(BF16)

    def pack2_body(ids_ref, fc_ref, wo_ref, far_ref, near_ref):
        ff = ids_ref[0, 2]

        def block(i):
            return fc_ref[:, pl.ds(pl.multiple_of((ff ^ i) * FS, 128), FS)]

        for ref in (far_ref, near_ref):
            ref[0:S] = wo_ref[...]
        far_ref[S : 2 * S] = block(3)
        far_ref[2 * S :] = block(2)
        near_ref[S:] = block(1)

    [part] = call(
        pack_body, "pack", [ids, w_qkv, ln_gain, ln_shift, qv_bias, out_bias, proj_bias],
        [sds((S + 16, 3 * W), BF16)])
    own1, own3 = flip_h(own, 1), flip_h(own, 3)
    own_y = [shift_q(own, j) for j in range(1, Q)]
    part, own1, own3 = barrier(part, own1, own3, own_y[0])[:3]
    own2 = flip_h(own3, 1)
    parts = gather_f(part)
    blocks = [[own, own1, own2, own3]]
    for j in range(1, Q):
        blocks.append([own_y[j - 1], shift_q(own1, j), shift_q(own2, j), shift_q(own3, j)])
    far0, near0 = call(
        pack2_body, "pack2", [ids, w_fc, w_out], [sds((3 * S, D), BF16), sds((2 * S, D), BF16)]
    )
    far0 = barrier(far0, parts[2], own2, blocks[1][1], blocks[1][3])[0]
    far_got = flip(far0, 2)

    pos = slot_pos
    pos_col = slot_pos.reshape(T, 1)
    pos_blk = slot_pos.reshape(n_blk, R)
    th_row = thoughts
    th_col = thoughts.reshape(NT, 1)

    def proj_body(ids_ref, p0, p1, p2, p3, x0, x1, x2, x3, qkv_ref, wq_ref, vec_ref, normed_ref, scaled_ref):
        zz, ff = ids_ref[0, 0], ids_ref[0, 2]
        smalls = []
        for i, p in enumerate((p0, p1, p2, p3)):
            wq_ref[pl.ds(pl.multiple_of((ff ^ i) * S, 64), S), :] = p[0:S, :]
            smalls.append(p[S : S + 16, 0:S].astype(F32)[0:8])
        for a in range(4):
            v = smalls[0]
            for i in range(1, 4):
                v = jnp.where((ff ^ i) == a, smalls[i], v)
            vec_ref[:, a * S : (a + 1) * S] = v
        bias = bias_of(vec_ref, zz)
        for k, x in enumerate((x0, x1, x2, x3)):
            n, scaled, _ = norm(x[...].astype(F32), vec_ref[0:1, :], vec_ref[2:3, :])
            normed_ref[k] = n
            scaled_ref[k] = scaled.astype(BF16)
            qkv_ref[k] = (dot(n, wq_ref[...]) + bias).astype(BF16)

    def bias_of(vec_ref, zz):
        qb = vec_ref[4:5, 0:W]
        vb = vec_ref[5:6, 0:W]
        for c in range(1, H):
            qb = jnp.where(zz == c, vec_ref[4:5, c * W : (c + 1) * W], qb)
            vb = jnp.where(zz == c, vec_ref[5:6, c * W : (c + 1) * W], vb)
        return jnp.concatenate([qb, jnp.zeros_like(qb), vb], axis=1)

    def proj_more(ids_ref, wq_ref, vec_ref, x0, x1, x2, x3, qkv_ref):
        bias = bias_of(vec_ref, ids_ref[0, 0])
        for k, x in enumerate((x0, x1, x2, x3)):
            n, _, _ = norm(x[...].astype(F32), vec_ref[0:1, :], vec_ref[2:3, :])
            qkv_ref[k] = (dot(n, wq_ref[...]) + bias).astype(BF16)

    qkv_y, wq, vec, normed_y, scaled_y = call(
        proj_body, "project", [ids, *parts, *blocks[0]],
        [sds((H, R, 3 * W), BF16), sds((D, 3 * W), BF16), sds((8, D), F32), sds((H, R, D), BF16), sds((H, R, D), BF16)],
    )
    qkvs = [qkv_y]
    for j in range(1, Q):
        qkvs += call(
            proj_more, "project_more", [ids, wq, vec, *blocks[j]], [sds((H, R, 3 * W), BF16)]
        )

    def attend(q, read_k, read_v, key_pos, q_pos, q_start, s_ref):
        n = q.shape[0]
        ctx, lse = [], []
        for h in range(NH):
            lanes = slice(h * HDIM, (h + 1) * HDIM)
            qh = q[:, lanes]

            def score(i, m):
                at = pl.multiple_of(i * KB, KB)
                s = dot(read_k(at, lanes), qh, 1, 1) * SCALE
                kp = key_pos(at)
                s = jnp.where((kp <= q_pos) & (kp >= q_start), s, -1e30)
                s_ref[pl.ds(at, KB), 0:n] = s
                return jnp.maximum(m, jnp.max(s, axis=0, keepdims=True))

            m = lax.fori_loop(0, T // KB, score, jnp.full((1, n), -1e30, F32), unroll=T // KB <= 4)

            def add(i, carry):
                total, acc = carry
                at = pl.multiple_of(i * KB, KB)
                e = jnp.exp(s_ref[pl.ds(at, KB), 0:n] - m)
                total = total + jnp.sum(e, axis=0, keepdims=True)
                return total, acc + dot(read_v(at, lanes), e.astype(BF16), 0, 0)

            total, acc = lax.fori_loop(
                0, T // KB, add, (jnp.zeros((1, n), F32), jnp.zeros((HDIM, n), F32)), unroll=T // KB <= 4
            )
            ctx.append(acc / total)
            lse.append(m + jnp.log(total))
        return jnp.concatenate(ctx, axis=0), jnp.concatenate(lse, axis=0)

    def latent_body(*refs):
        ids_ref, len_ref, pos_ref, posb_ref, posc_ref, thr_ref, thc_ref = refs[:7]
        qkv_refs = refs[7 : 7 + Q]
        x_refs = refs[7 + Q : 7 + Q + n_blk]
        low_ref, ctx_ref, lse_ref, q_ref, x_ref, abs_ref, s_ref = refs[7 + Q + n_blk :]
        zz, yy = ids_ref[0, 0], ids_ref[0, 1]
        src = thc_ref[...] - 1
        x_lat = jnp.zeros((NT, D), F32)
        for j in range(Q):
            for k in range(H):
                a = (zz ^ k) * Q + lax.rem(yy + j, Q)
                abs_ref[pl.ds(pl.multiple_of(a * R, R), R), :] = qkv_refs[j][k]
                hot = jnp.where(posb_ref[pl.ds(a, 1), :] == src, 1.0, 0.0).astype(BF16)
                x_lat = x_lat + dot(hot, x_refs[j * H + k][...])
        x_ref[...] = x_lat
        hot = jnp.where(pos_ref[...] == src, 1.0, 0.0).astype(BF16)
        q = dot(hot, abs_ref[:, 0:W]).astype(BF16)
        q_ref[...] = q
        p = thr_ref[...] - 1
        ctx, lse = attend(
            q,
            lambda at, c: abs_ref[pl.ds(at, KB), W + c.start : W + c.stop],
            lambda at, c: abs_ref[pl.ds(at, KB), 2 * W + c.start : 2 * W + c.stop],
            lambda at: posc_ref[pl.ds(at, KB), :],
            p,
            start_of(p, len_ref),
            s_ref,
        )
        ctx_ref[...] = ctx
        lse_ref[...] = lse
        low_ref[...] = ctx.T.astype(BF16)

    flat = [x for group in blocks for x in group]
    ctx_lat_low, ctx_lat, lse_lat, q_lat, x_lat, qkv_abs = call(
        latent_body, "latent_attention",
        [ids, lengths, pos, pos_blk, pos_col, th_row, th_col, *qkvs, *flat],
        [
            sds((NT, W), BF16), sds((W, NT), F32), sds((NH, NT), F32), sds((NT, W), BF16),
            sds((NT, D), F32), sds((T, 3 * W), BF16),
        ],
        scratch=[pltpu.VMEM((T, 128), F32)],
        n_smem=2,
    )
    ctx_lat_blocks = gather_h(ctx_lat_low)

    far_got, near0 = barrier(far_got, near0, ctx_lat_low)[:2]
    near_got = flip(near0, 1)
    both_got = flip(far_got, 1)

    def place_body(ids_ref, far0_ref, far_ref, near_ref, both_ref, fc_ref, wo_ref, wf_ref):
        ff = ids_ref[0, 2]

        def at(i):
            return pl.ds(pl.multiple_of((ff ^ i) * S, 64), S)

        for i, ref in enumerate((far0_ref, near_ref, far_ref, both_ref)):
            wo_ref[at(i), :] = ref[0:S]
        wf_ref[at(0), :] = fc_ref[:, pl.ds(pl.multiple_of(ff * FS, 128), FS)]
        wf_ref[at(1), :] = near_ref[S:]
        wf_ref[at(2), :] = far_ref[2 * S :]
        wf_ref[at(3), :] = both_ref[S : 2 * S]

    wo, wf = call(
        place_body, "place", [ids, far0, far_got, near_got, both_got, w_fc], [sds((D, D), BF16), sds((D, FS), BF16)]
    )
    fb = fc_bias[None]

    def columns(x, i):
        v = x[:, 0:S]
        for c in range(1, 4):
            v = jnp.where(i == c, x[:, c * S : (c + 1) * S], v)
        return v

    def latent_out_body(ids_ref, c0, c1, c2, c3, x_ref, wo_ref, vec_ref, mid_ref, low_ref, l0, l1, l2, l3, all_ref, tmp):
        zz, ff = ids_ref[0, 0], ids_ref[0, 2]
        for k, c in enumerate((c0, c1, c2, c3)):
            tmp[zz ^ k] = c[...]
        for i in range(H):
            all_ref[:, i * W : (i + 1) * W] = tmp[i]
        mid = x_ref[...] + (dot(all_ref[...], wo_ref[...]) + vec_ref[6:7, :])
        mid_ref[...] = mid
        low_ref[...] = norm(mid, vec_ref[1:2, :], vec_ref[3:4, :])[0]
        both = all_ref[...].astype(F32)
        for i, o in enumerate((l0, l1, l2, l3)):
            o[...] = columns(both, ff ^ i).astype(BF16)

    mid_lat, second_lat, *lat_cols = call(
        latent_out_body, "latent_out", [ids, *ctx_lat_blocks, x_lat, wo, vec],
        [sds((NT, D), F32), sds((NT, D), BF16)] + [sds((NT, S), BF16)] * 4,
        scratch=[pltpu.VMEM((NT, D), BF16), pltpu.VMEM((H, NT, W), BF16)],
    )
    second_lat_blocks = gather_f(second_lat)

    def latent_ffn_body(s0, s1, s2, s3, wf_ref, wp_ref, fb_ref, hid_ref, act_ref, all_ref, o0, o1, o2, o3):
        for i, s in enumerate((s0, s1, s2, s3)):
            all_ref[i * NT : (i + 1) * NT] = s[...]
        hidden = dot(all_ref[...], wf_ref[...]) + fb_ref[...].astype(F32)
        hid_ref[...] = hidden
        act_ref[...] = gelu(hidden).astype(BF16)
        out = dot(act_ref[...], wp_ref[...])
        for i, o in enumerate((o0, o1, o2, o3)):
            o[...] = out[i * NT : (i + 1) * NT].astype(o.dtype)

    hidden_lat, active_lat, second_lat_all, *outs = call(
        latent_ffn_body, "latent_ffn", [*second_lat_blocks, wf, w_proj, fb],
        [sds((4 * NT, FS), F32), sds((4 * NT, FS), BF16), sds((4 * NT, D), BF16), sds((NT, D), F32)]
        + [sds((NT, D), BF16)] * 3,
        n_smem=0,
    )
    outs = [outs[0]] + [flip(outs[i], i) for i in range(1, 4)]
    dm_blocks = gather_f(barrier(cot, outs[2], outs[3])[0])

    def token_body(
        ids_ref, len_ref, o0, o1, o2, o3, mid_ref, vec_ref, wq_ref, abs_ref, qy_ref, posb_ref, posc_ref, thr_ref,
        lat_ref, nth_ref, kv_ref, q_ref, ctx_ref, lse_ref, c0, c1, c2, c3, s_ref,
    ):
        zz, yy = ids_ref[0, 0], ids_ref[0, 1]
        lat = mid_ref[...] + (
            (o0[...] + o1[...].astype(F32) + (o2[...].astype(F32) + o3[...].astype(F32))) + vec_ref[7:8, :]
        )
        lat_ref[...] = lat
        nth = norm(lat, vec_ref[0:1, :], vec_ref[2:3, :])[0]
        nth_ref[...] = nth
        qkv_th = (dot(nth, wq_ref[...]) + bias_of(vec_ref, zz)).astype(BF16)

        def fill(i, _):
            at = pl.multiple_of(i * KB, KB)
            hot = posc_ref[pl.ds(at, KB), :] == thr_ref[...]
            is_th = jnp.max(jnp.where(hot, 1.0, 0.0), axis=1, keepdims=True) > 0
            new = dot(jnp.where(hot, 1.0, 0.0).astype(BF16), qkv_th[:, W:])
            kv_ref[pl.ds(at, KB), :] = jnp.where(is_th, new, abs_ref[pl.ds(at, KB), W:].astype(F32)).astype(BF16)
            return 0

        lax.fori_loop(0, T // KB, fill, 0, unroll=T // KB <= 4)
        rows = []
        for k in range(H):
            a = (zz ^ k) * Q + yy
            hot = posc_ref[pl.ds(pl.multiple_of(a * R, R), R), :] == thr_ref[...]
            is_th = jnp.max(jnp.where(hot, 1.0, 0.0), axis=1, keepdims=True) > 0
            new = dot(jnp.where(hot, 1.0, 0.0).astype(BF16), qkv_th[:, 0:W])
            q_ref[k] = jnp.where(is_th, new, qy_ref[k][:, 0:W].astype(F32)).astype(BF16)
            rows.append(posb_ref[pl.ds(a, 1), :])
        p = jnp.concatenate(rows, axis=1)
        ctx, lse = attend(
            q_ref[...].reshape(NQ, W),
            lambda at, c: kv_ref[pl.ds(at, KB), c],
            lambda at, c: kv_ref[pl.ds(at, KB), W + c.start : W + c.stop],
            lambda at: posc_ref[pl.ds(at, KB), :],
            p,
            start_of(p, len_ref),
            s_ref,
        )
        ctx_ref[...] = ctx
        lse_ref[...] = lse
        low = ctx.T.astype(BF16)
        for k, c in enumerate((c0, c1, c2, c3)):
            c[...] = low[k * R : (k + 1) * R]

    lat_out, normed_th, kv_tok, q_tok, ctx_t, lse, *ctx_blocks = call(
        token_body, "token_attention",
        [ids, lengths, *outs, mid_lat, vec, wq, qkv_abs, qkv_y, pos_blk, pos_col, th_row],
        [
            sds((NT, D), F32), sds((NT, D), BF16), sds((T, 2 * W), BF16), sds((H, R, W), BF16),
            sds((W, NQ), F32), sds((NH, NQ), F32),
        ]
        + [sds((R, W), BF16)] * 4,
        scratch=[pltpu.VMEM((T, NQ), F32)],
        n_smem=2,
    )
    ctx_blocks = [ctx_blocks[0]] + [flip_h(ctx_blocks[k], k) for k in range(1, H)]
    own_pos = lax.dynamic_slice_in_dim(pos_col, b * R, R, axis=0)

    def token_out_body(
        ids_ref, c0, c1, c2, c3, x_ref, posc_ref, thr_ref, lat_ref, wo_ref, vec_ref, mid_ref, low_ref, all_ref, tmp
    ):
        zz = ids_ref[0, 0]
        for k, c in enumerate((c0, c1, c2, c3)):
            tmp[zz ^ k] = c[...]
        for i in range(H):
            all_ref[:, i * W : (i + 1) * W] = tmp[i]
        hot = jnp.where(posc_ref[...] == thr_ref[...], 1.0, 0.0)
        is_th = jnp.max(hot, axis=1, keepdims=True) > 0
        x = jnp.where(is_th, spread(hot.astype(BF16), lat_ref[...], 1), x_ref[...].astype(F32))
        mid = x + (dot(all_ref[...], wo_ref[...]) + vec_ref[6:7, :])
        mid_ref[...] = mid
        low_ref[...] = norm(mid, vec_ref[1:2, :], vec_ref[3:4, :])[0]

    mid, second, ctx_own = call(
        token_out_body, "token_out", [ids, *ctx_blocks, own, own_pos, th_row, lat_out, wo, vec],
        [sds((R, D), F32), sds((R, D), BF16), sds((R, D), BF16)],
        scratch=[pltpu.VMEM((H, R, W), BF16)],
    )
    second_blocks = gather_f(second)

    def ffn_body(s0, s1, s2, s3, d0, d1, d2, d3, wf_ref, wp_ref, fb_ref, act_ref, dh_ref, all_ref, dm_ref, sum_ref, o0, o1, o2, o3):
        for i, (s, d, o) in enumerate(zip((s0, s1, s2, s3), (d0, d1, d2, d3), (o0, o1, o2, o3))):
            rows = slice(i * R, (i + 1) * R)
            all_ref[rows] = s[...]
            dm_ref[rows] = d[...]
            hidden = dot(s[...], wf_ref[...]) + fb_ref[...].astype(F32)
            t = jnp.tanh(C0 * (hidden + C1 * hidden * hidden * hidden))
            act_ref[rows] = (0.5 * hidden * (1.0 + t)).astype(BF16)
            back = 0.5 * (1.0 + t) + 0.5 * hidden * (1.0 - t * t) * C0 * (1.0 + 3 * C1 * hidden * hidden)
            dh = (dot(d[...], wp_ref[...], 1, 1) * back).astype(BF16)
            dh_ref[rows] = dh
            o[...] = dot(dh, wf_ref[...], 1, 1).astype(o.dtype)
        sum_ref[...] = jnp.sum(dh_ref[...].astype(F32), axis=0, keepdims=True)

    active, dh, second_all, dm_all, dh_sum, *back = call(
        ffn_body, "ffn", [*second_blocks, *dm_blocks, wf, w_proj, fb],
        [sds((4 * R, FS), BF16), sds((4 * R, FS), BF16), sds((4 * R, D), BF16), sds((4 * R, D), BF16), sds((1, FS), F32), sds((R, D), F32)]
        + [sds((R, D), BF16)] * 3,
        n_smem=0,
    )
    back = [back[0]] + [flip(back[i], i) for i in range(1, 4)]

    def grads_body(act_ref, dh_ref, all_ref, dm_ref, wp_ref, g_ref, o0, o1, o2, o3):
        out = dot(act_ref[...], wp_ref[...])
        for i, o in enumerate((o0, o1, o2, o3)):
            o[...] = out[i * R : (i + 1) * R].astype(o.dtype)
        g_ref[:, 0:D] = dot(act_ref[...], dm_ref[...], 0, 0).astype(BF16)
        g_ref[:, D:] = dot(dh_ref[...], all_ref[...], 0, 0).astype(BF16)

    g_ffn, *res = call(
        grads_body, "ffn_grads", [active, dh, second_all, dm_all, w_proj],
        [sds((FS, 2 * D), BF16), sds((R, D), F32)] + [sds((R, D), BF16)] * 3,
        n_smem=0,
    )
    g_ffn_later = barrier(g_ffn, back[2], back[3])[0]
    g_sum = lax.psum_scatter(g_ffn_later, "blk", scatter_dimension=0, tiled=True)
    back[0] = barrier(back[0], g_ffn)[0]

    def attn_in_body(ids_ref, b0, b1, b2, b3, mid_ref, cot_ref, wo_ref, vec_ref, dmid_ref, da_ref, sum_ref, c0, c1, c2, c3):
        zz = ids_ref[0, 0]
        up = (b0[...] + b1[...].astype(F32)) + (b2[...].astype(F32) + b3[...].astype(F32))
        _, scaled, inverse = norm(mid_ref[...], vec_ref[1:2, :], vec_ref[3:4, :])
        cot_now = cot_ref[...].astype(F32)
        d_mid = cot_now + norm_back(up, scaled, inverse, vec_ref[1:2, :])
        dmid_ref[...] = d_mid
        da = d_mid.astype(BF16)
        da_ref[...] = da
        for k, c in enumerate((c0, c1, c2, c3)):
            w = wo_ref[pl.ds(pl.multiple_of((zz ^ k) * W, 64), W), :]
            c[...] = dot(da, w, 1, 1).astype(BF16)
        sum_ref[0:1] = jnp.sum(up * scaled, axis=0, keepdims=True)
        sum_ref[1:2] = jnp.sum(up, axis=0, keepdims=True)
        sum_ref[2:3] = jnp.sum(da.astype(F32), axis=0, keepdims=True)
        sum_ref[3:4] = jnp.sum(cot_now, axis=0, keepdims=True)

    d_mid, da, sums2, *grad_blocks = call(
        attn_in_body, "attention_gradient", [ids, *back, mid, cot, wo, vec],
        [sds((R, D), F32), sds((R, D), BF16), sds((4, D), F32)] + [sds((R, W), BF16)] * 4,
    )
    grad_blocks = [grad_blocks[0]] + [flip_h(grad_blocks[k], k) for k in range(1, H)]

    def out_grad_body(ids_ref, ctx_ref, da_ref, r1, r2, r3, l1, l2, l3, o0, o1, o2, o3, tmp):
        ff = ids_ref[0, 2]
        tmp[...] = dot(ctx_ref[...], da_ref[...], 0, 0)
        own_rows = pl.ds(pl.multiple_of(ff * S, 64), S)
        o0[...] = tmp[own_rows, :]
        for i, (r, l, o) in enumerate(((r1, l1, o1), (r2, l2, o2), (r3, l3, o3)), 1):
            o[0:R] = r[...]
            o[R : R + S] = tmp[pl.ds(pl.multiple_of((ff ^ i) * S, 64), S), :].astype(BF16)
            for c in range(4):
                o[R + S :, c * S : (c + 1) * S] = l[c * NT // 4 : (c + 1) * NT // 4, :]

    g_out, *mix = call(
        out_grad_body, "out_grad", [ids, ctx_own, da, *res[1:], *lat_cols[1:]],
        [sds((S, D), F32)] + [sds((R + S + NT // 4, D), BF16)] * 3,
        scratch=[pltpu.VMEM((D, D), F32)],
    )
    grad_blocks[0] = barrier(grad_blocks[0], g_out)[0]
    mix = list(barrier(*mix, *grad_blocks[1:])[:3])
    mix = [flip(mix[i - 1], i) for i in range(1, 4)]

    def attend_back(q, g, read_k, read_v, key_pos, q_pos, q_start, lse, ctx, n_keys, put):
        n = q.shape[0]
        g_t = g.astype(F32).T
        dqs = []
        deltas = [
            jnp.sum(g_t[h * HDIM : (h + 1) * HDIM] * ctx[h * HDIM : (h + 1) * HDIM], axis=0, keepdims=True)
            for h in range(NH)
        ]

        def step(i, dq):
            at = pl.multiple_of(i * KB, KB)
            kp = key_pos(at)
            mask = (kp <= q_pos) & (kp >= q_start)
            dks, dvs, new = [], [], []
            for h in range(NH):
                lanes = slice(h * HDIM, (h + 1) * HDIM)
                kh = read_k(at, lanes)
                s = dot(kh, q[:, lanes], 1, 1) * SCALE
                p = jnp.where(mask, jnp.exp(s - lse[h : h + 1]), 0.0)
                dp = dot(read_v(at, lanes), g[:, lanes], 1, 1)
                ds = (p * (dp - deltas[h])).astype(BF16)
                new.append(dq[h] + dot(kh, ds, 0, 0))
                dks.append(dot(ds, q[:, lanes]) * SCALE)
                dvs.append(dot(p.astype(BF16), g[:, lanes]))
            put(at, jnp.concatenate(dks, axis=1), jnp.concatenate(dvs, axis=1))
            return tuple(new)

        dq = lax.fori_loop(
            0, n_keys // KB, step, tuple(jnp.zeros((HDIM, n), F32) for _ in range(NH)), unroll=n_keys // KB <= 4
        )
        return jnp.concatenate(dq, axis=0).T * SCALE

    def token_back_body(
        ids_ref, len_ref, g0, g1, g2, g3, q_ref, kv_ref, ctx_ref, lse_ref, pos_ref, posb_ref, posc_ref, thr_ref, thc_ref,
        ownp_ref, wq_ref, lat_ref, vec_ref, dmid_ref,
        up_ref, dq_ref, dkv_ref, sum_ref, *rest,
    ):
        msgs, acc = rest[:-1], rest[-1]
        zz, yy = ids_ref[0, 0], ids_ref[0, 1]
        rows = [posb_ref[pl.ds((zz ^ k) * Q + yy, 1), :] for k in range(H)]
        p = jnp.concatenate(rows, axis=1)

        def put(at, dk, dv):
            acc[pl.ds(at, KB), 0:W] = dk
            acc[pl.ds(at, KB), W:] = dv

        dq = attend_back(
            q_ref[...].reshape(NQ, W),
            jnp.concatenate([g0[...], g1[...], g2[...], g3[...]], axis=0),
            lambda at, c: kv_ref[pl.ds(at, KB), c],
            lambda at, c: kv_ref[pl.ds(at, KB), W + c.start : W + c.stop],
            lambda at: posc_ref[pl.ds(at, KB), :],
            p,
            start_of(p, len_ref),
            lse_ref[...],
            ctx_ref[...],
            T,
            put,
        ).astype(BF16)
        hot_y = jnp.where(p == thc_ref[...], 1.0, 0.0).astype(BF16)
        hot = jnp.where(pos_ref[...] == thc_ref[...], 1.0, 0.0).astype(BF16)
        d_q = dot(hot_y, dq).astype(BF16)
        d_kv = dot(hot, acc[...].astype(BF16)).astype(BF16)
        gn = dot(d_q, wq_ref[:, 0:W], 1, 1) + dot(d_kv, wq_ref[:, W:], 1, 1)
        _, scaled, inverse = norm(lat_ref[...], vec_ref[0:1, :], vec_ref[2:3, :])
        sum_ref[0:1] = jnp.sum(gn * scaled, axis=0, keepdims=True)
        sum_ref[1:2] = jnp.sum(gn, axis=0, keepdims=True)
        hot_own = jnp.where(ownp_ref[...] == thr_ref[...], 1.0, 0.0).astype(BF16)
        up = norm_back(gn, scaled, inverse, vec_ref[0:1, :]) + spread(hot_own, dmid_ref[...], 0)
        up_ref[...] = up.astype(BF16)
        for k in range(H):
            dq_ref[k] = dq[k * R : (k + 1) * R]
            for j in range(Q):
                a = (zz ^ k) * Q + lax.rem(yy - j + Q, Q)
                block = acc[pl.ds(pl.multiple_of(a * R, R), R), :]
                if j == 0:
                    dkv_ref[k] = block
                else:
                    msgs[j - 1][k] = block.astype(BF16)

    up, dq, dkv, sums1, *kv_msgs = call(
        token_back_body, "token_backward",
        [
            ids, lengths, *grad_blocks, q_tok, kv_tok, ctx_t, lse, pos, pos_blk, pos_col, th_row, th_col,
            own_pos, wq, lat_out, vec, d_mid,
        ],
        [sds((NT, D), BF16), sds((H, R, W), BF16), sds((H, R, 2 * W), F32), sds((2, D), F32)]
        + [sds((H, R, 2 * W), BF16)] * (Q - 1),
        scratch=[pltpu.VMEM((T, 2 * W), F32)],
        n_smem=2,
    )
    if Q == 2:
        up = (up.astype(F32) + shift_q(up, 1).astype(F32)).astype(BF16)
    else:
        ups = jnp.roll(jnp.stack([up] + [shift_q(up, j) for j in range(1, Q)]), y, axis=0)
        up = jnp.sum(ups.astype(F32), axis=0).astype(BF16)
    ups = [x.astype(F32) for x in gather_h(up)]
    up = (ups[0] + ups[2]) + (ups[1] + ups[3])
    kv_msgs = list(barrier(*kv_msgs, up)[:-1])
    kv_msgs = [shift_q(kv_msgs[j - 1], j) for j in range(1, Q)]

    dm_lat = up.astype(BF16)
    dm_lat_blocks = gather_f(dm_lat)

    def latent_ffn_back_body(d0, d1, d2, d3, hid_ref, wf_ref, wp_ref, all_ref, dh_ref, sum_ref, o0, o1, o2, o3):
        for i, d in enumerate((d0, d1, d2, d3)):
            all_ref[i * NT : (i + 1) * NT] = d[...]
        dh = (dot(all_ref[...], wp_ref[...], 1, 1) * gelu_back(hid_ref[...])).astype(BF16)
        dh_ref[...] = dh
        out = dot(dh, wf_ref[...], 1, 1)
        for i, o in enumerate((o0, o1, o2, o3)):
            o[...] = out[i * NT : (i + 1) * NT].astype(o.dtype)
        sum_ref[...] = jnp.sum(dh.astype(F32), axis=0, keepdims=True)

    CR = FS // n_blk
    FR = CR // 3

    def out_sum_body(g0, m1, m2, m3, mid_ref, vec_ref, r0, out_ref, g_ref):
        rows = slice(R, R + S)
        g = (g0[...] + m1[rows].astype(F32)) + (m2[rows].astype(F32) + m3[rows].astype(F32))
        g_ref[...] = g.T.astype(BF16)
        out = (r0[...] + m1[0:R].astype(F32)) + (m2[0:R].astype(F32) + m3[0:R].astype(F32))
        out_ref[...] = (mid_ref[...] + (out + vec_ref[7:8, :])).astype(BF16)

    mix_now = barrier(*mix, ups[2])[:3]
    result, g_out = call(
        out_sum_body, "out_sum", [g_out, *mix_now, mid, vec, res[0]], [sds((R, D), BF16), sds((D, S), BF16)], n_smem=0
    )
    g_out = g_out.reshape(H, Q, CR, S)
    got = [shift_q(take(g_out, (y - j) % Q, 1), j).astype(F32) for j in range(1, Q)]
    g_out = take(g_out, y, 1).astype(F32)
    for t in got:
        g_out = g_out + t
    g_out = g_out.astype(BF16)
    dm_lat_blocks[0], g_out = barrier(dm_lat_blocks[0], g_out)
    g_out = [take(g_out, z)] + [flip_h(take(g_out, z ^ k), k) for k in range(1, H)]

    dm_lat_all, dh_lat, dh_lat_sum, *lat_back = call(
        latent_ffn_back_body, "latent_ffn_backward", [*dm_lat_blocks, hidden_lat, wf, w_proj],
        [sds((4 * NT, D), BF16), sds((4 * NT, FS), BF16), sds((1, FS), F32), sds((NT, D), F32)]
        + [sds((NT, D), BF16)] * 3,
        n_smem=0,
    )
    lat_back = [lat_back[0]] + [flip(lat_back[i], i) for i in range(1, 4)]
    def join_body(g_ref, c0, c1, c2, c3, out_ref):
        out_ref[:, 0:D] = g_ref[:, 0:D]
        c = (c0[...].astype(F32) + c2[...].astype(F32)) + (c1[...].astype(F32) + c3[...].astype(F32))
        out_ref[:, D:] = c.astype(BF16)

    def gather_blk(x):
        x3 = flip_h(x, 3)
        x12 = flip_h(jnp.concatenate([x, x3], axis=0), 1)
        got = [x, x3, x12]
        for j in range(1, Q):
            got += [shift_q(t, j) for t in (x, x3, x12)]
        return got

    g_sum = barrier(g_sum, lat_back[2], lat_back[3])[0]
    [piece_a] = call(join_body, "join", [g_sum, *g_out], [sds((CR, D + S), BF16)], n_smem=0)
    lat_back[0] = barrier(lat_back[0], piece_a)[0]
    every_a = gather_blk(piece_a) if CR % 16 == 0 else [lax.all_gather(piece_a, "blk", axis=0, tiled=True)]
    dh_lat_blocks = gather_f(barrier(dh_lat, lat_back[2], lat_back[3])[0])

    def latent_back_body(*refs):
        ids_ref, len_ref, b0, b1, b2, b3, up_ref, mid_ref, wo_ref, vec_ref, q_ref, ctx_ref, lse_ref = refs[:13]
        qkv_refs = refs[13 : 13 + Q]
        posb_ref, posc_ref, thr_ref, thc_ref, dq_ref, dkv_ref = refs[13 + Q : 19 + Q]
        msgs = refs[19 + Q : 18 + 2 * Q]
        normed_ref, nth_ref, wq_ref, scaled_ref, s1_ref, s2_ref, dh1_ref, dh2_ref, gsum_ref = refs[18 + 2 * Q : 27 + 2 * Q]
        dmid_ref, da_ref, o0, o1, o2, o3, n0, n3, n12, tmp, acc, small_ref = refs[27 + 2 * Q :]
        once = jnp.where(ids_ref[0, 3] == 0, 1.0, 0.0)
        zz, yy, ff = ids_ref[0, 0], ids_ref[0, 1], ids_ref[0, 2]
        back = (b0[...] + b1[...].astype(F32)) + (b2[...].astype(F32) + b3[...].astype(F32))
        _, scaled, inverse = norm(mid_ref[...], vec_ref[1:2, :], vec_ref[3:4, :])
        d_mid = up_ref[...] + norm_back(back, scaled, inverse, vec_ref[1:2, :])
        dmid_ref[...] = d_mid
        da = d_mid.astype(BF16)
        da_ref[...] = da
        col = lambda t: jnp.sum(t, axis=0, keepdims=True)
        small_ref[1:2] = s2_ref[0:1] + once * col(back * scaled)
        small_ref[3:4] = s2_ref[1:2] + once * col(back)
        small_ref[6:7] = s2_ref[2:3] + once * col(da.astype(F32))
        small_ref[7:8] = s2_ref[3:4] + once * col(up_ref[...].astype(BF16).astype(F32))
        g = dot(da, wo_ref[pl.ds(pl.multiple_of(zz * W, 64), W), :], 1, 1).astype(BF16)
        q = q_ref[...]
        p_row = thr_ref[...] - 1
        start = start_of(p_row, len_ref)
        lse = lse_ref[...]
        g_t = g.astype(F32).T
        deltas = [
            jnp.sum(g_t[h * HDIM : (h + 1) * HDIM] * ctx_ref[h * HDIM : (h + 1) * HDIM], axis=0, keepdims=True)
            for h in range(NH)
        ]
        dq_t = [jnp.zeros((HDIM, NT), F32) for _ in range(NH)]
        for j in range(Q):
            kps = [posc_ref[pl.ds(pl.multiple_of(((zz ^ k) * Q + lax.rem(yy + j, Q)) * R, R), R), :] for k in range(H)]
            kp = jnp.concatenate(kps, axis=0)
            mask = (kp <= p_row) & (kp >= start)
            dks, dvs = [], []
            for h in range(NH):
                c = slice(h * HDIM, (h + 1) * HDIM)
                kh = qkv_refs[j][:, :, W + c.start : W + c.stop].reshape(NQ, HDIM)
                vh = qkv_refs[j][:, :, 2 * W + c.start : 2 * W + c.stop].reshape(NQ, HDIM)
                s = dot(kh, q[:, c], 1, 1) * SCALE
                p = jnp.where(mask, jnp.exp(s - lse[h : h + 1]), 0.0)
                dp = dot(vh, g[:, c], 1, 1)
                ds = (p * (dp - deltas[h])).astype(BF16)
                dq_t[h] = dq_t[h] + dot(kh, ds, 0, 0)
                if j == 0:
                    dks.append(dot(ds, q[:, c]) * SCALE)
                    dvs.append(dot(p.astype(BF16), g[:, c]))
            if j == 0:
                acc[0:NQ, W : 2 * W] = jnp.concatenate(dks, axis=1)
                acc[0:NQ, 2 * W :] = jnp.concatenate(dvs, axis=1)
        dq_l = (jnp.concatenate(dq_t, axis=0).T * SCALE).astype(BF16)
        th_grad = jnp.zeros((NT, 3 * W), F32)
        bias = jnp.zeros((1, 3 * W), F32)
        for k in range(H):
            a = (zz ^ k) * Q + yy
            rows = slice(k * R, (k + 1) * R)
            kp = posc_ref[pl.ds(pl.multiple_of(a * R, R), R), :]
            src = jnp.where(kp == thr_ref[...] - 1, 1.0, 0.0).astype(BF16)
            tgt = jnp.where(kp == thr_ref[...], 1.0, 0.0)
            is_th = jnp.max(tgt, axis=1, keepdims=True) > 0
            kv = dkv_ref[k]
            for m in msgs:
                kv = kv + m[k].astype(F32)
            tok = jnp.concatenate([dq_ref[k].astype(F32), kv], axis=1)
            lat = jnp.concatenate([dot(src, dq_l), acc[rows, W:]], axis=1)
            both = (jnp.where(is_th, 0.0, tok) + lat).astype(BF16)
            hot = jnp.where(posb_ref[pl.ds(a, 1), :] == thc_ref[...], 1.0, 0.0).astype(BF16)
            th_grad = th_grad + dot(hot, tok.astype(BF16))
            tmp[rows] = both
        th_low = th_grad.astype(BF16)
        both = tmp[...]
        bias = col(both.astype(F32)) + col(th_low.astype(F32))
        for c in range(H):
            mine = jnp.where(zz == c, 1.0, 0.0)
            small_ref[4:5, c * W : (c + 1) * W] = bias[:, 0:W] * mine
            small_ref[5:6, c * W : (c + 1) * W] = bias[:, 2 * W :] * mine
        gain, shift = s1_ref[0:1], s1_ref[1:2]
        for k in range(H):
            gn = dot(tmp[k * R : (k + 1) * R], wq_ref[...], 1, 1)
            gain = gain + col(gn * scaled_ref[k].astype(F32))
            shift = shift + col(gn)
            if k in (0, 3):
                (n0, n3)[k // 3][...] = gn
            else:
                n12[(k - 1) * R : k * R] = gn.astype(BF16)
        small_ref[0:1] = gain
        small_ref[2:3] = shift
        acc[...] = dot(normed_ref[...].reshape(NQ, D), both, 0, 0) + dot(nth_ref[...], th_low, 0, 0)
        fc = dh1_ref[...] + once * dh2_ref[...]
        fc_part = gsum_ref[:, D:].astype(F32)
        smalls = small_ref[...]
        for i, o in enumerate((o0, o1, o2, o3)):
            o[0:S] = acc[pl.ds(pl.multiple_of((ff ^ i) * S, 64), S), :].astype(o.dtype)
            rows = [jnp.concatenate([columns(smalls, ff ^ i), jnp.zeros((8, 3 * W - S), F32)], axis=1)]
            if i == 0:
                rows += [fc[:, c * S : (c + 1) * S] for c in range(FS // S)]
                rows[1:] = [
                    jnp.concatenate([jnp.concatenate(rows[1:], axis=0), jnp.zeros((8 - FS // S, S), F32)], axis=0)
                ]
                rows[1] = jnp.concatenate([rows[1], jnp.zeros((8, 3 * W - S), F32)], axis=1)
            else:
                rows += [jnp.zeros((8, 3 * W), F32)]
            o[S : S + 16] = jnp.concatenate(rows, axis=0).astype(o.dtype)
            block = columns(fc_part, ff ^ i)
            for c in range(3):
                o[S + 16 :, c * W : (c + 1) * W] = block[c * FR : (c + 1) * FR].astype(o.dtype)

    d_mid_lat, da_lat, *more = call(
        latent_back_body, "latent_backward",
        [
            ids, lengths, *lat_back, up, mid_lat, wo, vec, q_lat, ctx_lat, lse_lat, *qkvs,
            pos_blk, pos_col, th_row, th_col, dq, dkv, *kv_msgs, normed_y, normed_th, wq, scaled_y, sums1, sums2,
            dh_sum, dh_lat_sum, g_sum,
        ],
        [
            sds((NT, D), F32), sds((NT, D), BF16),
            sds((S + 16 + FR, 3 * W), F32), *[sds((S + 16 + FR, 3 * W), BF16)] * 3,
            sds((R, D), F32), sds((R, D), F32), sds((2 * R, D), BF16),
        ],
        scratch=[pltpu.VMEM((NQ, 3 * W), BF16), pltpu.VMEM((D, 3 * W), F32), pltpu.VMEM((8, D), F32)],
        n_smem=2,
    )
    gq, gn = more[:4], more[4:]
    gq = [gq[0]] + [flip(gq[i], i) for i in range(1, 4)]
    gn12 = flip_h(gn[2], 1)
    def tail_sum_body(g0, m1, m2, m3, gq_ref, fc_ref):
        rows = slice(0, S + 16)
        g = (g0[rows] + m1[rows].astype(F32)) + (m2[rows].astype(F32) + m3[rows].astype(F32))
        gq_ref[...] = g.astype(BF16)
        for i, m in enumerate((g0, m1, m2, m3)):
            for c in range(3):
                fc_ref[c * FR : (c + 1) * FR, i * S : (i + 1) * S] = m[S + 16 :, c * W : (c + 1) * W].astype(BF16)

    gq, piece_b = call(
        tail_sum_body, "tail_sum", gq, [sds((S + 16, 3 * W), BF16), sds((CR, 4 * S), BF16)], n_smem=0
    )
    gn3 = flip_h((gn[1] + barrier(gn12, gq)[0][R:].astype(F32)).astype(BF16), 3)
    if Q == 2:
        gq = (gq.astype(F32) + shift_q(gq, 1).astype(F32)).astype(BF16)
    else:
        every = jnp.roll(jnp.stack([gq] + [shift_q(gq, j) for j in range(1, Q)]), y, axis=0)
        gq = jnp.sum(every.astype(F32), axis=0).astype(BF16)
    gq3 = flip_h(gq, 3)
    gq12 = flip_h(jnp.concatenate([gq, gq3], axis=0), 1)
    piece_b = barrier(piece_b, gq)[0]
    every_b = gather_blk(piece_b) if CR % 16 == 0 else [lax.all_gather(piece_b, "blk", axis=0, tiled=True)]

    def final_body(n0, n3, n12, x_ref, dmid_ref, ownp_ref, thr_ref, dlat_ref, vec_ref, grad_ref):
        gn_now = (n0[...] + n3[...].astype(F32)) + n12[0:R].astype(F32)
        _, scaled, inverse = norm(x_ref[...].astype(F32), vec_ref[0:1, :], vec_ref[2:3, :])
        tgt = jnp.where(ownp_ref[...] == thr_ref[...], 1.0, 0.0)
        is_th = jnp.max(tgt, axis=1, keepdims=True) > 0
        src = jnp.where(ownp_ref[...] == thr_ref[...] - 1, 1.0, 0.0).astype(BF16)
        grad = jnp.where(is_th, 0.0, dmid_ref[...]) + norm_back(gn_now, scaled, inverse, vec_ref[0:1, :])
        grad_ref[...] = grad + spread(src, dlat_ref[...], 1)

    [grad_in] = call(
        final_body, "input_grad", [gn[0], gn3, gn12, own, d_mid, own_pos, th_row, d_mid_lat, vec], [sds((R, D), F32)], n_smem=0
    )

    da_lat_blocks = gather_f(barrier(da_lat, gq)[0])

    def place_blocks(ids_ref, refs, tmp):
        if len(refs) == 1:
            tmp[...] = refs[0][...]
            return
        for j in range(Q):
            for k in range(H):
                a = (ids_ref[0, 0] ^ k) * Q + lax.rem(ids_ref[0, 1] + j, Q)
                ref = refs[3 * j + (0, 2, 2, 1)[k]]
                block = ref[(k - 1) * CR : k * CR] if k in (1, 2) else ref[...]
                tmp[pl.ds(pl.multiple_of(a * CR, CR), CR), :] = block

    def a_grad_body(*refs):
        ids_ref, parts_a = refs[0], refs[1 : 1 + len(every_a)]
        act_ref, dm_ref, l0, m1, m2, m3, a0, a1, a2, a3, wp_ref, wo_ref, tmp = refs[1 + len(every_a) :]
        place_blocks(ids_ref, parts_a, tmp)
        wp_ref[...] = tmp[:, 0:D].astype(F32) + dot(act_ref[...], dm_ref[...], 0, 0)
        lats = [l0[...]]
        for m in (m1, m2, m3):
            lats.append(jnp.concatenate([m[R + S :, c * S : (c + 1) * S] for c in range(4)], axis=0))
        lat = [dot(l, a[...], 0, 0) for l, a in zip(lats, (a0, a1, a2, a3))]
        wo_ref[...] = tmp[:, D:].astype(F32).T + ((lat[0] + lat[1]) + (lat[2] + lat[3]))

    def b_grad_body(*refs):
        ids_ref, parts_b = refs[0], refs[1 : 1 + len(every_b)]
        second_ref, d0, d1, d2, d3, out_ref, tmp = refs[1 + len(every_b) :]
        ff = ids_ref[0, 2]
        place_blocks(ids_ref, parts_b, tmp)
        cols = columns(second_ref[...].astype(F32), ff).astype(BF16)
        for i, d in enumerate((d0, d1, d2, d3)):
            rows = jnp.concatenate([cols[(i ^ m) * NT : ((i ^ m) + 1) * NT] for m in range(4)], axis=0)
            block = tmp[:, i * S : (i + 1) * S].astype(F32).T + dot(rows, d[...], 0, 0)
            out_ref[:, pl.ds(pl.multiple_of((ff ^ i) * FS, 128), FS)] = block

    w_proj_g, w_out_g = call(
        a_grad_body, "proj_out_grad",
        [ids, *every_a, active_lat, dm_lat_all, lat_cols[0], *mix, *da_lat_blocks],
        [sds((FS, D), F32), sds((S, D), F32)],
        scratch=[pltpu.VMEM((FS, D + S), BF16)],
    )
    [w_fc_g] = call(
        b_grad_body, "fc_grad", [ids, *every_b, second_lat_all, *dh_lat_blocks], [sds((S, 4 * FS), F32)],
        scratch=[pltpu.VMEM((FS, 4 * S), BF16)],
    )

    def qkv_grad_body(
        ids_ref, g0, g3, g12, out_ref, gain_ref, shift_ref, qv_ref, ob_ref, fb_ref, pb_ref, tmp
    ):
        zz = ids_ref[0, 0]
        tmp[zz] = g0[...]
        tmp[zz ^ 3] = g3[...]
        tmp[zz ^ 1] = g12[0 : S + 16]
        tmp[zz ^ 2] = g12[S + 16 :]
        small = [tmp[c][S:, 0:S].astype(F32) for c in range(H)]
        small = (small[0] + small[2]) + (small[1] + small[3])
        for i, ref in enumerate((gain_ref, shift_ref, qv_ref)):
            ref[...] = small[2 * i : 2 * i + 2]
        ob_ref[...] = small[6]
        pb_ref[...] = small[7]
        for c in range(FS // S):
            fb_ref[c * S : (c + 1) * S] = small[8 + c]
        for c in range(H):
            for i in range(3):
                out_ref[:, i * D + c * W : i * D + (c + 1) * W] = tmp[c][0:S, i * W : (i + 1) * W].astype(F32)

    w_qkv_g, gain_g, shift_g, qv_g, ob_g, fb_g, pb_g = call(
        qkv_grad_body, "qkv_grad", [ids, gq, gq3, gq12],
        [sds((S, 3 * D), F32)] + [sds((2, S), F32)] * 3 + [sds((S,), F32), sds((FS,), F32), sds((S,), F32)],
        scratch=[pltpu.VMEM((H, S + 16, 3 * W), BF16)],
    )
    return (
        result[None],
        grad_in[None],
        gain_g,
        shift_g,
        w_qkv_g,
        qv_g,
        w_out_g,
        ob_g,
        w_fc_g,
        fb_g,
        w_proj_g,
        pb_g,
    )


def solution(mesh):
    a, r, v = P("fsdp", "blk", None), P("fsdp", None), P("fsdp")
    c = P(None, "fsdp")
    return jax.shard_map(
        local,
        mesh=mesh,
        in_specs=(a, r, r, r, c, c, r, c, r, v, r, v, r, v, a),
        out_specs=(a, a, c, c, r, c, r, v, r, v, r, v),
        check_vma=False,
    )
```

```python
import jax
import jax.numpy as jnp
from jax import lax
from jax.experimental import pallas as pl
from jax.experimental.pallas import tpu as pltpu
from jax.sharding import PartitionSpec as P

HDIM = 64
PARTS = 4
EPS = 1e-05
SCALE = HDIM ** (-0.5)
F32 = jnp.float32
BF16 = jnp.bfloat16
VMEM_BYTES = 60 * 1024 * 1024
INTERPRET = False


def dot(a, b, ca=1, cb=0):
    return lax.dot_general(a, b, (((ca,), (cb,)), ((), ())), preferred_element_type=F32)


def spread(hot, x, axis):
    total = None
    for _ in range(3):
        low = x.astype(BF16)
        x = x - low.astype(F32)
        part = dot(hot, low, axis, 0)
        total = part if total is None else total + part
    return total


def norm(x, gain, shift):
    center = x - jnp.mean(x, axis=-1, keepdims=True)
    inverse = lax.rsqrt(jnp.mean(center * center, axis=-1, keepdims=True) + EPS)
    scaled = center * inverse
    return (scaled * gain + shift).astype(BF16), scaled, inverse


def norm_back(up, scaled, inverse, gain):
    w = up * gain
    return inverse * (
        w - jnp.mean(w, axis=-1, keepdims=True) - scaled * jnp.mean(w * scaled, axis=-1, keepdims=True)
    )


C0 = 0.7978845608028654
C1 = 0.044715


def gelu(v):
    return 0.5 * v * (1.0 + jnp.tanh(C0 * (v + C1 * v * v * v)))


def gelu_back(v):
    t = jnp.tanh(C0 * (v + C1 * v * v * v))
    return 0.5 * (1.0 + t) + 0.5 * v * (1.0 - t * t) * C0 * (1.0 + 3 * C1 * v * v)


def start_of(p, len_ref):
    start = jnp.zeros_like(p)
    end = jnp.int32(0)
    for i in range(len_ref.shape[1] - 1):
        end = end + len_ref[0, i]
        start = jnp.where(p >= end, end, start)
    return start


def sds(shape, dtype):
    return jax.ShapeDtypeStruct(shape, dtype)


TIMES = {
    "pack": 2.0, "pack2": 2.5, "project": 4.1, "project_more": 3.5, "latent_attention": 4.6, "place": 3.8,
    "latent_out": 2.9, "latent_ffn": 3.8, "token_attention": 8.0, "token_out": 3.1, "ffn": 7.3, "ffn_grads": 5.6,
    "attention_gradient": 3.4, "out_grad": 3.2, "token_backward": 9.8, "out_sum": 2.9, "latent_ffn_backward": 3.9,
    "latent_grads": 3.1, "join": 2.0, "latent_backward": 9.6, "tail_sum": 2.3, "input_grad": 2.8, "proj_out_grad": 4.7, "fc_grad": 4.6,
    "qkv_grad": 3.1,
}
FLOPS_PER_US = 330_000_000


def call(body, name, args, outs, scratch=(), n_smem=1):
    vm = pl.BlockSpec(memory_space=pltpu.VMEM)
    sm = pl.BlockSpec(memory_space=pltpu.SMEM)
    return pl.pallas_call(
        body,
        name=name,
        out_shape=list(outs),
        in_specs=[sm] * n_smem + [vm] * (len(args) - n_smem),
        out_specs=[vm] * len(outs),
        scratch_shapes=list(scratch),
        cost_estimate=pl.CostEstimate(
            flops=int(TIMES.get(name, 2.0) * FLOPS_PER_US), bytes_accessed=0, transcendentals=0
        ),
        compiler_params=pltpu.CompilerParams(vmem_limit_bytes=VMEM_BYTES),
        interpret=INTERPRET,
    )(*args)


def local(
    tokens, slot_pos, lengths, thoughts, ln_gain, ln_shift, w_qkv, qv_bias, w_out, out_bias,
    w_fc, fc_bias, w_proj, proj_bias, cotangent,
):
    n_blk, n_f = lax.axis_size("blk"), lax.axis_size("fsdp")
    H = PARTS
    Q = n_blk // H
    b, f = lax.axis_index("blk"), lax.axis_index("fsdp")
    z, y = b // Q, b % Q
    R, D = tokens.shape[1], tokens.shape[2]
    T = R * n_blk
    W = D // H
    NH = W // HDIM
    S = D // n_f
    FS = w_proj.shape[0]
    NT = thoughts.shape[1]
    NQ = H * R
    KB = min(T, 256)

    def take(x, i, axis=0):
        return lax.dynamic_index_in_dim(x, i, axis, keepdims=False)

    def flip_h(x, k):
        return lax.ppermute(x, "blk", [((((c // Q) ^ k) * Q) + c % Q, c) for c in range(n_blk)])

    def shift_q(x, j):
        return lax.ppermute(x, "blk", [((c // Q) * Q + (c % Q + j) % Q, c) for c in range(n_blk)])

    def flip(x, bit):
        return lax.ppermute(x, "fsdp", [(c, c ^ bit) for c in range(n_f)])

    def gather_f(x):
        far = flip(x, 2)
        return [x, flip(x, 1), far, flip(far, 1)]

    def gather_h(x):
        return [x] + [flip_h(x, k) for k in range(1, H)]

    def barrier(*xs):
        return lax.optimization_barrier(xs)

    ids = jnp.stack([z, y, f, b]).astype(jnp.int32)[None]

    own = tokens[0]
    cot = cotangent[0]
    def pack_body(ids_ref, w_ref, gain_ref, shift_ref, qv_ref, ob_ref, pb_ref, out_ref):
        zz = ids_ref[0, 0]
        for c in range(H):

            @pl.when(zz == c)
            def _():
                for i in range(3):
                    out_ref[0:S, i * W : (i + 1) * W] = w_ref[:, i * D + c * W : i * D + (c + 1) * W]

        rows = [gain_ref[...].astype(F32), shift_ref[...].astype(F32), qv_ref[...].astype(F32)]
        rows += [ob_ref[...].astype(F32)[None, :], pb_ref[...].astype(F32)[None, :], jnp.zeros((8, S), F32)]
        rows = jnp.concatenate(rows, axis=0)
        rows = jnp.concatenate([rows, jnp.zeros((16, 3 * W - S), F32)], axis=1)
        out_ref[S : S + 16, :] = rows.astype(BF16)

    def pack2_body(ids_ref, fc_ref, wo_ref, far_ref, near_ref):
        ff = ids_ref[0, 2]

        def block(i):
            return fc_ref[:, pl.ds(pl.multiple_of((ff ^ i) * FS, 128), FS)]

        for ref in (far_ref, near_ref):
            ref[0:S] = wo_ref[...]
        far_ref[S : 2 * S] = block(3)
        far_ref[2 * S :] = block(2)
        near_ref[S:] = block(1)

    [part] = call(
        pack_body, "pack", [ids, w_qkv, ln_gain, ln_shift, qv_bias, out_bias, proj_bias],
        [sds((S + 16, 3 * W), BF16)])
    own1, own3 = flip_h(own, 1), flip_h(own, 3)
    own_y = [shift_q(own, j) for j in range(1, Q)]
    part, own1, own3 = barrier(part, own1, own3, own_y[0])[:3]
    own2 = flip_h(own3, 1)
    parts = gather_f(part)
    blocks = [[own, own1, own2, own3]]
    for j in range(1, Q):
        blocks.append([own_y[j - 1], shift_q(own1, j), shift_q(own2, j), shift_q(own3, j)])
    far0, near0 = call(
        pack2_body, "pack2", [ids, w_fc, w_out], [sds((3 * S, D), BF16), sds((2 * S, D), BF16)]
    )
    far0 = barrier(far0, parts[2], own2, blocks[1][1], blocks[1][3])[0]
    far_got = flip(far0, 2)

    pos = slot_pos
    pos_col = slot_pos.reshape(T, 1)
    pos_blk = slot_pos.reshape(n_blk, R)
    th_row = thoughts
    th_col = thoughts.reshape(NT, 1)

    def proj_body(ids_ref, p0, p1, p2, p3, x0, x1, x2, x3, qkv_ref, wq_ref, vec_ref, normed_ref, scaled_ref):
        zz, ff = ids_ref[0, 0], ids_ref[0, 2]
        smalls = []
        for i, p in enumerate((p0, p1, p2, p3)):
            wq_ref[pl.ds(pl.multiple_of((ff ^ i) * S, 64), S), :] = p[0:S, :]
            smalls.append(p[S : S + 16, 0:S].astype(F32)[0:8])
        for a in range(4):
            v = smalls[0]
            for i in range(1, 4):
                v = jnp.where((ff ^ i) == a, smalls[i], v)
            vec_ref[:, a * S : (a + 1) * S] = v
        bias = bias_of(vec_ref, zz)
        for k, x in enumerate((x0, x1, x2, x3)):
            n, scaled, _ = norm(x[...].astype(F32), vec_ref[0:1, :], vec_ref[2:3, :])
            normed_ref[k] = n
            scaled_ref[k] = scaled.astype(BF16)
            qkv_ref[k] = (dot(n, wq_ref[...]) + bias).astype(BF16)

    def bias_of(vec_ref, zz):
        qb = vec_ref[4:5, 0:W]
        vb = vec_ref[5:6, 0:W]
        for c in range(1, H):
            qb = jnp.where(zz == c, vec_ref[4:5, c * W : (c + 1) * W], qb)
            vb = jnp.where(zz == c, vec_ref[5:6, c * W : (c + 1) * W], vb)
        return jnp.concatenate([qb, jnp.zeros_like(qb), vb], axis=1)

    def proj_more(ids_ref, wq_ref, vec_ref, x0, x1, x2, x3, qkv_ref):
        bias = bias_of(vec_ref, ids_ref[0, 0])
        for k, x in enumerate((x0, x1, x2, x3)):
            n, _, _ = norm(x[...].astype(F32), vec_ref[0:1, :], vec_ref[2:3, :])
            qkv_ref[k] = (dot(n, wq_ref[...]) + bias).astype(BF16)

    qkv_y, wq, vec, normed_y, scaled_y = call(
        proj_body, "project", [ids, *parts, *blocks[0]],
        [sds((H, R, 3 * W), BF16), sds((D, 3 * W), BF16), sds((8, D), F32), sds((H, R, D), BF16), sds((H, R, D), BF16)],
    )
    qkvs = [qkv_y]
    for j in range(1, Q):
        qkvs += call(
            proj_more, "project_more", [ids, wq, vec, *blocks[j]], [sds((H, R, 3 * W), BF16)]
        )

    def attend(q, read_k, read_v, key_pos, q_pos, q_start, s_ref):
        n = q.shape[0]
        ctx, lse = [], []
        for h in range(NH):
            lanes = slice(h * HDIM, (h + 1) * HDIM)
            qh = q[:, lanes]

            def score(i, m):
                at = pl.multiple_of(i * KB, KB)
                s = dot(read_k(at, lanes), qh, 1, 1) * SCALE
                kp = key_pos(at)
                s = jnp.where((kp <= q_pos) & (kp >= q_start), s, -1e30)
                s_ref[pl.ds(at, KB), 0:n] = s
                return jnp.maximum(m, jnp.max(s, axis=0, keepdims=True))

            m = lax.fori_loop(0, T // KB, score, jnp.full((1, n), -1e30, F32), unroll=T // KB <= 4)

            def add(i, carry):
                total, acc = carry
                at = pl.multiple_of(i * KB, KB)
                e = jnp.exp(s_ref[pl.ds(at, KB), 0:n] - m)
                total = total + jnp.sum(e, axis=0, keepdims=True)
                return total, acc + dot(read_v(at, lanes), e.astype(BF16), 0, 0)

            total, acc = lax.fori_loop(
                0, T // KB, add, (jnp.zeros((1, n), F32), jnp.zeros((HDIM, n), F32)), unroll=T // KB <= 4
            )
            ctx.append(acc / total)
            lse.append(m + jnp.log(total))
        return jnp.concatenate(ctx, axis=0), jnp.concatenate(lse, axis=0)

    def latent_body(*refs):
        ids_ref, len_ref, pos_ref, posb_ref, posc_ref, thr_ref, thc_ref = refs[:7]
        qkv_refs = refs[7 : 7 + Q]
        x_refs = refs[7 + Q : 7 + Q + n_blk]
        low_ref, ctx_ref, lse_ref, q_ref, x_ref, abs_ref, s_ref = refs[7 + Q + n_blk :]
        zz, yy = ids_ref[0, 0], ids_ref[0, 1]
        src = thc_ref[...] - 1
        x_lat = jnp.zeros((NT, D), F32)
        for j in range(Q):
            for k in range(H):
                a = (zz ^ k) * Q + lax.rem(yy + j, Q)
                abs_ref[pl.ds(pl.multiple_of(a * R, R), R), :] = qkv_refs[j][k]
                hot = jnp.where(posb_ref[pl.ds(a, 1), :] == src, 1.0, 0.0).astype(BF16)
                x_lat = x_lat + dot(hot, x_refs[j * H + k][...])
        x_ref[...] = x_lat
        hot = jnp.where(pos_ref[...] == src, 1.0, 0.0).astype(BF16)
        q = dot(hot, abs_ref[:, 0:W]).astype(BF16)
        q_ref[...] = q
        p = thr_ref[...] - 1
        ctx, lse = attend(
            q,
            lambda at, c: abs_ref[pl.ds(at, KB), W + c.start : W + c.stop],
            lambda at, c: abs_ref[pl.ds(at, KB), 2 * W + c.start : 2 * W + c.stop],
            lambda at: posc_ref[pl.ds(at, KB), :],
            p,
            start_of(p, len_ref),
            s_ref,
        )
        ctx_ref[...] = ctx
        lse_ref[...] = lse
        low_ref[...] = ctx.T.astype(BF16)

    flat = [x for group in blocks for x in group]
    ctx_lat_low, ctx_lat, lse_lat, q_lat, x_lat, qkv_abs = call(
        latent_body, "latent_attention",
        [ids, lengths, pos, pos_blk, pos_col, th_row, th_col, *qkvs, *flat],
        [
            sds((NT, W), BF16), sds((W, NT), F32), sds((NH, NT), F32), sds((NT, W), BF16),
            sds((NT, D), F32), sds((T, 3 * W), BF16),
        ],
        scratch=[pltpu.VMEM((T, 128), F32)],
        n_smem=2,
    )
    ctx_lat_blocks = gather_h(ctx_lat_low)

    far_got, near0 = barrier(far_got, near0, ctx_lat_low)[:2]
    near_got = flip(near0, 1)
    both_got = flip(far_got, 1)

    def place_body(ids_ref, far0_ref, far_ref, near_ref, both_ref, fc_ref, wo_ref, wf_ref):
        ff = ids_ref[0, 2]

        def at(i):
            return pl.ds(pl.multiple_of((ff ^ i) * S, 64), S)

        for i, ref in enumerate((far0_ref, near_ref, far_ref, both_ref)):
            wo_ref[at(i), :] = ref[0:S]
        wf_ref[at(0), :] = fc_ref[:, pl.ds(pl.multiple_of(ff * FS, 128), FS)]
        wf_ref[at(1), :] = near_ref[S:]
        wf_ref[at(2), :] = far_ref[2 * S :]
        wf_ref[at(3), :] = both_ref[S : 2 * S]

    wo, wf = call(
        place_body, "place", [ids, far0, far_got, near_got, both_got, w_fc], [sds((D, D), BF16), sds((D, FS), BF16)]
    )
    fb = fc_bias[None]

    def columns(x, i):
        v = x[:, 0:S]
        for c in range(1, 4):
            v = jnp.where(i == c, x[:, c * S : (c + 1) * S], v)
        return v

    def latent_out_body(ids_ref, c0, c1, c2, c3, x_ref, wo_ref, vec_ref, mid_ref, low_ref, l0, l1, l2, l3, all_ref, tmp):
        zz, ff = ids_ref[0, 0], ids_ref[0, 2]
        for k, c in enumerate((c0, c1, c2, c3)):
            tmp[zz ^ k] = c[...]
        for i in range(H):
            all_ref[:, i * W : (i + 1) * W] = tmp[i]
        mid = x_ref[...] + (dot(all_ref[...], wo_ref[...]) + vec_ref[6:7, :])
        mid_ref[...] = mid
        low_ref[...] = norm(mid, vec_ref[1:2, :], vec_ref[3:4, :])[0]
        both = all_ref[...].astype(F32)
        for i, o in enumerate((l0, l1, l2, l3)):
            o[...] = columns(both, ff ^ i).astype(BF16)

    mid_lat, second_lat, *lat_cols = call(
        latent_out_body, "latent_out", [ids, *ctx_lat_blocks, x_lat, wo, vec],
        [sds((NT, D), F32), sds((NT, D), BF16)] + [sds((NT, S), BF16)] * 4,
        scratch=[pltpu.VMEM((NT, D), BF16), pltpu.VMEM((H, NT, W), BF16)],
    )
    second_lat_blocks = gather_f(second_lat)

    def latent_ffn_body(s0, s1, s2, s3, wf_ref, wp_ref, fb_ref, hid_ref, act_ref, all_ref, o0, o1, o2, o3):
        for i, s in enumerate((s0, s1, s2, s3)):
            all_ref[i * NT : (i + 1) * NT] = s[...]
        hidden = dot(all_ref[...], wf_ref[...]) + fb_ref[...].astype(F32)
        hid_ref[...] = hidden
        act_ref[...] = gelu(hidden).astype(BF16)
        out = dot(act_ref[...], wp_ref[...])
        for i, o in enumerate((o0, o1, o2, o3)):
            o[...] = out[i * NT : (i + 1) * NT].astype(o.dtype)

    hidden_lat, active_lat, second_lat_all, *outs = call(
        latent_ffn_body, "latent_ffn", [*second_lat_blocks, wf, w_proj, fb],
        [sds((4 * NT, FS), F32), sds((4 * NT, FS), BF16), sds((4 * NT, D), BF16), sds((NT, D), F32)]
        + [sds((NT, D), BF16)] * 3,
        n_smem=0,
    )
    outs = [outs[0]] + [flip(outs[i], i) for i in range(1, 4)]
    dm_blocks = gather_f(barrier(cot, outs[2], outs[3])[0])

    def token_body(
        ids_ref, len_ref, o0, o1, o2, o3, mid_ref, vec_ref, wq_ref, abs_ref, qy_ref, posb_ref, posc_ref, thr_ref,
        lat_ref, nth_ref, kv_ref, q_ref, ctx_ref, lse_ref, c0, c1, c2, c3, s_ref,
    ):
        zz, yy = ids_ref[0, 0], ids_ref[0, 1]
        lat = mid_ref[...] + (
            (o0[...] + o1[...].astype(F32) + (o2[...].astype(F32) + o3[...].astype(F32))) + vec_ref[7:8, :]
        )
        lat_ref[...] = lat
        nth = norm(lat, vec_ref[0:1, :], vec_ref[2:3, :])[0]
        nth_ref[...] = nth
        qkv_th = (dot(nth, wq_ref[...]) + bias_of(vec_ref, zz)).astype(BF16)

        def fill(i, _):
            at = pl.multiple_of(i * KB, KB)
            hot = posc_ref[pl.ds(at, KB), :] == thr_ref[...]
            is_th = jnp.max(jnp.where(hot, 1.0, 0.0), axis=1, keepdims=True) > 0
            new = dot(jnp.where(hot, 1.0, 0.0).astype(BF16), qkv_th[:, W:])
            kv_ref[pl.ds(at, KB), :] = jnp.where(is_th, new, abs_ref[pl.ds(at, KB), W:].astype(F32)).astype(BF16)
            return 0

        lax.fori_loop(0, T // KB, fill, 0, unroll=T // KB <= 4)
        rows = []
        for k in range(H):
            a = (zz ^ k) * Q + yy
            hot = posc_ref[pl.ds(pl.multiple_of(a * R, R), R), :] == thr_ref[...]
            is_th = jnp.max(jnp.where(hot, 1.0, 0.0), axis=1, keepdims=True) > 0
            new = dot(jnp.where(hot, 1.0, 0.0).astype(BF16), qkv_th[:, 0:W])
            q_ref[k] = jnp.where(is_th, new, qy_ref[k][:, 0:W].astype(F32)).astype(BF16)
            rows.append(posb_ref[pl.ds(a, 1), :])
        p = jnp.concatenate(rows, axis=1)
        ctx, lse = attend(
            q_ref[...].reshape(NQ, W),
            lambda at, c: kv_ref[pl.ds(at, KB), c],
            lambda at, c: kv_ref[pl.ds(at, KB), W + c.start : W + c.stop],
            lambda at: posc_ref[pl.ds(at, KB), :],
            p,
            start_of(p, len_ref),
            s_ref,
        )
        ctx_ref[...] = ctx
        lse_ref[...] = lse
        low = ctx.T.astype(BF16)
        for k, c in enumerate((c0, c1, c2, c3)):
            c[...] = low[k * R : (k + 1) * R]

    lat_out, normed_th, kv_tok, q_tok, ctx_t, lse, *ctx_blocks = call(
        token_body, "token_attention",
        [ids, lengths, *outs, mid_lat, vec, wq, qkv_abs, qkv_y, pos_blk, pos_col, th_row],
        [
            sds((NT, D), F32), sds((NT, D), BF16), sds((T, 2 * W), BF16), sds((H, R, W), BF16),
            sds((W, NQ), F32), sds((NH, NQ), F32),
        ]
        + [sds((R, W), BF16)] * 4,
        scratch=[pltpu.VMEM((T, NQ), F32)],
        n_smem=2,
    )
    ctx_blocks = [ctx_blocks[0]] + [flip_h(ctx_blocks[k], k) for k in range(1, H)]
    own_pos = lax.dynamic_slice_in_dim(pos_col, b * R, R, axis=0)

    def token_out_body(
        ids_ref, c0, c1, c2, c3, x_ref, posc_ref, thr_ref, lat_ref, wo_ref, vec_ref, mid_ref, low_ref, all_ref, tmp
    ):
        zz = ids_ref[0, 0]
        for k, c in enumerate((c0, c1, c2, c3)):
            tmp[zz ^ k] = c[...]
        for i in range(H):
            all_ref[:, i * W : (i + 1) * W] = tmp[i]
        hot = jnp.where(posc_ref[...] == thr_ref[...], 1.0, 0.0)
        is_th = jnp.max(hot, axis=1, keepdims=True) > 0
        x = jnp.where(is_th, spread(hot.astype(BF16), lat_ref[...], 1), x_ref[...].astype(F32))
        mid = x + (dot(all_ref[...], wo_ref[...]) + vec_ref[6:7, :])
        mid_ref[...] = mid
        low_ref[...] = norm(mid, vec_ref[1:2, :], vec_ref[3:4, :])[0]

    mid, second, ctx_own = call(
        token_out_body, "token_out", [ids, *ctx_blocks, own, own_pos, th_row, lat_out, wo, vec],
        [sds((R, D), F32), sds((R, D), BF16), sds((R, D), BF16)],
        scratch=[pltpu.VMEM((H, R, W), BF16)],
    )
    second_blocks = gather_f(second)

    def ffn_body(s0, s1, s2, s3, d0, d1, d2, d3, wf_ref, wp_ref, fb_ref, act_ref, dh_ref, all_ref, dm_ref, sum_ref, o0, o1, o2, o3):
        for i, (s, d, o) in enumerate(zip((s0, s1, s2, s3), (d0, d1, d2, d3), (o0, o1, o2, o3))):
            rows = slice(i * R, (i + 1) * R)
            all_ref[rows] = s[...]
            dm_ref[rows] = d[...]
            hidden = dot(s[...], wf_ref[...]) + fb_ref[...].astype(F32)
            t = jnp.tanh(C0 * (hidden + C1 * hidden * hidden * hidden))
            act_ref[rows] = (0.5 * hidden * (1.0 + t)).astype(BF16)
            back = 0.5 * (1.0 + t) + 0.5 * hidden * (1.0 - t * t) * C0 * (1.0 + 3 * C1 * hidden * hidden)
            dh = (dot(d[...], wp_ref[...], 1, 1) * back).astype(BF16)
            dh_ref[rows] = dh
            o[...] = dot(dh, wf_ref[...], 1, 1).astype(o.dtype)
        sum_ref[...] = jnp.sum(dh_ref[...].astype(F32), axis=0, keepdims=True)

    active, dh, second_all, dm_all, dh_sum, *back = call(
        ffn_body, "ffn", [*second_blocks, *dm_blocks, wf, w_proj, fb],
        [sds((4 * R, FS), BF16), sds((4 * R, FS), BF16), sds((4 * R, D), BF16), sds((4 * R, D), BF16), sds((1, FS), F32), sds((R, D), F32)]
        + [sds((R, D), BF16)] * 3,
        n_smem=0,
    )
    back = [back[0]] + [flip(back[i], i) for i in range(1, 4)]

    def grads_body(act_ref, dh_ref, all_ref, dm_ref, wp_ref, g_ref, o0, o1, o2, o3):
        out = dot(act_ref[...], wp_ref[...])
        for i, o in enumerate((o0, o1, o2, o3)):
            o[...] = out[i * R : (i + 1) * R].astype(o.dtype)
        g_ref[:, 0:D] = dot(act_ref[...], dm_ref[...], 0, 0).astype(BF16)
        g_ref[:, D:] = dot(dh_ref[...], all_ref[...], 0, 0).astype(BF16)

    g_ffn, *res = call(
        grads_body, "ffn_grads", [active, dh, second_all, dm_all, w_proj],
        [sds((FS, 2 * D), BF16), sds((R, D), F32)] + [sds((R, D), BF16)] * 3,
        n_smem=0,
    )
    g_ffn_later = barrier(g_ffn, back[2], back[3])[0]
    g_sum = lax.psum_scatter(g_ffn_later, "blk", scatter_dimension=0, tiled=True)
    back[0] = barrier(back[0], g_ffn)[0]

    def attn_in_body(ids_ref, b0, b1, b2, b3, mid_ref, cot_ref, wo_ref, vec_ref, dmid_ref, da_ref, sum_ref, c0, c1, c2, c3):
        zz = ids_ref[0, 0]
        up = (b0[...] + b1[...].astype(F32)) + (b2[...].astype(F32) + b3[...].astype(F32))
        _, scaled, inverse = norm(mid_ref[...], vec_ref[1:2, :], vec_ref[3:4, :])
        cot_now = cot_ref[...].astype(F32)
        d_mid = cot_now + norm_back(up, scaled, inverse, vec_ref[1:2, :])
        dmid_ref[...] = d_mid
        da = d_mid.astype(BF16)
        da_ref[...] = da
        for k, c in enumerate((c0, c1, c2, c3)):
            w = wo_ref[pl.ds(pl.multiple_of((zz ^ k) * W, 64), W), :]
            c[...] = dot(da, w, 1, 1).astype(BF16)
        sum_ref[0:1] = jnp.sum(up * scaled, axis=0, keepdims=True)
        sum_ref[1:2] = jnp.sum(up, axis=0, keepdims=True)
        sum_ref[2:3] = jnp.sum(da.astype(F32), axis=0, keepdims=True)
        sum_ref[3:4] = jnp.sum(cot_now, axis=0, keepdims=True)

    d_mid, da, sums2, *grad_blocks = call(
        attn_in_body, "attention_gradient", [ids, *back, mid, cot, wo, vec],
        [sds((R, D), F32), sds((R, D), BF16), sds((4, D), F32)] + [sds((R, W), BF16)] * 4,
    )
    grad_blocks = [grad_blocks[0]] + [flip_h(grad_blocks[k], k) for k in range(1, H)]

    def out_grad_body(ids_ref, ctx_ref, da_ref, r1, r2, r3, l1, l2, l3, o0, o1, o2, o3, tmp):
        ff = ids_ref[0, 2]
        tmp[...] = dot(ctx_ref[...], da_ref[...], 0, 0)
        own_rows = pl.ds(pl.multiple_of(ff * S, 64), S)
        o0[...] = tmp[own_rows, :]
        for i, (r, l, o) in enumerate(((r1, l1, o1), (r2, l2, o2), (r3, l3, o3)), 1):
            o[0:R] = r[...]
            o[R : R + S] = tmp[pl.ds(pl.multiple_of((ff ^ i) * S, 64), S), :].astype(BF16)
            for c in range(4):
                o[R + S :, c * S : (c + 1) * S] = l[c * NT // 4 : (c + 1) * NT // 4, :]

    g_out, *mix = call(
        out_grad_body, "out_grad", [ids, ctx_own, da, *res[1:], *lat_cols[1:]],
        [sds((S, D), F32)] + [sds((R + S + NT // 4, D), BF16)] * 3,
        scratch=[pltpu.VMEM((D, D), F32)],
    )
    grad_blocks[0] = barrier(grad_blocks[0], g_out)[0]
    mix = list(barrier(*mix, *grad_blocks[1:])[:3])
    mix = [flip(mix[i - 1], i) for i in range(1, 4)]

    def attend_back(q, g, read_k, read_v, key_pos, q_pos, q_start, lse, ctx, n_keys, put):
        n = q.shape[0]
        g_t = g.astype(F32).T
        dqs = []
        deltas = [
            jnp.sum(g_t[h * HDIM : (h + 1) * HDIM] * ctx[h * HDIM : (h + 1) * HDIM], axis=0, keepdims=True)
            for h in range(NH)
        ]

        def step(i, dq):
            at = pl.multiple_of(i * KB, KB)
            kp = key_pos(at)
            mask = (kp <= q_pos) & (kp >= q_start)
            dks, dvs, new = [], [], []
            for h in range(NH):
                lanes = slice(h * HDIM, (h + 1) * HDIM)
                kh = read_k(at, lanes)
                s = dot(kh, q[:, lanes], 1, 1) * SCALE
                p = jnp.where(mask, jnp.exp(s - lse[h : h + 1]), 0.0)
                dp = dot(read_v(at, lanes), g[:, lanes], 1, 1)
                ds = (p * (dp - deltas[h])).astype(BF16)
                new.append(dq[h] + dot(kh, ds, 0, 0))
                dks.append(dot(ds, q[:, lanes]) * SCALE)
                dvs.append(dot(p.astype(BF16), g[:, lanes]))
            put(at, jnp.concatenate(dks, axis=1), jnp.concatenate(dvs, axis=1))
            return tuple(new)

        dq = lax.fori_loop(
            0, n_keys // KB, step, tuple(jnp.zeros((HDIM, n), F32) for _ in range(NH)), unroll=n_keys // KB <= 4
        )
        return jnp.concatenate(dq, axis=0).T * SCALE

    def token_back_body(
        ids_ref, len_ref, g0, g1, g2, g3, q_ref, kv_ref, ctx_ref, lse_ref, pos_ref, posb_ref, posc_ref, thr_ref, thc_ref,
        ownp_ref, wq_ref, lat_ref, vec_ref, dmid_ref,
        up_ref, dq_ref, dkv_ref, sum_ref, *rest,
    ):
        msgs, acc = rest[:-1], rest[-1]
        zz, yy = ids_ref[0, 0], ids_ref[0, 1]
        rows = [posb_ref[pl.ds((zz ^ k) * Q + yy, 1), :] for k in range(H)]
        p = jnp.concatenate(rows, axis=1)

        def put(at, dk, dv):
            acc[pl.ds(at, KB), 0:W] = dk
            acc[pl.ds(at, KB), W:] = dv

        dq = attend_back(
            q_ref[...].reshape(NQ, W),
            jnp.concatenate([g0[...], g1[...], g2[...], g3[...]], axis=0),
            lambda at, c: kv_ref[pl.ds(at, KB), c],
            lambda at, c: kv_ref[pl.ds(at, KB), W + c.start : W + c.stop],
            lambda at: posc_ref[pl.ds(at, KB), :],
            p,
            start_of(p, len_ref),
            lse_ref[...],
            ctx_ref[...],
            T,
            put,
        ).astype(BF16)
        hot_y = jnp.where(p == thc_ref[...], 1.0, 0.0).astype(BF16)
        hot = jnp.where(pos_ref[...] == thc_ref[...], 1.0, 0.0).astype(BF16)
        d_q = dot(hot_y, dq).astype(BF16)
        d_kv = dot(hot, acc[...].astype(BF16)).astype(BF16)
        gn = dot(d_q, wq_ref[:, 0:W], 1, 1) + dot(d_kv, wq_ref[:, W:], 1, 1)
        _, scaled, inverse = norm(lat_ref[...], vec_ref[0:1, :], vec_ref[2:3, :])
        sum_ref[0:1] = jnp.sum(gn * scaled, axis=0, keepdims=True)
        sum_ref[1:2] = jnp.sum(gn, axis=0, keepdims=True)
        hot_own = jnp.where(ownp_ref[...] == thr_ref[...], 1.0, 0.0).astype(BF16)
        up = norm_back(gn, scaled, inverse, vec_ref[0:1, :]) + spread(hot_own, dmid_ref[...], 0)
        up_ref[...] = up.astype(BF16)
        for k in range(H):
            dq_ref[k] = dq[k * R : (k + 1) * R]
            for j in range(Q):
                a = (zz ^ k) * Q + lax.rem(yy - j + Q, Q)
                block = acc[pl.ds(pl.multiple_of(a * R, R), R), :]
                if j == 0:
                    dkv_ref[k] = block
                else:
                    msgs[j - 1][k] = block.astype(BF16)

    up, dq, dkv, sums1, *kv_msgs = call(
        token_back_body, "token_backward",
        [
            ids, lengths, *grad_blocks, q_tok, kv_tok, ctx_t, lse, pos, pos_blk, pos_col, th_row, th_col,
            own_pos, wq, lat_out, vec, d_mid,
        ],
        [sds((NT, D), BF16), sds((H, R, W), BF16), sds((H, R, 2 * W), F32), sds((2, D), F32)]
        + [sds((H, R, 2 * W), BF16)] * (Q - 1),
        scratch=[pltpu.VMEM((T, 2 * W), F32)],
        n_smem=2,
    )
    if Q == 2:
        up = (up.astype(F32) + shift_q(up, 1).astype(F32)).astype(BF16)
    else:
        ups = jnp.roll(jnp.stack([up] + [shift_q(up, j) for j in range(1, Q)]), y, axis=0)
        up = jnp.sum(ups.astype(F32), axis=0).astype(BF16)
    ups = [x.astype(F32) for x in gather_h(up)]
    up = (ups[0] + ups[2]) + (ups[1] + ups[3])
    kv_msgs = list(barrier(*kv_msgs, up)[:-1])
    kv_msgs = [shift_q(kv_msgs[j - 1], j) for j in range(1, Q)]

    dm_lat = up.astype(BF16)
    dm_lat_blocks = gather_f(dm_lat)

    def latent_ffn_back_body(d0, d1, d2, d3, hid_ref, wf_ref, wp_ref, all_ref, dh_ref, sum_ref, o0, o1, o2, o3):
        for i, d in enumerate((d0, d1, d2, d3)):
            all_ref[i * NT : (i + 1) * NT] = d[...]
        dh = (dot(all_ref[...], wp_ref[...], 1, 1) * gelu_back(hid_ref[...])).astype(BF16)
        dh_ref[...] = dh
        out = dot(dh, wf_ref[...], 1, 1)
        for i, o in enumerate((o0, o1, o2, o3)):
            o[...] = out[i * NT : (i + 1) * NT].astype(o.dtype)
        sum_ref[...] = jnp.sum(dh.astype(F32), axis=0, keepdims=True)

    CR = FS // n_blk
    FR = CR // 3

    def out_sum_body(g0, m1, m2, m3, mid_ref, vec_ref, r0, out_ref, g_ref):
        rows = slice(R, R + S)
        g = (g0[...] + m1[rows].astype(F32)) + (m2[rows].astype(F32) + m3[rows].astype(F32))
        g_ref[...] = g.T.astype(BF16)
        out = (r0[...] + m1[0:R].astype(F32)) + (m2[0:R].astype(F32) + m3[0:R].astype(F32))
        out_ref[...] = (mid_ref[...] + (out + vec_ref[7:8, :])).astype(BF16)

    mix_now = barrier(*mix, ups[2])[:3]
    result, g_out = call(
        out_sum_body, "out_sum", [g_out, *mix_now, mid, vec, res[0]], [sds((R, D), BF16), sds((D, S), BF16)], n_smem=0
    )
    g_out = g_out.reshape(H, Q, CR, S)
    got = [shift_q(take(g_out, (y - j) % Q, 1), j).astype(F32) for j in range(1, Q)]
    g_out = take(g_out, y, 1).astype(F32)
    for t in got:
        g_out = g_out + t
    g_out = g_out.astype(BF16)
    dm_lat_blocks[0], g_out = barrier(dm_lat_blocks[0], g_out)
    g_out = [take(g_out, z)] + [flip_h(take(g_out, z ^ k), k) for k in range(1, H)]

    dm_lat_all, dh_lat, dh_lat_sum, *lat_back = call(
        latent_ffn_back_body, "latent_ffn_backward", [*dm_lat_blocks, hidden_lat, wf, w_proj],
        [sds((4 * NT, D), BF16), sds((4 * NT, FS), BF16), sds((1, FS), F32), sds((NT, D), F32)]
        + [sds((NT, D), BF16)] * 3,
        n_smem=0,
    )
    lat_back = [lat_back[0]] + [flip(lat_back[i], i) for i in range(1, 4)]
    def latent_grads_body(ids_ref, act_ref, dm_ref, dh_ref, second_ref, out_ref, tmp):
        rows = pl.ds(pl.multiple_of(ids_ref[0, 3] * CR, CR), CR)
        tmp[...] = dot(act_ref[...], dm_ref[...], 0, 0)
        out_ref[:, 0:D] = tmp[rows, :]
        tmp[...] = dot(dh_ref[...], second_ref[...], 0, 0)
        out_ref[:, D:] = tmp[rows, :]

    if CR % 16 == 0:
        [lat_part] = call(
            latent_grads_body, "latent_grads", [ids, active_lat, dm_lat_all, dh_lat, second_lat_all],
            [sds((CR, 2 * D), F32)], scratch=[pltpu.VMEM((FS, D), F32)],
        )
    else:
        lat_part = jnp.concatenate([dot(active_lat, dm_lat_all, 0, 0), dot(dh_lat, second_lat_all, 0, 0)], axis=1)
        lat_part = lax.dynamic_slice_in_dim(lat_part, b * CR, CR, axis=0)

    def join_body(g_ref, lat_ref, c0, c1, c2, c3, out_ref, fc_ref):
        out_ref[:, 0:D] = (g_ref[:, 0:D].astype(F32) + lat_ref[:, 0:D]).astype(BF16)
        fc_ref[...] = (g_ref[:, D:].astype(F32) + lat_ref[:, D:]).astype(BF16)
        c = (c0[...].astype(F32) + c2[...].astype(F32)) + (c1[...].astype(F32) + c3[...].astype(F32))
        out_ref[:, D:] = c.astype(BF16)

    def gather_blk(x):
        x3 = flip_h(x, 3)
        x12 = flip_h(jnp.concatenate([x, x3], axis=0), 1)
        got = [x, x3, x12]
        for j in range(1, Q):
            got += [shift_q(t, j) for t in (x, x3, x12)]
        return got

    g_sum = barrier(g_sum, lat_back[2], lat_back[3], lat_part)[0]
    piece_a, fc_sum = call(
        join_body, "join", [g_sum, lat_part, *g_out], [sds((CR, D + S), BF16), sds((CR, D), BF16)], n_smem=0
    )
    lat_back[0] = barrier(lat_back[0], piece_a)[0]
    every_a = gather_blk(piece_a) if CR % 16 == 0 else [lax.all_gather(piece_a, "blk", axis=0, tiled=True)]

    def latent_back_body(*refs):
        ids_ref, len_ref, b0, b1, b2, b3, up_ref, mid_ref, wo_ref, vec_ref, q_ref, ctx_ref, lse_ref = refs[:13]
        qkv_refs = refs[13 : 13 + Q]
        posb_ref, posc_ref, thr_ref, thc_ref, dq_ref, dkv_ref = refs[13 + Q : 19 + Q]
        msgs = refs[19 + Q : 18 + 2 * Q]
        normed_ref, nth_ref, wq_ref, scaled_ref, s1_ref, s2_ref, dh1_ref, dh2_ref, gsum_ref = refs[18 + 2 * Q : 27 + 2 * Q]
        dmid_ref, da_ref, o0, o1, o2, o3, n0, n3, n12, tmp, acc, small_ref = refs[27 + 2 * Q :]
        once = jnp.where(ids_ref[0, 3] == 0, 1.0, 0.0)
        zz, yy, ff = ids_ref[0, 0], ids_ref[0, 1], ids_ref[0, 2]
        back = (b0[...] + b1[...].astype(F32)) + (b2[...].astype(F32) + b3[...].astype(F32))
        _, scaled, inverse = norm(mid_ref[...], vec_ref[1:2, :], vec_ref[3:4, :])
        d_mid = up_ref[...] + norm_back(back, scaled, inverse, vec_ref[1:2, :])
        dmid_ref[...] = d_mid
        da = d_mid.astype(BF16)
        da_ref[...] = da
        col = lambda t: jnp.sum(t, axis=0, keepdims=True)
        small_ref[1:2] = s2_ref[0:1] + once * col(back * scaled)
        small_ref[3:4] = s2_ref[1:2] + once * col(back)
        small_ref[6:7] = s2_ref[2:3] + once * col(da.astype(F32))
        small_ref[7:8] = s2_ref[3:4] + once * col(up_ref[...].astype(BF16).astype(F32))
        g = dot(da, wo_ref[pl.ds(pl.multiple_of(zz * W, 64), W), :], 1, 1).astype(BF16)
        q = q_ref[...]
        p_row = thr_ref[...] - 1
        start = start_of(p_row, len_ref)
        lse = lse_ref[...]
        g_t = g.astype(F32).T
        deltas = [
            jnp.sum(g_t[h * HDIM : (h + 1) * HDIM] * ctx_ref[h * HDIM : (h + 1) * HDIM], axis=0, keepdims=True)
            for h in range(NH)
        ]
        dq_t = [jnp.zeros((HDIM, NT), F32) for _ in range(NH)]
        for j in range(Q):
            kps = [posc_ref[pl.ds(pl.multiple_of(((zz ^ k) * Q + lax.rem(yy + j, Q)) * R, R), R), :] for k in range(H)]
            kp = jnp.concatenate(kps, axis=0)
            mask = (kp <= p_row) & (kp >= start)
            dks, dvs = [], []
            for h in range(NH):
                c = slice(h * HDIM, (h + 1) * HDIM)
                kh = qkv_refs[j][:, :, W + c.start : W + c.stop].reshape(NQ, HDIM)
                vh = qkv_refs[j][:, :, 2 * W + c.start : 2 * W + c.stop].reshape(NQ, HDIM)
                s = dot(kh, q[:, c], 1, 1) * SCALE
                p = jnp.where(mask, jnp.exp(s - lse[h : h + 1]), 0.0)
                dp = dot(vh, g[:, c], 1, 1)
                ds = (p * (dp - deltas[h])).astype(BF16)
                dq_t[h] = dq_t[h] + dot(kh, ds, 0, 0)
                if j == 0:
                    dks.append(dot(ds, q[:, c]) * SCALE)
                    dvs.append(dot(p.astype(BF16), g[:, c]))
            if j == 0:
                acc[0:NQ, W : 2 * W] = jnp.concatenate(dks, axis=1)
                acc[0:NQ, 2 * W :] = jnp.concatenate(dvs, axis=1)
        dq_l = (jnp.concatenate(dq_t, axis=0).T * SCALE).astype(BF16)
        th_grad = jnp.zeros((NT, 3 * W), F32)
        bias = jnp.zeros((1, 3 * W), F32)
        for k in range(H):
            a = (zz ^ k) * Q + yy
            rows = slice(k * R, (k + 1) * R)
            kp = posc_ref[pl.ds(pl.multiple_of(a * R, R), R), :]
            src = jnp.where(kp == thr_ref[...] - 1, 1.0, 0.0).astype(BF16)
            tgt = jnp.where(kp == thr_ref[...], 1.0, 0.0)
            is_th = jnp.max(tgt, axis=1, keepdims=True) > 0
            kv = dkv_ref[k]
            for m in msgs:
                kv = kv + m[k].astype(F32)
            tok = jnp.concatenate([dq_ref[k].astype(F32), kv], axis=1)
            lat = jnp.concatenate([dot(src, dq_l), acc[rows, W:]], axis=1)
            both = (jnp.where(is_th, 0.0, tok) + lat).astype(BF16)
            hot = jnp.where(posb_ref[pl.ds(a, 1), :] == thc_ref[...], 1.0, 0.0).astype(BF16)
            th_grad = th_grad + dot(hot, tok.astype(BF16))
            tmp[rows] = both
        th_low = th_grad.astype(BF16)
        both = tmp[...]
        bias = col(both.astype(F32)) + col(th_low.astype(F32))
        for c in range(H):
            mine = jnp.where(zz == c, 1.0, 0.0)
            small_ref[4:5, c * W : (c + 1) * W] = bias[:, 0:W] * mine
            small_ref[5:6, c * W : (c + 1) * W] = bias[:, 2 * W :] * mine
        gain, shift = s1_ref[0:1], s1_ref[1:2]
        for k in range(H):
            gn = dot(tmp[k * R : (k + 1) * R], wq_ref[...], 1, 1)
            gain = gain + col(gn * scaled_ref[k].astype(F32))
            shift = shift + col(gn)
            if k in (0, 3):
                (n0, n3)[k // 3][...] = gn
            else:
                n12[(k - 1) * R : k * R] = gn.astype(BF16)
        small_ref[0:1] = gain
        small_ref[2:3] = shift
        acc[...] = dot(normed_ref[...].reshape(NQ, D), both, 0, 0) + dot(nth_ref[...], th_low, 0, 0)
        fc = dh1_ref[...] + once * dh2_ref[...]
        fc_part = gsum_ref[...].astype(F32)
        smalls = small_ref[...]
        for i, o in enumerate((o0, o1, o2, o3)):
            o[0:S] = acc[pl.ds(pl.multiple_of((ff ^ i) * S, 64), S), :].astype(o.dtype)
            rows = [jnp.concatenate([columns(smalls, ff ^ i), jnp.zeros((8, 3 * W - S), F32)], axis=1)]
            if i == 0:
                rows += [fc[:, c * S : (c + 1) * S] for c in range(FS // S)]
                rows[1:] = [
                    jnp.concatenate([jnp.concatenate(rows[1:], axis=0), jnp.zeros((8 - FS // S, S), F32)], axis=0)
                ]
                rows[1] = jnp.concatenate([rows[1], jnp.zeros((8, 3 * W - S), F32)], axis=1)
            else:
                rows += [jnp.zeros((8, 3 * W), F32)]
            o[S : S + 16] = jnp.concatenate(rows, axis=0).astype(o.dtype)
            block = columns(fc_part, ff ^ i)
            for c in range(3):
                o[S + 16 :, c * W : (c + 1) * W] = block[c * FR : (c + 1) * FR].astype(o.dtype)

    d_mid_lat, da_lat, *more = call(
        latent_back_body, "latent_backward",
        [
            ids, lengths, *lat_back, up, mid_lat, wo, vec, q_lat, ctx_lat, lse_lat, *qkvs,
            pos_blk, pos_col, th_row, th_col, dq, dkv, *kv_msgs, normed_y, normed_th, wq, scaled_y, sums1, sums2,
            dh_sum, dh_lat_sum, fc_sum,
        ],
        [
            sds((NT, D), F32), sds((NT, D), BF16),
            sds((S + 16 + FR, 3 * W), F32), *[sds((S + 16 + FR, 3 * W), BF16)] * 3,
            sds((R, D), F32), sds((R, D), F32), sds((2 * R, D), BF16),
        ],
        scratch=[pltpu.VMEM((NQ, 3 * W), BF16), pltpu.VMEM((D, 3 * W), F32), pltpu.VMEM((8, D), F32)],
        n_smem=2,
    )
    gq, gn = more[:4], more[4:]
    gq = [gq[0]] + [flip(gq[i], i) for i in range(1, 4)]
    gn12 = flip_h(gn[2], 1)
    def tail_sum_body(g0, m1, m2, m3, gq_ref, fc_ref):
        rows = slice(0, S + 16)
        g = (g0[rows] + m1[rows].astype(F32)) + (m2[rows].astype(F32) + m3[rows].astype(F32))
        gq_ref[...] = g.astype(BF16)
        for i, m in enumerate((g0, m1, m2, m3)):
            for c in range(3):
                fc_ref[c * FR : (c + 1) * FR, i * S : (i + 1) * S] = m[S + 16 :, c * W : (c + 1) * W].astype(BF16)

    gq, piece_b = call(
        tail_sum_body, "tail_sum", gq, [sds((S + 16, 3 * W), BF16), sds((CR, 4 * S), BF16)], n_smem=0
    )
    gn3 = flip_h((gn[1] + barrier(gn12, gq)[0][R:].astype(F32)).astype(BF16), 3)
    if Q == 2:
        gq = (gq.astype(F32) + shift_q(gq, 1).astype(F32)).astype(BF16)
    else:
        every = jnp.roll(jnp.stack([gq] + [shift_q(gq, j) for j in range(1, Q)]), y, axis=0)
        gq = jnp.sum(every.astype(F32), axis=0).astype(BF16)
    gq = barrier(gq, gn3)[0]
    gq3 = flip_h(gq, 3)
    gq12 = flip_h(jnp.concatenate([gq, gq3], axis=0), 1)
    piece_b = barrier(piece_b, gq)[0]
    every_b = gather_blk(piece_b) if CR % 16 == 0 else [lax.all_gather(piece_b, "blk", axis=0, tiled=True)]

    def final_body(n0, n3, n12, x_ref, dmid_ref, ownp_ref, thr_ref, dlat_ref, vec_ref, grad_ref):
        gn_now = (n0[...] + n3[...].astype(F32)) + n12[0:R].astype(F32)
        _, scaled, inverse = norm(x_ref[...].astype(F32), vec_ref[0:1, :], vec_ref[2:3, :])
        tgt = jnp.where(ownp_ref[...] == thr_ref[...], 1.0, 0.0)
        is_th = jnp.max(tgt, axis=1, keepdims=True) > 0
        src = jnp.where(ownp_ref[...] == thr_ref[...] - 1, 1.0, 0.0).astype(BF16)
        grad = jnp.where(is_th, 0.0, dmid_ref[...]) + norm_back(gn_now, scaled, inverse, vec_ref[0:1, :])
        grad_ref[...] = grad + spread(src, dlat_ref[...], 1)

    [grad_in] = call(
        final_body, "input_grad", [gn[0], gn3, gn12, own, d_mid, own_pos, th_row, d_mid_lat, vec], [sds((R, D), F32)], n_smem=0
    )

    da_lat_blocks = gather_f(barrier(da_lat, gq)[0])

    def place_blocks(ids_ref, refs, tmp):
        if len(refs) == 1:
            tmp[...] = refs[0][...]
            return
        for j in range(Q):
            for k in range(H):
                a = (ids_ref[0, 0] ^ k) * Q + lax.rem(ids_ref[0, 1] + j, Q)
                ref = refs[3 * j + (0, 2, 2, 1)[k]]
                block = ref[(k - 1) * CR : k * CR] if k in (1, 2) else ref[...]
                tmp[pl.ds(pl.multiple_of(a * CR, CR), CR), :] = block

    def a_grad_body(*refs):
        ids_ref, parts_a = refs[0], refs[1 : 1 + len(every_a)]
        l0, m1, m2, m3, a0, a1, a2, a3, wp_ref, wo_ref, tmp = refs[1 + len(every_a) :]
        place_blocks(ids_ref, parts_a, tmp)
        wp_ref[...] = tmp[:, 0:D].astype(F32)
        lats = [l0[...]]
        for m in (m1, m2, m3):
            lats.append(jnp.concatenate([m[R + S :, c * S : (c + 1) * S] for c in range(4)], axis=0))
        lat = [dot(l, a[...], 0, 0) for l, a in zip(lats, (a0, a1, a2, a3))]
        wo_ref[...] = tmp[:, D:].astype(F32).T + ((lat[0] + lat[1]) + (lat[2] + lat[3]))

    def b_grad_body(*refs):
        ids_ref, parts_b = refs[0], refs[1 : 1 + len(every_b)]
        out_ref, tmp = refs[1 + len(every_b) :]
        ff = ids_ref[0, 2]
        place_blocks(ids_ref, parts_b, tmp)
        for i in range(4):
            block = tmp[:, i * S : (i + 1) * S].astype(F32).T
            out_ref[:, pl.ds(pl.multiple_of((ff ^ i) * FS, 128), FS)] = block

    w_proj_g, w_out_g = call(
        a_grad_body, "proj_out_grad",
        [ids, *every_a, lat_cols[0], *mix, *da_lat_blocks],
        [sds((FS, D), F32), sds((S, D), F32)],
        scratch=[pltpu.VMEM((FS, D + S), BF16)],
    )
    [w_fc_g] = call(
        b_grad_body, "fc_grad", [ids, *every_b], [sds((S, 4 * FS), F32)],
        scratch=[pltpu.VMEM((FS, 4 * S), BF16)],
    )

    def qkv_grad_body(
        ids_ref, g0, g3, g12, out_ref, gain_ref, shift_ref, qv_ref, ob_ref, fb_ref, pb_ref, tmp
    ):
        zz = ids_ref[0, 0]
        tmp[zz] = g0[...]
        tmp[zz ^ 3] = g3[...]
        tmp[zz ^ 1] = g12[0 : S + 16]
        tmp[zz ^ 2] = g12[S + 16 :]
        small = [tmp[c][S:, 0:S].astype(F32) for c in range(H)]
        small = (small[0] + small[2]) + (small[1] + small[3])
        for i, ref in enumerate((gain_ref, shift_ref, qv_ref)):
            ref[...] = small[2 * i : 2 * i + 2]
        ob_ref[...] = small[6]
        pb_ref[...] = small[7]
        for c in range(FS // S):
            fb_ref[c * S : (c + 1) * S] = small[8 + c]
        for c in range(H):
            for i in range(3):
                out_ref[:, i * D + c * W : i * D + (c + 1) * W] = tmp[c][0:S, i * W : (i + 1) * W].astype(F32)

    w_qkv_g, gain_g, shift_g, qv_g, ob_g, fb_g, pb_g = call(
        qkv_grad_body, "qkv_grad", [ids, gq, gq3, gq12],
        [sds((S, 3 * D), F32)] + [sds((2, S), F32)] * 3 + [sds((S,), F32), sds((FS,), F32), sds((S,), F32)],
        scratch=[pltpu.VMEM((H, S + 16, 3 * W), BF16)],
    )
    return (
        result[None],
        grad_in[None],
        gain_g,
        shift_g,
        w_qkv_g,
        qv_g,
        w_out_g,
        ob_g,
        w_fc_g,
        fb_g,
        w_proj_g,
        pb_g,
    )


def solution(mesh):
    a, r, v = P("fsdp", "blk", None), P("fsdp", None), P("fsdp")
    c = P(None, "fsdp")
    return jax.shard_map(
        local,
        mesh=mesh,
        in_specs=(a, r, r, r, c, c, r, c, r, v, r, v, r, v, a),
        out_specs=(a, a, c, c, r, c, r, v, r, v, r, v),
        check_vma=False,
    )
```

```python
import jax
import jax.numpy as jnp
from jax import lax
from jax.experimental import pallas as pl
from jax.experimental.pallas import tpu as pltpu
from jax.sharding import PartitionSpec as P

HDIM = 64
PARTS = 4
EPS = 1e-05
SCALE = HDIM ** (-0.5)
F32 = jnp.float32
BF16 = jnp.bfloat16
VMEM_BYTES = 60 * 1024 * 1024
INTERPRET = False


def dot(a, b, ca=1, cb=0):
    return lax.dot_general(a, b, (((ca,), (cb,)), ((), ())), preferred_element_type=F32)


def spread(hot, x, axis):
    total = None
    for _ in range(3):
        low = x.astype(BF16)
        x = x - low.astype(F32)
        part = dot(hot, low, axis, 0)
        total = part if total is None else total + part
    return total


def norm(x, gain, shift):
    center = x - jnp.mean(x, axis=-1, keepdims=True)
    inverse = lax.rsqrt(jnp.mean(center * center, axis=-1, keepdims=True) + EPS)
    scaled = center * inverse
    return (scaled * gain + shift).astype(BF16), scaled, inverse


def norm_back(up, scaled, inverse, gain):
    w = up * gain
    return inverse * (
        w - jnp.mean(w, axis=-1, keepdims=True) - scaled * jnp.mean(w * scaled, axis=-1, keepdims=True)
    )


C0 = 0.7978845608028654
C1 = 0.044715


def gelu(v):
    return 0.5 * v * (1.0 + jnp.tanh(C0 * (v + C1 * v * v * v)))


def gelu_back(v):
    t = jnp.tanh(C0 * (v + C1 * v * v * v))
    return 0.5 * (1.0 + t) + 0.5 * v * (1.0 - t * t) * C0 * (1.0 + 3 * C1 * v * v)


def start_of(p, len_ref):
    start = jnp.zeros_like(p)
    end = jnp.int32(0)
    for i in range(len_ref.shape[1] - 1):
        end = end + len_ref[0, i]
        start = jnp.where(p >= end, end, start)
    return start


def sds(shape, dtype):
    return jax.ShapeDtypeStruct(shape, dtype)


TIMES = {
    "pack": 2.0, "pack2": 2.5, "project": 4.1, "project_more": 3.5, "latent_attention": 4.6, "place": 3.8,
    "latent_out": 2.9, "latent_ffn": 3.8, "token_attention": 8.0, "token_out": 3.1, "ffn": 7.3, "ffn_grads": 5.6,
    "attention_gradient": 3.4, "out_grad": 3.2, "token_backward": 9.8, "out_sum": 2.9, "latent_ffn_backward": 3.9,
    "latent_grads": 3.1, "join": 2.0, "latent_backward": 9.6, "tail_sum": 2.3, "input_grad": 2.8, "proj_out_grad": 4.7, "fc_grad": 4.6,
    "qkv_grad": 3.1,
}
FLOPS_PER_US = 550_000_000


def call(body, name, args, outs, scratch=(), n_smem=1):
    vm = pl.BlockSpec(memory_space=pltpu.VMEM)
    sm = pl.BlockSpec(memory_space=pltpu.SMEM)
    return pl.pallas_call(
        body,
        name=name,
        out_shape=list(outs),
        in_specs=[sm] * n_smem + [vm] * (len(args) - n_smem),
        out_specs=[vm] * len(outs),
        scratch_shapes=list(scratch),
        cost_estimate=pl.CostEstimate(
            flops=int(TIMES.get(name, 2.0) * FLOPS_PER_US), bytes_accessed=0, transcendentals=0
        ),
        compiler_params=pltpu.CompilerParams(vmem_limit_bytes=VMEM_BYTES),
        interpret=INTERPRET,
    )(*args)


def local(
    tokens, slot_pos, lengths, thoughts, ln_gain, ln_shift, w_qkv, qv_bias, w_out, out_bias,
    w_fc, fc_bias, w_proj, proj_bias, cotangent,
):
    n_blk, n_f = lax.axis_size("blk"), lax.axis_size("fsdp")
    H = PARTS
    Q = n_blk // H
    b, f = lax.axis_index("blk"), lax.axis_index("fsdp")
    z, y = b // Q, b % Q
    R, D = tokens.shape[1], tokens.shape[2]
    T = R * n_blk
    W = D // H
    NH = W // HDIM
    S = D // n_f
    FS = w_proj.shape[0]
    NT = thoughts.shape[1]
    NQ = H * R
    KB = min(T, 256)

    def take(x, i, axis=0):
        return lax.dynamic_index_in_dim(x, i, axis, keepdims=False)

    def flip_h(x, k):
        return lax.ppermute(x, "blk", [((((c // Q) ^ k) * Q) + c % Q, c) for c in range(n_blk)])

    def shift_q(x, j):
        return lax.ppermute(x, "blk", [((c // Q) * Q + (c % Q + j) % Q, c) for c in range(n_blk)])

    def flip(x, bit):
        return lax.ppermute(x, "fsdp", [(c, c ^ bit) for c in range(n_f)])

    def gather_f(x):
        far = flip(x, 2)
        return [x, flip(x, 1), far, flip(far, 1)]

    def gather_h(x):
        return [x] + [flip_h(x, k) for k in range(1, H)]

    def barrier(*xs):
        return lax.optimization_barrier(xs)

    ids = jnp.stack([z, y, f, b]).astype(jnp.int32)[None]

    own = tokens[0]
    cot = cotangent[0]
    def pack_body(ids_ref, w_ref, gain_ref, shift_ref, qv_ref, ob_ref, pb_ref, out_ref):
        zz = ids_ref[0, 0]
        for c in range(H):

            @pl.when(zz == c)
            def _():
                for i in range(3):
                    out_ref[0:S, i * W : (i + 1) * W] = w_ref[:, i * D + c * W : i * D + (c + 1) * W]

        rows = [gain_ref[...].astype(F32), shift_ref[...].astype(F32), qv_ref[...].astype(F32)]
        rows += [ob_ref[...].astype(F32)[None, :], pb_ref[...].astype(F32)[None, :], jnp.zeros((8, S), F32)]
        rows = jnp.concatenate(rows, axis=0)
        rows = jnp.concatenate([rows, jnp.zeros((16, 3 * W - S), F32)], axis=1)
        out_ref[S : S + 16, :] = rows.astype(BF16)

    def pack2_body(ids_ref, fc_ref, wo_ref, far_ref, near_ref):
        ff = ids_ref[0, 2]

        def block(i):
            return fc_ref[:, pl.ds(pl.multiple_of((ff ^ i) * FS, 128), FS)]

        for ref in (far_ref, near_ref):
            ref[0:S] = wo_ref[...]
        far_ref[S : 2 * S] = block(3)
        far_ref[2 * S :] = block(2)
        near_ref[S:] = block(1)

    [part] = call(
        pack_body, "pack", [ids, w_qkv, ln_gain, ln_shift, qv_bias, out_bias, proj_bias],
        [sds((S + 16, 3 * W), BF16)])
    own1, own3 = flip_h(own, 1), flip_h(own, 3)
    own_y = [shift_q(own, j) for j in range(1, Q)]
    part, own1, own3 = barrier(part, own1, own3, own_y[0])[:3]
    own2 = flip_h(own3, 1)
    parts = gather_f(part)
    blocks = [[own, own1, own2, own3]]
    for j in range(1, Q):
        blocks.append([own_y[j - 1], shift_q(own1, j), shift_q(own2, j), shift_q(own3, j)])
    far0, near0 = call(
        pack2_body, "pack2", [ids, w_fc, w_out], [sds((3 * S, D), BF16), sds((2 * S, D), BF16)]
    )
    far0 = barrier(far0, parts[2], own2, blocks[1][1], blocks[1][3])[0]
    far_got = flip(far0, 2)

    pos = slot_pos
    pos_col = slot_pos.reshape(T, 1)
    pos_blk = slot_pos.reshape(n_blk, R)
    th_row = thoughts
    th_col = thoughts.reshape(NT, 1)

    def proj_body(ids_ref, p0, p1, p2, p3, x0, x1, x2, x3, qkv_ref, wq_ref, vec_ref, normed_ref, scaled_ref):
        zz, ff = ids_ref[0, 0], ids_ref[0, 2]
        smalls = []
        for i, p in enumerate((p0, p1, p2, p3)):
            wq_ref[pl.ds(pl.multiple_of((ff ^ i) * S, 64), S), :] = p[0:S, :]
            smalls.append(p[S : S + 16, 0:S].astype(F32)[0:8])
        for a in range(4):
            v = smalls[0]
            for i in range(1, 4):
                v = jnp.where((ff ^ i) == a, smalls[i], v)
            vec_ref[:, a * S : (a + 1) * S] = v
        bias = bias_of(vec_ref, zz)
        for k, x in enumerate((x0, x1, x2, x3)):
            n, scaled, _ = norm(x[...].astype(F32), vec_ref[0:1, :], vec_ref[2:3, :])
            normed_ref[k] = n
            scaled_ref[k] = scaled.astype(BF16)
            qkv_ref[k] = (dot(n, wq_ref[...]) + bias).astype(BF16)

    def bias_of(vec_ref, zz):
        qb = vec_ref[4:5, 0:W]
        vb = vec_ref[5:6, 0:W]
        for c in range(1, H):
            qb = jnp.where(zz == c, vec_ref[4:5, c * W : (c + 1) * W], qb)
            vb = jnp.where(zz == c, vec_ref[5:6, c * W : (c + 1) * W], vb)
        return jnp.concatenate([qb, jnp.zeros_like(qb), vb], axis=1)

    def proj_more(ids_ref, wq_ref, vec_ref, x0, x1, x2, x3, qkv_ref):
        bias = bias_of(vec_ref, ids_ref[0, 0])
        for k, x in enumerate((x0, x1, x2, x3)):
            n, _, _ = norm(x[...].astype(F32), vec_ref[0:1, :], vec_ref[2:3, :])
            qkv_ref[k] = (dot(n, wq_ref[...]) + bias).astype(BF16)

    qkv_y, wq, vec, normed_y, scaled_y = call(
        proj_body, "project", [ids, *parts, *blocks[0]],
        [sds((H, R, 3 * W), BF16), sds((D, 3 * W), BF16), sds((8, D), F32), sds((H, R, D), BF16), sds((H, R, D), BF16)],
    )
    qkvs = [qkv_y]
    for j in range(1, Q):
        qkvs += call(
            proj_more, "project_more", [ids, wq, vec, *blocks[j]], [sds((H, R, 3 * W), BF16)]
        )

    def attend(q, read_k, read_v, key_pos, q_pos, q_start, s_ref):
        n = q.shape[0]
        ctx, lse = [], []
        for h in range(NH):
            lanes = slice(h * HDIM, (h + 1) * HDIM)
            qh = q[:, lanes]

            def score(i, m):
                at = pl.multiple_of(i * KB, KB)
                s = dot(read_k(at, lanes), qh, 1, 1) * SCALE
                kp = key_pos(at)
                s = jnp.where((kp <= q_pos) & (kp >= q_start), s, -1e30)
                s_ref[pl.ds(at, KB), 0:n] = s
                return jnp.maximum(m, jnp.max(s, axis=0, keepdims=True))

            m = lax.fori_loop(0, T // KB, score, jnp.full((1, n), -1e30, F32), unroll=T // KB <= 4)

            def add(i, carry):
                total, acc = carry
                at = pl.multiple_of(i * KB, KB)
                e = jnp.exp(s_ref[pl.ds(at, KB), 0:n] - m)
                total = total + jnp.sum(e, axis=0, keepdims=True)
                return total, acc + dot(read_v(at, lanes), e.astype(BF16), 0, 0)

            total, acc = lax.fori_loop(
                0, T // KB, add, (jnp.zeros((1, n), F32), jnp.zeros((HDIM, n), F32)), unroll=T // KB <= 4
            )
            ctx.append(acc / total)
            lse.append(m + jnp.log(total))
        return jnp.concatenate(ctx, axis=0), jnp.concatenate(lse, axis=0)

    def latent_body(*refs):
        ids_ref, len_ref, pos_ref, posb_ref, posc_ref, thr_ref, thc_ref = refs[:7]
        qkv_refs = refs[7 : 7 + Q]
        x_refs = refs[7 + Q : 7 + Q + n_blk]
        low_ref, ctx_ref, lse_ref, q_ref, x_ref, abs_ref, s_ref = refs[7 + Q + n_blk :]
        zz, yy = ids_ref[0, 0], ids_ref[0, 1]
        src = thc_ref[...] - 1
        x_lat = jnp.zeros((NT, D), F32)
        for j in range(Q):
            for k in range(H):
                a = (zz ^ k) * Q + lax.rem(yy + j, Q)
                abs_ref[pl.ds(pl.multiple_of(a * R, R), R), :] = qkv_refs[j][k]
                hot = jnp.where(posb_ref[pl.ds(a, 1), :] == src, 1.0, 0.0).astype(BF16)
                x_lat = x_lat + dot(hot, x_refs[j * H + k][...])
        x_ref[...] = x_lat
        hot = jnp.where(pos_ref[...] == src, 1.0, 0.0).astype(BF16)
        q = dot(hot, abs_ref[:, 0:W]).astype(BF16)
        q_ref[...] = q
        p = thr_ref[...] - 1
        ctx, lse = attend(
            q,
            lambda at, c: abs_ref[pl.ds(at, KB), W + c.start : W + c.stop],
            lambda at, c: abs_ref[pl.ds(at, KB), 2 * W + c.start : 2 * W + c.stop],
            lambda at: posc_ref[pl.ds(at, KB), :],
            p,
            start_of(p, len_ref),
            s_ref,
        )
        ctx_ref[...] = ctx
        lse_ref[...] = lse
        low_ref[...] = ctx.T.astype(BF16)

    flat = [x for group in blocks for x in group]
    ctx_lat_low, ctx_lat, lse_lat, q_lat, x_lat, qkv_abs = call(
        latent_body, "latent_attention",
        [ids, lengths, pos, pos_blk, pos_col, th_row, th_col, *qkvs, *flat],
        [
            sds((NT, W), BF16), sds((W, NT), F32), sds((NH, NT), F32), sds((NT, W), BF16),
            sds((NT, D), F32), sds((T, 3 * W), BF16),
        ],
        scratch=[pltpu.VMEM((T, 128), F32)],
        n_smem=2,
    )
    ctx_lat_blocks = gather_h(ctx_lat_low)

    far_got, near0 = barrier(far_got, near0, ctx_lat_low)[:2]
    near_got = flip(near0, 1)
    both_got = flip(far_got, 1)

    def place_body(ids_ref, far0_ref, far_ref, near_ref, both_ref, fc_ref, wo_ref, wf_ref):
        ff = ids_ref[0, 2]

        def at(i):
            return pl.ds(pl.multiple_of((ff ^ i) * S, 64), S)

        for i, ref in enumerate((far0_ref, near_ref, far_ref, both_ref)):
            wo_ref[at(i), :] = ref[0:S]
        wf_ref[at(0), :] = fc_ref[:, pl.ds(pl.multiple_of(ff * FS, 128), FS)]
        wf_ref[at(1), :] = near_ref[S:]
        wf_ref[at(2), :] = far_ref[2 * S :]
        wf_ref[at(3), :] = both_ref[S : 2 * S]

    wo, wf = call(
        place_body, "place", [ids, far0, far_got, near_got, both_got, w_fc], [sds((D, D), BF16), sds((D, FS), BF16)]
    )
    fb = fc_bias[None]

    def columns(x, i):
        v = x[:, 0:S]
        for c in range(1, 4):
            v = jnp.where(i == c, x[:, c * S : (c + 1) * S], v)
        return v

    def latent_out_body(ids_ref, c0, c1, c2, c3, x_ref, wo_ref, vec_ref, mid_ref, low_ref, l0, l1, l2, l3, all_ref, tmp):
        zz, ff = ids_ref[0, 0], ids_ref[0, 2]
        for k, c in enumerate((c0, c1, c2, c3)):
            tmp[zz ^ k] = c[...]
        for i in range(H):
            all_ref[:, i * W : (i + 1) * W] = tmp[i]
        mid = x_ref[...] + (dot(all_ref[...], wo_ref[...]) + vec_ref[6:7, :])
        mid_ref[...] = mid
        low_ref[...] = norm(mid, vec_ref[1:2, :], vec_ref[3:4, :])[0]
        both = all_ref[...].astype(F32)
        for i, o in enumerate((l0, l1, l2, l3)):
            o[...] = columns(both, ff ^ i).astype(BF16)

    mid_lat, second_lat, *lat_cols = call(
        latent_out_body, "latent_out", [ids, *ctx_lat_blocks, x_lat, wo, vec],
        [sds((NT, D), F32), sds((NT, D), BF16)] + [sds((NT, S), BF16)] * 4,
        scratch=[pltpu.VMEM((NT, D), BF16), pltpu.VMEM((H, NT, W), BF16)],
    )
    second_lat_blocks = gather_f(second_lat)

    def latent_ffn_body(s0, s1, s2, s3, wf_ref, wp_ref, fb_ref, hid_ref, act_ref, all_ref, o0, o1, o2, o3):
        for i, s in enumerate((s0, s1, s2, s3)):
            all_ref[i * NT : (i + 1) * NT] = s[...]
        hidden = dot(all_ref[...], wf_ref[...]) + fb_ref[...].astype(F32)
        hid_ref[...] = hidden
        act_ref[...] = gelu(hidden).astype(BF16)
        out = dot(act_ref[...], wp_ref[...])
        for i, o in enumerate((o0, o1, o2, o3)):
            o[...] = out[i * NT : (i + 1) * NT].astype(o.dtype)

    hidden_lat, active_lat, second_lat_all, *outs = call(
        latent_ffn_body, "latent_ffn", [*second_lat_blocks, wf, w_proj, fb],
        [sds((4 * NT, FS), F32), sds((4 * NT, FS), BF16), sds((4 * NT, D), BF16), sds((NT, D), F32)]
        + [sds((NT, D), BF16)] * 3,
        n_smem=0,
    )
    outs = [outs[0]] + [flip(outs[i], i) for i in range(1, 4)]
    dm_blocks = gather_f(barrier(cot, outs[2], outs[3])[0])

    def token_body(
        ids_ref, len_ref, o0, o1, o2, o3, mid_ref, vec_ref, wq_ref, abs_ref, qy_ref, posb_ref, posc_ref, thr_ref,
        lat_ref, nth_ref, kv_ref, q_ref, ctx_ref, lse_ref, c0, c1, c2, c3, s_ref,
    ):
        zz, yy = ids_ref[0, 0], ids_ref[0, 1]
        lat = mid_ref[...] + (
            (o0[...] + o1[...].astype(F32) + (o2[...].astype(F32) + o3[...].astype(F32))) + vec_ref[7:8, :]
        )
        lat_ref[...] = lat
        nth = norm(lat, vec_ref[0:1, :], vec_ref[2:3, :])[0]
        nth_ref[...] = nth
        qkv_th = (dot(nth, wq_ref[...]) + bias_of(vec_ref, zz)).astype(BF16)

        def fill(i, _):
            at = pl.multiple_of(i * KB, KB)
            hot = posc_ref[pl.ds(at, KB), :] == thr_ref[...]
            is_th = jnp.max(jnp.where(hot, 1.0, 0.0), axis=1, keepdims=True) > 0
            new = dot(jnp.where(hot, 1.0, 0.0).astype(BF16), qkv_th[:, W:])
            kv_ref[pl.ds(at, KB), :] = jnp.where(is_th, new, abs_ref[pl.ds(at, KB), W:].astype(F32)).astype(BF16)
            return 0

        lax.fori_loop(0, T // KB, fill, 0, unroll=T // KB <= 4)
        rows = []
        for k in range(H):
            a = (zz ^ k) * Q + yy
            hot = posc_ref[pl.ds(pl.multiple_of(a * R, R), R), :] == thr_ref[...]
            is_th = jnp.max(jnp.where(hot, 1.0, 0.0), axis=1, keepdims=True) > 0
            new = dot(jnp.where(hot, 1.0, 0.0).astype(BF16), qkv_th[:, 0:W])
            q_ref[k] = jnp.where(is_th, new, qy_ref[k][:, 0:W].astype(F32)).astype(BF16)
            rows.append(posb_ref[pl.ds(a, 1), :])
        p = jnp.concatenate(rows, axis=1)
        ctx, lse = attend(
            q_ref[...].reshape(NQ, W),
            lambda at, c: kv_ref[pl.ds(at, KB), c],
            lambda at, c: kv_ref[pl.ds(at, KB), W + c.start : W + c.stop],
            lambda at: posc_ref[pl.ds(at, KB), :],
            p,
            start_of(p, len_ref),
            s_ref,
        )
        ctx_ref[...] = ctx
        lse_ref[...] = lse
        low = ctx.T.astype(BF16)
        for k, c in enumerate((c0, c1, c2, c3)):
            c[...] = low[k * R : (k + 1) * R]

    lat_out, normed_th, kv_tok, q_tok, ctx_t, lse, *ctx_blocks = call(
        token_body, "token_attention",
        [ids, lengths, *outs, mid_lat, vec, wq, qkv_abs, qkv_y, pos_blk, pos_col, th_row],
        [
            sds((NT, D), F32), sds((NT, D), BF16), sds((T, 2 * W), BF16), sds((H, R, W), BF16),
            sds((W, NQ), F32), sds((NH, NQ), F32),
        ]
        + [sds((R, W), BF16)] * 4,
        scratch=[pltpu.VMEM((T, NQ), F32)],
        n_smem=2,
    )
    ctx_blocks = [ctx_blocks[0]] + [flip_h(ctx_blocks[k], k) for k in range(1, H)]
    own_pos = lax.dynamic_slice_in_dim(pos_col, b * R, R, axis=0)

    def token_out_body(
        ids_ref, c0, c1, c2, c3, x_ref, posc_ref, thr_ref, lat_ref, wo_ref, vec_ref, mid_ref, low_ref, all_ref, tmp
    ):
        zz = ids_ref[0, 0]
        for k, c in enumerate((c0, c1, c2, c3)):
            tmp[zz ^ k] = c[...]
        for i in range(H):
            all_ref[:, i * W : (i + 1) * W] = tmp[i]
        hot = jnp.where(posc_ref[...] == thr_ref[...], 1.0, 0.0)
        is_th = jnp.max(hot, axis=1, keepdims=True) > 0
        x = jnp.where(is_th, spread(hot.astype(BF16), lat_ref[...], 1), x_ref[...].astype(F32))
        mid = x + (dot(all_ref[...], wo_ref[...]) + vec_ref[6:7, :])
        mid_ref[...] = mid
        low_ref[...] = norm(mid, vec_ref[1:2, :], vec_ref[3:4, :])[0]

    mid, second, ctx_own = call(
        token_out_body, "token_out", [ids, *ctx_blocks, own, own_pos, th_row, lat_out, wo, vec],
        [sds((R, D), F32), sds((R, D), BF16), sds((R, D), BF16)],
        scratch=[pltpu.VMEM((H, R, W), BF16)],
    )
    second_blocks = gather_f(second)

    def ffn_body(s0, s1, s2, s3, d0, d1, d2, d3, wf_ref, wp_ref, fb_ref, act_ref, dh_ref, all_ref, dm_ref, sum_ref, o0, o1, o2, o3):
        for i, (s, d, o) in enumerate(zip((s0, s1, s2, s3), (d0, d1, d2, d3), (o0, o1, o2, o3))):
            rows = slice(i * R, (i + 1) * R)
            all_ref[rows] = s[...]
            dm_ref[rows] = d[...]
            hidden = dot(s[...], wf_ref[...]) + fb_ref[...].astype(F32)
            t = jnp.tanh(C0 * (hidden + C1 * hidden * hidden * hidden))
            act_ref[rows] = (0.5 * hidden * (1.0 + t)).astype(BF16)
            back = 0.5 * (1.0 + t) + 0.5 * hidden * (1.0 - t * t) * C0 * (1.0 + 3 * C1 * hidden * hidden)
            dh = (dot(d[...], wp_ref[...], 1, 1) * back).astype(BF16)
            dh_ref[rows] = dh
            o[...] = dot(dh, wf_ref[...], 1, 1).astype(o.dtype)
        sum_ref[...] = jnp.sum(dh_ref[...].astype(F32), axis=0, keepdims=True)

    active, dh, second_all, dm_all, dh_sum, *back = call(
        ffn_body, "ffn", [*second_blocks, *dm_blocks, wf, w_proj, fb],
        [sds((4 * R, FS), BF16), sds((4 * R, FS), BF16), sds((4 * R, D), BF16), sds((4 * R, D), BF16), sds((1, FS), F32), sds((R, D), F32)]
        + [sds((R, D), BF16)] * 3,
        n_smem=0,
    )
    back = [back[0]] + [flip(back[i], i) for i in range(1, 4)]

    def grads_body(act_ref, dh_ref, all_ref, dm_ref, wp_ref, g_ref, o0, o1, o2, o3):
        out = dot(act_ref[...], wp_ref[...])
        for i, o in enumerate((o0, o1, o2, o3)):
            o[...] = out[i * R : (i + 1) * R].astype(o.dtype)
        g_ref[:, 0:D] = dot(act_ref[...], dm_ref[...], 0, 0).astype(BF16)
        g_ref[:, D:] = dot(dh_ref[...], all_ref[...], 0, 0).astype(BF16)

    g_ffn, *res = call(
        grads_body, "ffn_grads", [active, dh, second_all, dm_all, w_proj],
        [sds((FS, 2 * D), BF16), sds((R, D), F32)] + [sds((R, D), BF16)] * 3,
        n_smem=0,
    )
    g_ffn_later = barrier(g_ffn, back[2], back[3])[0]
    g_sum = lax.psum_scatter(g_ffn_later, "blk", scatter_dimension=0, tiled=True)
    back[0] = barrier(back[0], g_ffn)[0]

    def attn_in_body(ids_ref, b0, b1, b2, b3, mid_ref, cot_ref, wo_ref, vec_ref, dmid_ref, da_ref, sum_ref, c0, c1, c2, c3):
        zz = ids_ref[0, 0]
        up = (b0[...] + b1[...].astype(F32)) + (b2[...].astype(F32) + b3[...].astype(F32))
        _, scaled, inverse = norm(mid_ref[...], vec_ref[1:2, :], vec_ref[3:4, :])
        cot_now = cot_ref[...].astype(F32)
        d_mid = cot_now + norm_back(up, scaled, inverse, vec_ref[1:2, :])
        dmid_ref[...] = d_mid
        da = d_mid.astype(BF16)
        da_ref[...] = da
        for k, c in enumerate((c0, c1, c2, c3)):
            w = wo_ref[pl.ds(pl.multiple_of((zz ^ k) * W, 64), W), :]
            c[...] = dot(da, w, 1, 1).astype(BF16)
        sum_ref[0:1] = jnp.sum(up * scaled, axis=0, keepdims=True)
        sum_ref[1:2] = jnp.sum(up, axis=0, keepdims=True)
        sum_ref[2:3] = jnp.sum(da.astype(F32), axis=0, keepdims=True)
        sum_ref[3:4] = jnp.sum(cot_now, axis=0, keepdims=True)

    d_mid, da, sums2, *grad_blocks = call(
        attn_in_body, "attention_gradient", [ids, *back, mid, cot, wo, vec],
        [sds((R, D), F32), sds((R, D), BF16), sds((4, D), F32)] + [sds((R, W), BF16)] * 4,
    )
    grad_blocks = [grad_blocks[0]] + [flip_h(grad_blocks[k], k) for k in range(1, H)]

    def out_grad_body(ids_ref, ctx_ref, da_ref, r1, r2, r3, l1, l2, l3, o0, o1, o2, o3, tmp):
        ff = ids_ref[0, 2]
        tmp[...] = dot(ctx_ref[...], da_ref[...], 0, 0)
        own_rows = pl.ds(pl.multiple_of(ff * S, 64), S)
        o0[...] = tmp[own_rows, :]
        for i, (r, l, o) in enumerate(((r1, l1, o1), (r2, l2, o2), (r3, l3, o3)), 1):
            o[0:R] = r[...]
            o[R : R + S] = tmp[pl.ds(pl.multiple_of((ff ^ i) * S, 64), S), :].astype(BF16)
            for c in range(4):
                o[R + S :, c * S : (c + 1) * S] = l[c * NT // 4 : (c + 1) * NT // 4, :]

    g_out, *mix = call(
        out_grad_body, "out_grad", [ids, ctx_own, da, *res[1:], *lat_cols[1:]],
        [sds((S, D), F32)] + [sds((R + S + NT // 4, D), BF16)] * 3,
        scratch=[pltpu.VMEM((D, D), F32)],
    )
    grad_blocks[0] = barrier(grad_blocks[0], g_out)[0]
    mix = list(barrier(*mix, *grad_blocks[1:])[:3])
    mix = [flip(mix[i - 1], i) for i in range(1, 4)]

    def attend_back(q, g, read_k, read_v, key_pos, q_pos, q_start, lse, ctx, n_keys, put):
        n = q.shape[0]
        g_t = g.astype(F32).T
        dqs = []
        deltas = [
            jnp.sum(g_t[h * HDIM : (h + 1) * HDIM] * ctx[h * HDIM : (h + 1) * HDIM], axis=0, keepdims=True)
            for h in range(NH)
        ]

        def step(i, dq):
            at = pl.multiple_of(i * KB, KB)
            kp = key_pos(at)
            mask = (kp <= q_pos) & (kp >= q_start)
            dks, dvs, new = [], [], []
            for h in range(NH):
                lanes = slice(h * HDIM, (h + 1) * HDIM)
                kh = read_k(at, lanes)
                s = dot(kh, q[:, lanes], 1, 1) * SCALE
                p = jnp.where(mask, jnp.exp(s - lse[h : h + 1]), 0.0)
                dp = dot(read_v(at, lanes), g[:, lanes], 1, 1)
                ds = (p * (dp - deltas[h])).astype(BF16)
                new.append(dq[h] + dot(kh, ds, 0, 0))
                dks.append(dot(ds, q[:, lanes]) * SCALE)
                dvs.append(dot(p.astype(BF16), g[:, lanes]))
            put(at, jnp.concatenate(dks, axis=1), jnp.concatenate(dvs, axis=1))
            return tuple(new)

        dq = lax.fori_loop(
            0, n_keys // KB, step, tuple(jnp.zeros((HDIM, n), F32) for _ in range(NH)), unroll=n_keys // KB <= 4
        )
        return jnp.concatenate(dq, axis=0).T * SCALE

    def token_back_body(
        ids_ref, len_ref, g0, g1, g2, g3, q_ref, kv_ref, ctx_ref, lse_ref, pos_ref, posb_ref, posc_ref, thr_ref, thc_ref,
        ownp_ref, wq_ref, lat_ref, vec_ref, dmid_ref,
        up_ref, dq_ref, dkv_ref, sum_ref, *rest,
    ):
        msgs, acc = rest[:-1], rest[-1]
        zz, yy = ids_ref[0, 0], ids_ref[0, 1]
        rows = [posb_ref[pl.ds((zz ^ k) * Q + yy, 1), :] for k in range(H)]
        p = jnp.concatenate(rows, axis=1)

        def put(at, dk, dv):
            acc[pl.ds(at, KB), 0:W] = dk
            acc[pl.ds(at, KB), W:] = dv

        dq = attend_back(
            q_ref[...].reshape(NQ, W),
            jnp.concatenate([g0[...], g1[...], g2[...], g3[...]], axis=0),
            lambda at, c: kv_ref[pl.ds(at, KB), c],
            lambda at, c: kv_ref[pl.ds(at, KB), W + c.start : W + c.stop],
            lambda at: posc_ref[pl.ds(at, KB), :],
            p,
            start_of(p, len_ref),
            lse_ref[...],
            ctx_ref[...],
            T,
            put,
        ).astype(BF16)
        hot_y = jnp.where(p == thc_ref[...], 1.0, 0.0).astype(BF16)
        hot = jnp.where(pos_ref[...] == thc_ref[...], 1.0, 0.0).astype(BF16)
        d_q = dot(hot_y, dq).astype(BF16)
        d_kv = dot(hot, acc[...].astype(BF16)).astype(BF16)
        gn = dot(d_q, wq_ref[:, 0:W], 1, 1) + dot(d_kv, wq_ref[:, W:], 1, 1)
        _, scaled, inverse = norm(lat_ref[...], vec_ref[0:1, :], vec_ref[2:3, :])
        sum_ref[0:1] = jnp.sum(gn * scaled, axis=0, keepdims=True)
        sum_ref[1:2] = jnp.sum(gn, axis=0, keepdims=True)
        hot_own = jnp.where(ownp_ref[...] == thr_ref[...], 1.0, 0.0).astype(BF16)
        up = norm_back(gn, scaled, inverse, vec_ref[0:1, :]) + spread(hot_own, dmid_ref[...], 0)
        up_ref[...] = up.astype(BF16)
        for k in range(H):
            dq_ref[k] = dq[k * R : (k + 1) * R]
            for j in range(Q):
                a = (zz ^ k) * Q + lax.rem(yy - j + Q, Q)
                block = acc[pl.ds(pl.multiple_of(a * R, R), R), :]
                if j == 0:
                    dkv_ref[k] = block
                else:
                    msgs[j - 1][k] = block.astype(BF16)

    up, dq, dkv, sums1, *kv_msgs = call(
        token_back_body, "token_backward",
        [
            ids, lengths, *grad_blocks, q_tok, kv_tok, ctx_t, lse, pos, pos_blk, pos_col, th_row, th_col,
            own_pos, wq, lat_out, vec, d_mid,
        ],
        [sds((NT, D), BF16), sds((H, R, W), BF16), sds((H, R, 2 * W), F32), sds((2, D), F32)]
        + [sds((H, R, 2 * W), BF16)] * (Q - 1),
        scratch=[pltpu.VMEM((T, 2 * W), F32)],
        n_smem=2,
    )
    if Q == 2:
        up = (up.astype(F32) + shift_q(up, 1).astype(F32)).astype(BF16)
    else:
        ups = jnp.roll(jnp.stack([up] + [shift_q(up, j) for j in range(1, Q)]), y, axis=0)
        up = jnp.sum(ups.astype(F32), axis=0).astype(BF16)
    ups = [x.astype(F32) for x in gather_h(up)]
    up = (ups[0] + ups[2]) + (ups[1] + ups[3])
    kv_msgs = list(barrier(*kv_msgs, up)[:-1])
    kv_msgs = [shift_q(kv_msgs[j - 1], j) for j in range(1, Q)]

    dm_lat = up.astype(BF16)
    dm_lat_blocks = gather_f(dm_lat)

    def latent_ffn_back_body(d0, d1, d2, d3, hid_ref, wf_ref, wp_ref, all_ref, dh_ref, sum_ref, o0, o1, o2, o3):
        for i, d in enumerate((d0, d1, d2, d3)):
            all_ref[i * NT : (i + 1) * NT] = d[...]
        dh = (dot(all_ref[...], wp_ref[...], 1, 1) * gelu_back(hid_ref[...])).astype(BF16)
        dh_ref[...] = dh
        out = dot(dh, wf_ref[...], 1, 1)
        for i, o in enumerate((o0, o1, o2, o3)):
            o[...] = out[i * NT : (i + 1) * NT].astype(o.dtype)
        sum_ref[...] = jnp.sum(dh.astype(F32), axis=0, keepdims=True)

    CR = FS // n_blk
    FR = CR // 3

    def out_sum_body(g0, m1, m2, m3, mid_ref, vec_ref, r0, out_ref, g_ref):
        rows = slice(R, R + S)
        g = (g0[...] + m1[rows].astype(F32)) + (m2[rows].astype(F32) + m3[rows].astype(F32))
        g_ref[...] = g.T.astype(BF16)
        out = (r0[...] + m1[0:R].astype(F32)) + (m2[0:R].astype(F32) + m3[0:R].astype(F32))
        out_ref[...] = (mid_ref[...] + (out + vec_ref[7:8, :])).astype(BF16)

    mix_now = barrier(*mix, ups[2])[:3]
    result, g_out = call(
        out_sum_body, "out_sum", [g_out, *mix_now, mid, vec, res[0]], [sds((R, D), BF16), sds((D, S), BF16)], n_smem=0
    )
    g_out = g_out.reshape(H, Q, CR, S)
    got = [shift_q(take(g_out, (y - j) % Q, 1), j).astype(F32) for j in range(1, Q)]
    g_out = take(g_out, y, 1).astype(F32)
    for t in got:
        g_out = g_out + t
    g_out = g_out.astype(BF16)
    dm_lat_blocks[0], g_out = barrier(dm_lat_blocks[0], g_out)
    g_out = [take(g_out, z)] + [flip_h(take(g_out, z ^ k), k) for k in range(1, H)]

    dm_lat_all, dh_lat, dh_lat_sum, *lat_back = call(
        latent_ffn_back_body, "latent_ffn_backward", [*dm_lat_blocks, hidden_lat, wf, w_proj],
        [sds((4 * NT, D), BF16), sds((4 * NT, FS), BF16), sds((1, FS), F32), sds((NT, D), F32)]
        + [sds((NT, D), BF16)] * 3,
        n_smem=0,
    )
    lat_back = [lat_back[0]] + [flip(lat_back[i], i) for i in range(1, 4)]
    def latent_grads_body(ids_ref, act_ref, dm_ref, dh_ref, second_ref, out_ref, tmp):
        rows = pl.ds(pl.multiple_of(ids_ref[0, 3] * CR, CR), CR)
        tmp[...] = dot(act_ref[...], dm_ref[...], 0, 0)
        out_ref[:, 0:D] = tmp[rows, :]
        tmp[...] = dot(dh_ref[...], second_ref[...], 0, 0)
        out_ref[:, D:] = tmp[rows, :]

    if CR % 16 == 0:
        [lat_part] = call(
            latent_grads_body, "latent_grads", [ids, active_lat, dm_lat_all, dh_lat, second_lat_all],
            [sds((CR, 2 * D), F32)], scratch=[pltpu.VMEM((FS, D), F32)],
        )
    else:
        lat_part = jnp.concatenate([dot(active_lat, dm_lat_all, 0, 0), dot(dh_lat, second_lat_all, 0, 0)], axis=1)
        lat_part = lax.dynamic_slice_in_dim(lat_part, b * CR, CR, axis=0)

    def join_body(g_ref, lat_ref, c0, c1, c2, c3, out_ref, fc_ref):
        out_ref[:, 0:D] = (g_ref[:, 0:D].astype(F32) + lat_ref[:, 0:D]).astype(BF16)
        fc_ref[...] = (g_ref[:, D:].astype(F32) + lat_ref[:, D:]).astype(BF16)
        c = (c0[...].astype(F32) + c2[...].astype(F32)) + (c1[...].astype(F32) + c3[...].astype(F32))
        out_ref[:, D:] = c.astype(BF16)

    def gather_blk(x):
        two = jnp.concatenate([x, flip_h(x, 3)], axis=0)
        other = flip_h(two, 1)
        got = [two, other]
        for j in range(1, Q):
            got += [shift_q(t, j) for t in (two, other)]
        return got

    g_sum = barrier(g_sum, lat_back[2], lat_back[3], lat_part)[0]
    piece_a, fc_sum = call(
        join_body, "join", [g_sum, lat_part, *g_out], [sds((CR, D + S), BF16), sds((CR, D), BF16)], n_smem=0
    )
    lat_back[0] = barrier(lat_back[0], piece_a)[0]
    every_a = gather_blk(piece_a) if CR % 16 == 0 else [lax.all_gather(piece_a, "blk", axis=0, tiled=True)]

    def latent_back_body(*refs):
        ids_ref, len_ref, b0, b1, b2, b3, up_ref, mid_ref, wo_ref, vec_ref, q_ref, ctx_ref, lse_ref = refs[:13]
        qkv_refs = refs[13 : 13 + Q]
        posb_ref, posc_ref, thr_ref, thc_ref, dq_ref, dkv_ref = refs[13 + Q : 19 + Q]
        msgs = refs[19 + Q : 18 + 2 * Q]
        normed_ref, nth_ref, wq_ref, scaled_ref, s1_ref, s2_ref, dh1_ref, dh2_ref, gsum_ref = refs[18 + 2 * Q : 27 + 2 * Q]
        dmid_ref, da_ref, o0, o1, o2, o3, n0, n3, n12, tmp, acc, small_ref = refs[27 + 2 * Q :]
        once = jnp.where(ids_ref[0, 3] == 0, 1.0, 0.0)
        zz, yy, ff = ids_ref[0, 0], ids_ref[0, 1], ids_ref[0, 2]
        back = (b0[...] + b1[...].astype(F32)) + (b2[...].astype(F32) + b3[...].astype(F32))
        _, scaled, inverse = norm(mid_ref[...], vec_ref[1:2, :], vec_ref[3:4, :])
        d_mid = up_ref[...] + norm_back(back, scaled, inverse, vec_ref[1:2, :])
        dmid_ref[...] = d_mid
        da = d_mid.astype(BF16)
        da_ref[...] = da
        col = lambda t: jnp.sum(t, axis=0, keepdims=True)
        small_ref[1:2] = s2_ref[0:1] + once * col(back * scaled)
        small_ref[3:4] = s2_ref[1:2] + once * col(back)
        small_ref[6:7] = s2_ref[2:3] + once * col(da.astype(F32))
        small_ref[7:8] = s2_ref[3:4] + once * col(up_ref[...].astype(BF16).astype(F32))
        g = dot(da, wo_ref[pl.ds(pl.multiple_of(zz * W, 64), W), :], 1, 1).astype(BF16)
        q = q_ref[...]
        p_row = thr_ref[...] - 1
        start = start_of(p_row, len_ref)
        lse = lse_ref[...]
        g_t = g.astype(F32).T
        deltas = [
            jnp.sum(g_t[h * HDIM : (h + 1) * HDIM] * ctx_ref[h * HDIM : (h + 1) * HDIM], axis=0, keepdims=True)
            for h in range(NH)
        ]
        dq_t = [jnp.zeros((HDIM, NT), F32) for _ in range(NH)]
        for j in range(Q):
            kps = [posc_ref[pl.ds(pl.multiple_of(((zz ^ k) * Q + lax.rem(yy + j, Q)) * R, R), R), :] for k in range(H)]
            kp = jnp.concatenate(kps, axis=0)
            mask = (kp <= p_row) & (kp >= start)
            dks, dvs = [], []
            for h in range(NH):
                c = slice(h * HDIM, (h + 1) * HDIM)
                kh = qkv_refs[j][:, :, W + c.start : W + c.stop].reshape(NQ, HDIM)
                vh = qkv_refs[j][:, :, 2 * W + c.start : 2 * W + c.stop].reshape(NQ, HDIM)
                s = dot(kh, q[:, c], 1, 1) * SCALE
                p = jnp.where(mask, jnp.exp(s - lse[h : h + 1]), 0.0)
                dp = dot(vh, g[:, c], 1, 1)
                ds = (p * (dp - deltas[h])).astype(BF16)
                dq_t[h] = dq_t[h] + dot(kh, ds, 0, 0)
                if j == 0:
                    dks.append(dot(ds, q[:, c]) * SCALE)
                    dvs.append(dot(p.astype(BF16), g[:, c]))
            if j == 0:
                acc[0:NQ, W : 2 * W] = jnp.concatenate(dks, axis=1)
                acc[0:NQ, 2 * W :] = jnp.concatenate(dvs, axis=1)
        dq_l = (jnp.concatenate(dq_t, axis=0).T * SCALE).astype(BF16)
        th_grad = jnp.zeros((NT, 3 * W), F32)
        bias = jnp.zeros((1, 3 * W), F32)
        for k in range(H):
            a = (zz ^ k) * Q + yy
            rows = slice(k * R, (k + 1) * R)
            kp = posc_ref[pl.ds(pl.multiple_of(a * R, R), R), :]
            src = jnp.where(kp == thr_ref[...] - 1, 1.0, 0.0).astype(BF16)
            tgt = jnp.where(kp == thr_ref[...], 1.0, 0.0)
            is_th = jnp.max(tgt, axis=1, keepdims=True) > 0
            kv = dkv_ref[k]
            for m in msgs:
                kv = kv + m[k].astype(F32)
            tok = jnp.concatenate([dq_ref[k].astype(F32), kv], axis=1)
            lat = jnp.concatenate([dot(src, dq_l), acc[rows, W:]], axis=1)
            both = (jnp.where(is_th, 0.0, tok) + lat).astype(BF16)
            hot = jnp.where(posb_ref[pl.ds(a, 1), :] == thc_ref[...], 1.0, 0.0).astype(BF16)
            th_grad = th_grad + dot(hot, tok.astype(BF16))
            tmp[rows] = both
        th_low = th_grad.astype(BF16)
        both = tmp[...]
        bias = col(both.astype(F32)) + col(th_low.astype(F32))
        for c in range(H):
            mine = jnp.where(zz == c, 1.0, 0.0)
            small_ref[4:5, c * W : (c + 1) * W] = bias[:, 0:W] * mine
            small_ref[5:6, c * W : (c + 1) * W] = bias[:, 2 * W :] * mine
        gain, shift = s1_ref[0:1], s1_ref[1:2]
        for k in range(H):
            gn = dot(tmp[k * R : (k + 1) * R], wq_ref[...], 1, 1)
            gain = gain + col(gn * scaled_ref[k].astype(F32))
            shift = shift + col(gn)
            if k in (0, 3):
                (n0, n3)[k // 3][...] = gn
            else:
                n12[(k - 1) * R : k * R] = gn.astype(BF16)
        small_ref[0:1] = gain
        small_ref[2:3] = shift
        acc[...] = dot(normed_ref[...].reshape(NQ, D), both, 0, 0) + dot(nth_ref[...], th_low, 0, 0)
        fc = dh1_ref[...] + once * dh2_ref[...]
        fc_part = gsum_ref[...].astype(F32)
        smalls = small_ref[...]
        for i, o in enumerate((o0, o1, o2, o3)):
            o[0:S] = acc[pl.ds(pl.multiple_of((ff ^ i) * S, 64), S), :].astype(o.dtype)
            rows = [jnp.concatenate([columns(smalls, ff ^ i), jnp.zeros((8, 3 * W - S), F32)], axis=1)]
            if i == 0:
                rows += [fc[:, c * S : (c + 1) * S] for c in range(FS // S)]
                rows[1:] = [
                    jnp.concatenate([jnp.concatenate(rows[1:], axis=0), jnp.zeros((8 - FS // S, S), F32)], axis=0)
                ]
                rows[1] = jnp.concatenate([rows[1], jnp.zeros((8, 3 * W - S), F32)], axis=1)
            else:
                rows += [jnp.zeros((8, 3 * W), F32)]
            o[S : S + 16] = jnp.concatenate(rows, axis=0).astype(o.dtype)
            block = columns(fc_part, ff ^ i)
            for c in range(3):
                o[S + 16 :, c * W : (c + 1) * W] = block[c * FR : (c + 1) * FR].astype(o.dtype)

    d_mid_lat, da_lat, *more = call(
        latent_back_body, "latent_backward",
        [
            ids, lengths, *lat_back, up, mid_lat, wo, vec, q_lat, ctx_lat, lse_lat, *qkvs,
            pos_blk, pos_col, th_row, th_col, dq, dkv, *kv_msgs, normed_y, normed_th, wq, scaled_y, sums1, sums2,
            dh_sum, dh_lat_sum, fc_sum,
        ],
        [
            sds((NT, D), F32), sds((NT, D), BF16),
            sds((S + 16 + FR, 3 * W), F32), *[sds((S + 16 + FR, 3 * W), BF16)] * 3,
            sds((R, D), F32), sds((R, D), F32), sds((2 * R, D), BF16),
        ],
        scratch=[pltpu.VMEM((NQ, 3 * W), BF16), pltpu.VMEM((D, 3 * W), F32), pltpu.VMEM((8, D), F32)],
        n_smem=2,
    )
    gq, gn = more[:4], more[4:]
    gq = [gq[0]] + [flip(gq[i], i) for i in range(1, 4)]
    gn12 = flip_h(gn[2], 1)
    def tail_sum_body(g0, m1, m2, m3, gq_ref, fc_ref):
        rows = slice(0, S + 16)
        g = (g0[rows] + m1[rows].astype(F32)) + (m2[rows].astype(F32) + m3[rows].astype(F32))
        gq_ref[...] = g.astype(BF16)
        for i, m in enumerate((g0, m1, m2, m3)):
            for c in range(3):
                fc_ref[c * FR : (c + 1) * FR, i * S : (i + 1) * S] = m[S + 16 :, c * W : (c + 1) * W].astype(BF16)

    gq, piece_b = call(
        tail_sum_body, "tail_sum", gq, [sds((S + 16, 3 * W), BF16), sds((CR, 4 * S), BF16)], n_smem=0
    )
    gn3 = flip_h((gn[1] + barrier(gn12, gq)[0][R:].astype(F32)).astype(BF16), 3)
    if Q == 2:
        gq = (gq.astype(F32) + shift_q(gq, 1).astype(F32)).astype(BF16)
    else:
        every = jnp.roll(jnp.stack([gq] + [shift_q(gq, j) for j in range(1, Q)]), y, axis=0)
        gq = jnp.sum(every.astype(F32), axis=0).astype(BF16)
    gq = barrier(gq, gn3)[0]
    gq3 = flip_h(gq, 3)
    gq12 = flip_h(jnp.concatenate([gq, gq3], axis=0), 1)
    piece_b = barrier(piece_b, gq)[0]
    every_b = gather_blk(piece_b) if CR % 16 == 0 else [lax.all_gather(piece_b, "blk", axis=0, tiled=True)]

    def final_body(n0, n3, n12, x_ref, dmid_ref, ownp_ref, thr_ref, dlat_ref, vec_ref, grad_ref):
        gn_now = (n0[...] + n3[...].astype(F32)) + n12[0:R].astype(F32)
        _, scaled, inverse = norm(x_ref[...].astype(F32), vec_ref[0:1, :], vec_ref[2:3, :])
        tgt = jnp.where(ownp_ref[...] == thr_ref[...], 1.0, 0.0)
        is_th = jnp.max(tgt, axis=1, keepdims=True) > 0
        src = jnp.where(ownp_ref[...] == thr_ref[...] - 1, 1.0, 0.0).astype(BF16)
        grad = jnp.where(is_th, 0.0, dmid_ref[...]) + norm_back(gn_now, scaled, inverse, vec_ref[0:1, :])
        grad_ref[...] = grad + spread(src, dlat_ref[...], 1)

    [grad_in] = call(
        final_body, "input_grad", [gn[0], gn3, gn12, own, d_mid, own_pos, th_row, d_mid_lat, vec], [sds((R, D), F32)], n_smem=0
    )

    da_lat_blocks = gather_f(barrier(da_lat, gq)[0])

    def place_blocks(ids_ref, refs, tmp):
        if len(refs) == 1:
            tmp[...] = refs[0][...]
            return
        for j in range(Q):
            for k in range(H):
                a = (ids_ref[0, 0] ^ k) * Q + lax.rem(ids_ref[0, 1] + j, Q)
                which, half = ((0, 0), (1, 0), (1, 1), (0, 1))[k]
                block = refs[2 * j + which][half * CR : (half + 1) * CR]
                tmp[pl.ds(pl.multiple_of(a * CR, CR), CR), :] = block

    def a_grad_body(*refs):
        ids_ref, parts_a = refs[0], refs[1 : 1 + len(every_a)]
        l0, m1, m2, m3, a0, a1, a2, a3, wp_ref, wo_ref, tmp = refs[1 + len(every_a) :]
        place_blocks(ids_ref, parts_a, tmp)
        wp_ref[...] = tmp[:, 0:D].astype(F32)
        lats = [l0[...]]
        for m in (m1, m2, m3):
            lats.append(jnp.concatenate([m[R + S :, c * S : (c + 1) * S] for c in range(4)], axis=0))
        lat = [dot(l, a[...], 0, 0) for l, a in zip(lats, (a0, a1, a2, a3))]
        wo_ref[...] = tmp[:, D:].astype(F32).T + ((lat[0] + lat[1]) + (lat[2] + lat[3]))

    def b_grad_body(*refs):
        ids_ref, parts_b = refs[0], refs[1 : 1 + len(every_b)]
        out_ref, tmp = refs[1 + len(every_b) :]
        ff = ids_ref[0, 2]
        place_blocks(ids_ref, parts_b, tmp)
        for i in range(4):
            block = tmp[:, i * S : (i + 1) * S].astype(F32).T
            out_ref[:, pl.ds(pl.multiple_of((ff ^ i) * FS, 128), FS)] = block

    w_proj_g, w_out_g = call(
        a_grad_body, "proj_out_grad",
        [ids, *every_a, lat_cols[0], *mix, *da_lat_blocks],
        [sds((FS, D), F32), sds((S, D), F32)],
        scratch=[pltpu.VMEM((FS, D + S), BF16)],
    )
    [w_fc_g] = call(
        b_grad_body, "fc_grad", [ids, *every_b], [sds((S, 4 * FS), F32)],
        scratch=[pltpu.VMEM((FS, 4 * S), BF16)],
    )

    def qkv_grad_body(
        ids_ref, g0, g3, g12, out_ref, gain_ref, shift_ref, qv_ref, ob_ref, fb_ref, pb_ref, tmp
    ):
        zz = ids_ref[0, 0]
        tmp[zz] = g0[...]
        tmp[zz ^ 3] = g3[...]
        tmp[zz ^ 1] = g12[0 : S + 16]
        tmp[zz ^ 2] = g12[S + 16 :]
        small = [tmp[c][S:, 0:S].astype(F32) for c in range(H)]
        small = (small[0] + small[2]) + (small[1] + small[3])
        for i, ref in enumerate((gain_ref, shift_ref, qv_ref)):
            ref[...] = small[2 * i : 2 * i + 2]
        ob_ref[...] = small[6]
        pb_ref[...] = small[7]
        for c in range(FS // S):
            fb_ref[c * S : (c + 1) * S] = small[8 + c]
        for c in range(H):
            for i in range(3):
                out_ref[:, i * D + c * W : i * D + (c + 1) * W] = tmp[c][0:S, i * W : (i + 1) * W].astype(F32)

    w_qkv_g, gain_g, shift_g, qv_g, ob_g, fb_g, pb_g = call(
        qkv_grad_body, "qkv_grad", [ids, gq, gq3, gq12],
        [sds((S, 3 * D), F32)] + [sds((2, S), F32)] * 3 + [sds((S,), F32), sds((FS,), F32), sds((S,), F32)],
        scratch=[pltpu.VMEM((H, S + 16, 3 * W), BF16)],
    )
    return (
        result[None],
        grad_in[None],
        gain_g,
        shift_g,
        w_qkv_g,
        qv_g,
        w_out_g,
        ob_g,
        w_fc_g,
        fb_g,
        w_proj_g,
        pb_g,
    )


def solution(mesh):
    a, r, v = P("fsdp", "blk", None), P("fsdp", None), P("fsdp")
    c = P(None, "fsdp")
    return jax.shard_map(
        local,
        mesh=mesh,
        in_specs=(a, r, r, r, c, c, r, c, r, v, r, v, r, v, a),
        out_specs=(a, a, c, c, r, c, r, v, r, v, r, v),
        check_vma=False,
    )
```
